128 devices in a mesh: ctx: 8 (over x, core), fsdp: 16 (over z, y).
Axes of the slice: x: 4, y: 4, z: 4, core: 2. Of those that a mesh axis runs over, the one named last changes fastest.
Arguments:
- old_master: float32 [16384, 1024], P(('ctx', 'fsdp')), may hold values from -6 to 6
- old_moment: float32 [16384, 1024], P(('ctx', 'fsdp')), may hold values from -2 to 2
- old_second: float32 [16384, 1024], P(('ctx', 'fsdp')), may hold values from 0.0001 to 1
- frag_list: int32 [3, 16384], P(None, ('ctx', 'fsdp')), may hold values from 0 to 1024, as said below
- pair_counts: int32 [128, 128], P(None, ('ctx', 'fsdp')), may hold values from 0 to 2, as said below
- grad_partial: bfloat16 [8, 8, 16, 128, 1024], P('ctx', None, 'fsdp'), may hold values from -6 to 6
Outputs:
- new_master: float32 [16384, 1024], P(('ctx', 'fsdp'))
- new_moment: float32 [16384, 1024], P(('ctx', 'fsdp'))
- new_second: float32 [16384, 1024], P(('ctx', 'fsdp'))
The draws below stay inside these ranges and needn't reach their ends.
Inputs may be any that keep to these rules, and one draw needn't show every extreme that they name: `frag_list`: row 0 names each fragment's new owner, row 1 its position among the fragments that its old owner sends to that owner (0 up to that pair's count less one), row 2 its live length (at least 512). Every new owner receives exactly 128 fragments. One old owner sends at most 2 fragments to one new owner, and some pair sends exactly 2. `pair_counts`: entry [o, n] is the number of fragments of old owner o whose new owner is n, as listed in frag_list; every row and every column sums to 128; some entry is 2.
All inputs are finite; a program needn't handle non-finite values.
Results may differ from the reference program's by a relative error of at most 0.0003.
Values sent between devices are 32-bit elements; how exact they have to be, the bound alone decides.
A program may use at most 64 MiB of HBM per device.

```python
import math
import jax
import jax.numpy as jnp
from jax import lax

FRAG = 1024
ROWS_DEV = 128
CAP = 2
ROWS = 16384
N_CTX = 8
N_FSDP = 16
DEVICES = 128


def owner_order(order_key):
    return jax.random.permutation(order_key, ROWS_DEV).astype(jnp.int32)


def fragment_plan(key):
    group_count = DEVICES // 2
    key_shift, key_size, key_order, key_length = jax.random.split(key, 4)
    perm = jax.random.permutation(key_shift, DEVICES).astype(jnp.int32)
    displaced = perm[group_count]
    perm = jnp.where(perm == DEVICES // 2, displaced, perm)
    shifts = perm.at[group_count].set(DEVICES // 2).astype(jnp.int32)
    first_sizes = jax.random.randint(key_size, (group_count,), 0, CAP + 1).astype(jnp.int32)
    first_sizes = first_sizes.at[0].set(0)
    group_sizes = jnp.concatenate([first_sizes, CAP - first_sizes])
    group_ends = jnp.cumsum(group_sizes)
    group_starts = group_ends - group_sizes
    order_keys = jax.random.split(key_order, DEVICES)
    positions = jax.vmap(owner_order)(order_keys)
    group_index = jnp.sum((positions[:, :, None] >= group_ends[None, None, :]).astype(jnp.int32), axis=2)
    senders = jnp.arange(DEVICES, dtype=jnp.int32)
    owners = (senders[:, None] + shifts[group_index]) % DEVICES
    offsets = positions - group_starts[group_index]
    lengths = jax.random.randint(key_length, (DEVICES, ROWS_DEV), FRAG // 2, FRAG + FRAG // 4).astype(jnp.int32)
    lengths = jnp.minimum(lengths, FRAG).at[0, 0].set(FRAG)
    frag_list = jnp.stack([owners, offsets, lengths]).reshape(3, DEVICES * ROWS_DEV).astype(jnp.int32)
    targets = (senders[:, None] + shifts[None, :]) % DEVICES
    match = (targets[:, :, None] == senders[None, None, :]).astype(jnp.int32)
    counts = jnp.sum(group_sizes[None, :, None] * match, axis=1).astype(jnp.int32)
    return (frag_list, counts)


def draw_frag_list(key, part):
    return fragment_plan(key)[0]


def draw_pair_counts(key, part):
    return fragment_plan(key)[1]


def spiked(entries, stream_key, source, target, shards_of, factor):
    def block_of(axis_at):
        return (jnp.arange(entries.shape[axis_at]) // (entries.shape[axis_at] // shards_of)).reshape((-1,) + (1,) * (entries.ndim - 1 - axis_at))

    one_side = jax.random.permutation(stream_key, shards_of)[block_of(target)]
    far = (block_of(target) + shards_of // 2) % shards_of
    return jnp.where((block_of(source) == one_side) | (block_of(source) == far), factor * entries, entries)


def shard_levels(key, shape, pieces, low, largest):
    def one(position, shards_of):
        steps = jax.random.uniform(jax.random.fold_in(jax.random.fold_in(key, 6), position), (shards_of,), jnp.float32, low / len(pieces), largest / len(pieces))
        return jnp.repeat(jnp.exp(steps), shape[position] // shards_of).reshape((-1,) + (1,) * (len(shape) - position - 1))

    loudness = one(*pieces[0])
    for cut in pieces[1:]:
        loudness = loudness * one(*cut)
    return loudness


def normal_values(own_key, extent, deviation, most, cuts=(), kind=jnp.bfloat16):
    drawn = deviation * jax.random.normal(own_key, extent, jnp.float32)
    if cuts:
        drawn = drawn * shard_levels(own_key, extent, cuts, -0.22, 0.18)
    return jnp.clip(drawn, -most, most).astype(kind)


def heavy_noise(key, dims, deviation, most, shards, heavy, held_as=jnp.bfloat16):
    array = deviation * jax.random.normal(key, dims, jnp.float32)
    if shards:
        array = array * shard_levels(key, dims, shards, -0.22, 0.18)
    return jnp.clip(spiked(array, jax.random.fold_in(key, 3), *heavy), -most, most).astype(held_as)


def setup_inputs(seed: int = 0) -> dict:
    key_list = jax.random.split(jax.random.key(seed), 7)
    return {
        "old_master": normal_values(key_list[0], (ROWS, FRAG), 1.0, 6.0, ((0, 128),), jnp.float32),
        "old_moment": normal_values(key_list[1], (ROWS, FRAG), 0.3, 2.0, ((0, 128),), jnp.float32),
        "old_second": jnp.clip(jnp.exp(math.log(1.0) - 9.2103404 * jax.random.uniform(key_list[2], (ROWS, FRAG), jnp.float32) ** shard_levels(key_list[2], (ROWS, FRAG), ((0, 128),), -0.2, 0.2)), 0.0001, 1.0),
        "frag_list": draw_frag_list(jax.random.fold_in(key_list[6], 71), 0),
        "pair_counts": draw_pair_counts(jax.random.fold_in(key_list[6], 71), 0),
        "grad_partial": heavy_noise(key_list[5], (N_CTX, N_CTX, N_FSDP, ROWS_DEV, FRAG), 1.0, 6.0, ((0, 8), (2, 16)), (0, 1, 8, 2.0)),
    }


beta_one = 0.9
beta_two = 0.95
learn_rate = 0.0003
decay_weight = 0.1
epsilon = 1e-08
step_count = 1001.0

def adamw_update(master, moment, second, grad):
    new_moment = beta_one * moment + (1.0 - beta_one) * grad
    new_second = beta_two * second + (1.0 - beta_two) * grad * grad
    moment_hat = new_moment / (1.0 - beta_one ** step_count)
    second_hat = new_second / (1.0 - beta_two ** step_count)
    new_master = master - learn_rate * (moment_hat / (jnp.sqrt(second_hat) + epsilon) + decay_weight * master)
    return (new_master, new_moment, new_second)

def reference(old_master, old_moment, old_second, frag_list, pair_counts, grad_partial):
    owners = frag_list[0]
    offsets = frag_list[1]
    lengths = frag_list[2]
    before = jnp.cumsum(pair_counts, axis=0) - pair_counts
    source = (jnp.arange(DEVICES * ROWS_DEV, dtype=jnp.int32) // ROWS_DEV).astype(jnp.int32)
    targets = (owners * ROWS_DEV + before[source, owners] + offsets).astype(jnp.int32)
    columns = jnp.arange(FRAG, dtype=jnp.int32)
    live_mask = columns[None, :] < lengths[:, None]

    def place_rows(values):
        masked = jnp.where(live_mask, values, jnp.zeros_like(values))
        return jnp.zeros_like(values).at[targets].set(masked)
    moved_master = place_rows(old_master)
    moved_moment = place_rows(old_moment)
    moved_second = place_rows(old_second)
    moved_length = jnp.zeros((DEVICES * ROWS_DEV,), jnp.int32).at[targets].set(lengths)
    grad = lax.optimization_barrier(jnp.sum(grad_partial, axis=0, dtype=jnp.float32)).reshape(DEVICES * ROWS_DEV, FRAG)
    grad = jnp.where(columns[None, :] < moved_length[:, None], grad, jnp.zeros_like(grad))
    new_master, new_moment, new_second = adamw_update(moved_master, moved_moment, moved_second, grad)
    return (new_master, new_moment, new_second)
```

```python
import functools

import jax
import jax.numpy as jnp
from jax import lax
from jax.experimental import pallas as pl
from jax.experimental.pallas import tpu as pltpu
from jax.sharding import PartitionSpec as P

MESH = pl.DeviceIdType.MESH

beta_one = 0.9
beta_two = 0.95
learn_rate = 0.0003
decay_weight = 0.1
epsilon = 1e-08
step_count = 1001.0

ROWS = 128
FRAG = 1024
TILES = 8
LANES = 128
N_CTX = 8
N_FSDP = 16
DEVICES = 128
CAP = 2


def place():
    ctx, fsdp = lax.axis_index("ctx"), lax.axis_index("fsdp")
    return ctx // 2, ctx % 2, fsdp // 4, fsdp % 4


def partner(k):
    x, core, z, y = place()
    dx, dy, dz, dcore = k % 4, (k // 4) % 4, (k // 16) % 4, (k // 64) % 2
    return ((x + dx) % 4) * 2 + (core + dcore) % 2, ((z + dz) % 4) * 4 + (y + dy) % 4


def kernel(
    master_hbm, moment_hbm, second_hbm, frag_hbm, counts_hbm, grad_hbm,
    new_master_hbm, new_moment_hbm, new_second_hbm,
    state, frag_v, counts_v, slot_v, row_v, frag_s, slot_s, row_s,
    send, recv, terms, pair_out, pair_in, sums, hop_in, last_in, total, out,
    state_sem, small_sem, terms_sem, out_sem,
    packet_send, packet_recv, pair_send, pair_recv, hop_send, hop_recv, last_send, last_recv,
    group_sem,
):
    ctx, fsdp = lax.axis_index("ctx"), lax.axis_index("fsdp")
    x, core, _, _ = place()
    me = ctx * N_FSDP + fsdp

    frag_load = pltpu.make_async_copy(frag_hbm, frag_v, small_sem.at[0])
    frag_load_s = pltpu.make_async_copy(frag_hbm, frag_s, small_sem.at[1])
    counts_load = pltpu.make_async_copy(counts_hbm, counts_v, small_sem.at[2])
    frag_load.start()
    frag_load_s.start()
    counts_load.start()
    barrier = pltpu.get_barrier_semaphore()
    for k in range(1, N_CTX):
        pl.semaphore_signal(barrier, inc=1, device_id=((ctx + k) % N_CTX, fsdp), device_id_type=MESH)
    for k in range(1, N_FSDP):
        pl.semaphore_signal(barrier, inc=1, device_id=(ctx, (fsdp + k) % N_FSDP), device_id_type=MESH)

    order = [(x + 2) % 4, (x + 1) % 4, (x + 3) % 4, x]

    def term_load(side, step):
        block = order[step] * 2 + (core + side) % 2
        return pltpu.make_async_copy(grad_hbm.at[0, block, 0], terms.at[side, step], terms_sem.at[side, step])

    for step in range(4):
        term_load(1, step).start()
    state_loads = []
    for a, source in enumerate((master_hbm, moment_hbm, second_hbm)):
        for j in range(TILES):
            state_loads.append(
                pltpu.make_async_copy(
                    source.at[:, pl.ds(j * LANES, LANES)],
                    state.at[a, pl.ds(j * ROWS, ROWS)],
                    state_sem.at[a, j],
                )
            )
    for load in state_loads:
        load.start()
    for step in range(4):
        term_load(0, step).start()

    frag_load.wait()
    counts_load.wait()
    owners, offsets = frag_v[pl.ds(0, 1), :], frag_v[pl.ds(1, 1), :]
    slot_of_row = owners * CAP + offsets
    slot_ids = lax.broadcasted_iota(jnp.int32, (DEVICES * CAP, ROWS), 0)
    hit = jnp.where(slot_ids == slot_of_row, 1.0, 0.0)
    row_ids = lax.broadcasted_iota(jnp.int32, (8, ROWS), 1).astype(jnp.float32)
    row_of_slot = lax.dot_general(row_ids, hit, (((1,), (1,)), ((), ())), preferred_element_type=jnp.float32)
    slot_v[...] = jnp.clip(row_of_slot.astype(jnp.int32), 0, ROWS - 1)
    counts = jnp.broadcast_to(counts_v[...].astype(jnp.float32), (8, DEVICES))
    earlier = jnp.where(
        lax.broadcasted_iota(jnp.int32, (DEVICES, DEVICES), 0) < lax.broadcasted_iota(jnp.int32, (DEVICES, DEVICES), 1),
        1.0, 0.0,
    )
    before = lax.dot_general(counts, earlier, (((1,), (0,)), ((), ())), preferred_element_type=jnp.float32)[0:1, :]
    rows_down = lax.broadcasted_iota(jnp.int32, (ROWS, DEVICES), 0).astype(jnp.float32)
    owner_ids = lax.broadcasted_iota(jnp.int32, (ROWS, DEVICES), 1).astype(jnp.float32)
    offset = rows_down - before
    from_owner = (offset >= 0.0) & (offset < counts[0:1, :])
    slot_here = jnp.where(from_owner, owner_ids * CAP + offset, 0.0)
    slot_of_new = lax.dot_general(
        jnp.ones((8, DEVICES), jnp.float32), slot_here, (((1,), (1,)), ((), ())), preferred_element_type=jnp.float32
    )
    row_v[...] = jnp.clip(slot_of_new.astype(jnp.int32), 0, DEVICES * CAP - 1)
    slot_copy = pltpu.make_async_copy(slot_v, slot_s, small_sem.at[3])
    row_copy = pltpu.make_async_copy(row_v, row_s, small_sem.at[4])
    slot_copy.start()
    row_copy.start()

    for step in range(4):
        term_load(1, step).wait()

        def widen(i, carry, step=step):
            rows = pl.ds(pl.multiple_of(i * 16, 16), 16)
            for j in range(TILES):
                pair_out[step, j, rows, :] = terms[1, step, rows, pl.ds(j * LANES, LANES)].astype(jnp.float32)
            return carry

        lax.fori_loop(0, ROWS // 16, widen, 0)

    pl.semaphore_wait(barrier, N_CTX - 1 + N_FSDP - 1)
    for k in range(1, N_FSDP):
        pl.semaphore_signal(group_sem, inc=1, device_id=(ctx, (fsdp + k) % N_FSDP), device_id_type=MESH)

    def pair_copy(step):
        return pltpu.make_async_remote_copy(
            src_ref=pair_out.at[step], dst_ref=pair_in.at[step], send_sem=pair_send.at[step],
            recv_sem=pair_recv.at[step], device_id=(x * 2 + 1 - core, fsdp), device_id_type=MESH,
        )

    def along_x(shift):
        return ((x + shift) % 4) * 2 + core, fsdp

    low, high = pl.ds(0, TILES // 2), pl.ds(TILES // 2, TILES // 2)
    half = (low, high)

    def hop_copy(way):
        return pltpu.make_async_remote_copy(
            src_ref=sums.at[0, half[way]], dst_ref=hop_in.at[way], send_sem=hop_send.at[way],
            recv_sem=hop_recv.at[way], device_id=along_x(1 if way == 0 else 3), device_id_type=MESH,
        )

    def last_copy(way, part):
        return pltpu.make_async_remote_copy(
            src_ref=sums.at[1 + way, half[part]], dst_ref=last_in.at[way, half[part]],
            send_sem=last_send.at[way, part], recv_sem=last_recv.at[way, part],
            device_id=along_x(1 if way == 0 else 3), device_id_type=MESH,
        )

    def add_pair(step):
        term_load(0, step).wait()
        pair_copy(step).wait_recv()

        def add(i, carry):
            rows = pl.ds(pl.multiple_of(i * 16, 16), 16)
            for j in range(TILES):
                own = terms[0, step, rows, pl.ds(j * LANES, LANES)].astype(jnp.float32)
                sums[step, j, rows, :] = own + pair_in[step, j, rows, :]
            return carry

        lax.fori_loop(0, ROWS // 16, add, 0)

    for step in range(4):
        pair_copy(step).start()

    for load in state_loads:
        load.wait()
    frag_load_s.wait()
    slot_copy.wait()
    row_copy.wait()

    place_in_row = (
        lax.broadcasted_iota(jnp.int32, (TILES, LANES), 0) * LANES + lax.broadcasted_iota(jnp.int32, (TILES, LANES), 1)
    )

    def pack(device, slot):
        row = slot_s[0, device * CAP + slot]
        live = place_in_row < frag_s[2, row]
        values = [state[a, pl.ds(row, TILES, stride=ROWS), :] for a in range(3)]
        return [jnp.where(live, v, 0.0 if a < 2 else -1.0) for a, v in enumerate(values)]

    def packet(k, device, target):
        return pltpu.make_async_remote_copy(
            src_ref=send.at[k], dst_ref=recv.at[pl.ds(me * CAP, CAP)], send_sem=packet_send, recv_sem=packet_recv,
            device_id=target, device_id_type=MESH,
        )

    def post(i, carry):
        k = (i * 45) % DEVICES
        target = partner(k)
        device = target[0] * N_FSDP + target[1]
        for slot in range(CAP):
            for a, v in enumerate(pack(device, slot)):
                send[i, slot, pl.ds(a * TILES, TILES), :] = v
        packet(i, device, target).start()
        return carry

    for step in (0, 1, 2):
        add_pair(step)
        if step == 0:
            hop_copy(0).start()
            hop_copy(1).start()
        else:
            last_copy(step - 1, 2 - step).start()

    pl.semaphore_wait(group_sem, N_FSDP - 1)
    lax.fori_loop(1, DEVICES // 2, post, 0)
    for way in range(2):
        hop_copy(way).wait()

        def add_hop(i, carry, way=way):
            rows = pl.ds(pl.multiple_of(i * 16, 16), 16)
            for j in range(TILES // 2):
                sums[1 + way, way * (TILES // 2) + j, rows, :] += hop_in[way, j, rows, :]
            return carry

        lax.fori_loop(0, ROWS // 16, add_hop, 0)
        last_copy(way, way).start()
    lax.fori_loop(DEVICES // 2, DEVICES, post, 0)
    for slot in range(CAP):
        for a, v in enumerate(pack(me, slot)):
            recv[me * CAP + slot, pl.ds(a * TILES, TILES), :] = v
    add_pair(3)

    for way in range(2):
        for part in range(2):
            last_copy(way, part).wait_recv()

    def add_last(i, carry):
        rows = pl.ds(pl.multiple_of(i * 16, 16), 16)
        for j in range(TILES):
            total[pl.ds(pl.multiple_of(j * ROWS + i * 16, 16), 16), :] = (
                sums[3, j, rows, :] + last_in[0, j, rows, :] + last_in[1, j, rows, :]
            )
        return carry

    lax.fori_loop(0, ROWS // 16, add_last, 0)

    all_sent = send.at[pl.ds(1, DEVICES - 1)]
    all_here = recv.at[pl.ds(0, (DEVICES - 1) * CAP)]
    pltpu.make_async_copy(all_here, all_here, packet_recv).wait()

    def update(row, carry):
        slot = row_s[0, row]
        master, moment, second = [recv[slot, pl.ds(a * TILES, TILES), :] for a in range(3)]
        live = second >= 0.0
        second = jnp.where(live, second, 0.0)
        grad = jnp.where(live, total[pl.ds(row, TILES, stride=ROWS), :], 0.0)
        new_moment = beta_one * moment + (1.0 - beta_one) * grad
        new_second = beta_two * second + (1.0 - beta_two) * grad * grad
        moment_hat = new_moment / (1.0 - beta_one**step_count)
        second_hat = new_second / (1.0 - beta_two**step_count)
        new_master = master - learn_rate * (
            moment_hat / (jnp.sqrt(second_hat) + epsilon) + decay_weight * master
        )
        for a, v in enumerate((new_master, new_moment, new_second)):
            out[a, pl.ds(row, TILES, stride=ROWS), :] = v
        return carry

    lax.fori_loop(0, ROWS, update, 0, unroll=4)
    stores = []
    for a, target in enumerate((new_master_hbm, new_moment_hbm, new_second_hbm)):
        for j in range(TILES):
            stores.append(
                pltpu.make_async_copy(
                    out.at[a, pl.ds(j * ROWS, ROWS)], target.at[:, pl.ds(j * LANES, LANES)], out_sem.at[a, j]
                )
            )
    for store in stores:
        store.start()
    pltpu.make_async_copy(all_sent, all_sent, packet_send).wait()
    for step in range(4):
        pair_copy(step).wait_send()
    for way in range(2):
        for part in range(2):
            last_copy(way, part).wait_send()
    for store in stores:
        store.wait()


def local(old_master, old_moment, old_second, frag_list, pair_counts, grad_partial):
    anywhere = pl.BlockSpec(memory_space=pl.ANY)
    shape = jax.ShapeDtypeStruct((ROWS, FRAG), jnp.float32)
    f32, i32 = jnp.float32, jnp.int32
    dma = pltpu.SemaphoreType.DMA
    return pl.pallas_call(
        kernel,
        out_shape=(shape, shape, shape),
        in_specs=[anywhere] * 6,
        out_specs=(anywhere, anywhere, anywhere),
        scratch_shapes=[
            pltpu.VMEM((3, TILES * ROWS, LANES), f32),
            pltpu.VMEM((3, ROWS), i32),
            pltpu.VMEM((1, DEVICES), i32),
            pltpu.VMEM((8, DEVICES * CAP), i32),
            pltpu.VMEM((8, ROWS), i32),
            pltpu.SMEM((3, ROWS), i32),
            pltpu.SMEM((8, DEVICES * CAP), i32),
            pltpu.SMEM((8, ROWS), i32),
            pltpu.VMEM((DEVICES, CAP, 3 * TILES, LANES), f32),
            pltpu.VMEM((DEVICES * CAP, 3 * TILES, LANES), f32),
            pltpu.VMEM((2, 4, ROWS, FRAG), jnp.bfloat16),
            pltpu.VMEM((4, TILES, ROWS, LANES), f32),
            pltpu.VMEM((4, TILES, ROWS, LANES), f32),
            pltpu.VMEM((4, TILES, ROWS, LANES), f32),
            pltpu.VMEM((2, TILES // 2, ROWS, LANES), f32),
            pltpu.VMEM((2, TILES, ROWS, LANES), f32),
            pltpu.VMEM((TILES * ROWS, LANES), f32),
            pltpu.VMEM((3, TILES * ROWS, LANES), f32),
            dma((3, TILES)),
            dma((5,)),
            dma((2, 4)),
            dma((3, TILES)),
            dma,
            dma,
            dma((4,)),
            dma((4,)),
            dma((2,)),
            dma((2,)),
            dma((2, 2)),
            dma((2, 2)),
            pltpu.SemaphoreType.REGULAR,
        ],
        compiler_params=pltpu.CompilerParams(
            collective_id=0, has_side_effects=True, vmem_limit_bytes=48 * 1024 * 1024
        ),
    )(old_master, old_moment, old_second, frag_list, pair_counts.reshape(1, DEVICES), grad_partial)


def solution(mesh):
    return jax.shard_map(
        local,
        mesh=mesh,
        in_specs=(
            P(("ctx", "fsdp"), None),
            P(("ctx", "fsdp"), None),
            P(("ctx", "fsdp"), None),
            P(None, ("ctx", "fsdp")),
            P(None, ("ctx", "fsdp")),
            P("ctx", None, "fsdp", None, None),
        ),
        out_specs=(P(("ctx", "fsdp"), None), P(("ctx", "fsdp"), None), P(("ctx", "fsdp"), None)),
        check_vma=False,
    )
```

```python
import functools

import jax
import jax.numpy as jnp
from jax import lax
from jax.experimental import pallas as pl
from jax.experimental.pallas import tpu as pltpu
from jax.sharding import PartitionSpec as P

MESH = pl.DeviceIdType.MESH

beta_one = 0.9
beta_two = 0.95
learn_rate = 0.0003
decay_weight = 0.1
epsilon = 1e-08
step_count = 1001.0

ROWS = 128
FRAG = 1024
TILES = 8
LANES = 128
N_CTX = 8
N_FSDP = 16
DEVICES = 128
CAP = 2
PARTS = 4
CHUNK = ROWS // PARTS


def place():
    ctx, fsdp = lax.axis_index("ctx"), lax.axis_index("fsdp")
    return ctx // 2, ctx % 2, fsdp // 4, fsdp % 4


def partner(k):
    x, core, z, y = place()
    dx, dy, dz, dcore = k % 4, (k // 4) % 4, (k // 16) % 4, (k // 64) % 2
    return ((x + dx) % 4) * 2 + (core + dcore) % 2, ((z + dz) % 4) * 4 + (y + dy) % 4


def kernel(
    master_hbm, moment_hbm, second_hbm, frag_hbm, counts_hbm, grad_hbm,
    out,
    state, frag_v, counts_v, slot_v, row_v, frag_s, slot_s, row_s,
    send, recv, terms, pair_out, pair_in, sums, hop_in, last_in, acc_in, total,
    state_sem, small_sem, terms_sem,
    packet_send, packet_recv, pair_send, pair_recv, hop_send, hop_recv, last_send, last_recv, acc_send, acc_recv,
    y_sem, z_sem,
):
    ctx, fsdp = lax.axis_index("ctx"), lax.axis_index("fsdp")
    x, core, z, y = place()
    me = ctx * N_FSDP + fsdp
    order = [(x + 2) % 4, (x + 1) % 4, (x + 3) % 4, x]

    def term_load(side, step):
        block = order[step] * 2 + (core + side) % 2
        return pltpu.make_async_copy(grad_hbm.at[0, block, 0], terms.at[side, step], terms_sem.at[side, step])

    def y_peer(k):
        return ctx, z * 4 + (y + k) % 4

    def z_peer(k):
        return ctx, ((z + k) % 4) * 4 + y

    barrier = pltpu.get_barrier_semaphore()
    for k in range(1, N_CTX):
        pl.semaphore_signal(barrier, inc=1, device_id=((ctx + k) % N_CTX, fsdp), device_id_type=MESH)
    for k in range(1, 4):
        pl.semaphore_signal(barrier, inc=1, device_id=y_peer(k), device_id_type=MESH)
    for k in range(1, 4):
        pl.semaphore_signal(barrier, inc=1, device_id=z_peer(k), device_id_type=MESH)

    for step in range(4):
        term_load(1, step).start()
    frag_load = pltpu.make_async_copy(frag_hbm, frag_v, small_sem.at[0])
    frag_load_s = pltpu.make_async_copy(frag_hbm, frag_s, small_sem.at[1])
    counts_load = pltpu.make_async_copy(counts_hbm, counts_v, small_sem.at[2])
    frag_load.start()
    frag_load_s.start()
    counts_load.start()
    for step in range(4):
        term_load(0, step).start()
    state_loads = []
    for a, source in enumerate((master_hbm, moment_hbm, second_hbm)):
        for j in range(TILES):
            state_loads.append(
                pltpu.make_async_copy(
                    source.at[:, pl.ds(j * LANES, LANES)],
                    state.at[a, pl.ds(j * ROWS, ROWS)],
                    state_sem.at[a, j],
                )
            )
    for load in state_loads:
        load.start()

    for step in range(4):
        term_load(1, step).wait()

        def widen(i, carry, step=step):
            rows = pl.ds(pl.multiple_of(i * 16, 16), 16)
            for j in range(TILES):
                pair_out[step, j, rows, :] = terms[1, step, rows, pl.ds(j * LANES, LANES)].astype(jnp.float32)
            return carry

        lax.fori_loop(0, ROWS // 16, widen, 0)

    frag_load.wait()
    counts_load.wait()
    owners, offsets = frag_v[pl.ds(0, 1), :], frag_v[pl.ds(1, 1), :]
    slot_of_row = owners * CAP + offsets
    slot_ids = lax.broadcasted_iota(jnp.int32, (DEVICES * CAP, ROWS), 0)
    hit = jnp.where(slot_ids == slot_of_row, 1.0, 0.0)
    row_ids = lax.broadcasted_iota(jnp.int32, (8, ROWS), 1).astype(jnp.float32)
    row_of_slot = lax.dot_general(row_ids, hit, (((1,), (1,)), ((), ())), preferred_element_type=jnp.float32)
    slot_v[...] = jnp.clip(row_of_slot.astype(jnp.int32), 0, ROWS - 1)
    counts = jnp.broadcast_to(counts_v[...].astype(jnp.float32), (8, DEVICES))
    earlier = jnp.where(
        lax.broadcasted_iota(jnp.int32, (DEVICES, DEVICES), 0) < lax.broadcasted_iota(jnp.int32, (DEVICES, DEVICES), 1),
        1.0, 0.0,
    )
    before = lax.dot_general(counts, earlier, (((1,), (0,)), ((), ())), preferred_element_type=jnp.float32)[0:1, :]
    rows_down = lax.broadcasted_iota(jnp.int32, (ROWS, DEVICES), 0).astype(jnp.float32)
    owner_ids = lax.broadcasted_iota(jnp.int32, (ROWS, DEVICES), 1).astype(jnp.float32)
    offset = rows_down - before
    from_owner = (offset >= 0.0) & (offset < counts[0:1, :])
    slot_here = jnp.where(from_owner, owner_ids * CAP + offset, 0.0)
    slot_of_new = lax.dot_general(
        jnp.ones((8, DEVICES), jnp.float32), slot_here, (((1,), (1,)), ((), ())), preferred_element_type=jnp.float32
    )
    row_v[...] = jnp.clip(slot_of_new.astype(jnp.int32), 0, DEVICES * CAP - 1)
    slot_copy = pltpu.make_async_copy(slot_v, slot_s, small_sem.at[3])
    row_copy = pltpu.make_async_copy(row_v, row_s, small_sem.at[4])
    slot_copy.start()
    row_copy.start()

    def pair_copy(step):
        return pltpu.make_async_remote_copy(
            src_ref=pair_out.at[step], dst_ref=pair_in.at[step], send_sem=pair_send.at[step],
            recv_sem=pair_recv.at[step], device_id=(x * 2 + 1 - core, fsdp), device_id_type=MESH,
        )

    def along_x(way):
        return ((x + (1 if way == 0 else 3)) % 4) * 2 + core, fsdp

    half = (pl.ds(0, TILES // 2), pl.ds(TILES // 2, TILES // 2))

    def hop_copy(way):
        return pltpu.make_async_remote_copy(
            src_ref=sums.at[0, half[way]], dst_ref=hop_in.at[way], send_sem=hop_send.at[way],
            recv_sem=hop_recv.at[way], device_id=along_x(way), device_id_type=MESH,
        )

    def last_copy(way):
        return pltpu.make_async_remote_copy(
            src_ref=sums.at[1 + way, half[1 - way]], dst_ref=last_in.at[way], send_sem=last_send.at[way],
            recv_sem=last_recv.at[way], device_id=along_x(way), device_id_type=MESH,
        )

    def acc_copy(way, part):
        rows = pl.ds(part * CHUNK, CHUNK)
        return pltpu.make_async_remote_copy(
            src_ref=sums.at[1 + way, half[way], rows], dst_ref=acc_in.at[half[way], rows],
            send_sem=acc_send.at[way, part], recv_sem=acc_recv.at[way, part],
            device_id=along_x(way), device_id_type=MESH,
        )

    def add_pair(step):
        term_load(0, step).wait()
        pair_copy(step).wait_recv()

        def add(i, carry):
            rows = pl.ds(pl.multiple_of(i * 16, 16), 16)
            for j in range(TILES):
                own = terms[0, step, rows, pl.ds(j * LANES, LANES)].astype(jnp.float32)
                sums[step, j, rows, :] = own + pair_in[step, j, rows, :]
            return carry

        lax.fori_loop(0, ROWS // 16, add, 0)

    place_in_row = (
        lax.broadcasted_iota(jnp.int32, (TILES, LANES), 0) * LANES + lax.broadcasted_iota(jnp.int32, (TILES, LANES), 1)
    )

    def pack(device, slot):
        row = slot_s[0, device * CAP + slot]
        live = place_in_row < frag_s[2, row]
        values = [state[a, pl.ds(row, TILES, stride=ROWS), :] for a in range(3)]
        return [jnp.where(live, v, 0.0 if a < 2 else -1.0) for a, v in enumerate(values)]

    def post(i, carry):
        target = partner((i * 45) % DEVICES)
        device = target[0] * N_FSDP + target[1]
        for slot in range(CAP):
            for a, v in enumerate(pack(device, slot)):
                send[i, slot, pl.ds(a * TILES, TILES), :] = v
        pltpu.make_async_remote_copy(
            src_ref=send.at[i], dst_ref=recv.at[pl.ds(me * CAP, CAP)], send_sem=packet_send, recv_sem=packet_recv,
            device_id=target, device_id_type=MESH,
        ).start()
        return carry

    pl.semaphore_wait(barrier, N_CTX - 1 + 6)
    for step in range(4):
        pair_copy(step).start()
    for k in range(1, 4):
        pl.semaphore_signal(y_sem, inc=1, device_id=y_peer(k), device_id_type=MESH)
    add_pair(0)
    hop_copy(0).start()
    hop_copy(1).start()
    pl.semaphore_wait(y_sem, 3)
    for k in range(1, 4):
        pl.semaphore_signal(z_sem, inc=1, device_id=z_peer(k), device_id_type=MESH)
    for way in range(2):
        add_pair(1 + way)
        last_copy(way).start()
    for load in state_loads:
        load.wait()
    frag_load_s.wait()
    slot_copy.wait()
    row_copy.wait()
    pl.semaphore_wait(z_sem, 3)

    lax.fori_loop(1, DEVICES, post, 0)

    for way in range(2):
        hop_copy(way).wait()

        def add_hop(i, carry, way=way):
            rows = pl.ds(pl.multiple_of(i * 16, 16), 16)
            for j in range(TILES // 2):
                sums[1 + way, way * (TILES // 2) + j, rows, :] += hop_in[way, j, rows, :]
            return carry

        lax.fori_loop(0, ROWS // 16, add_hop, 0)
        last_copy(way).wait_send()
    for part in range(PARTS):
        for way in range(2):
            acc_copy(way, part).start()

    for slot in range(CAP):
        for a, v in enumerate(pack(me, slot)):
            recv[me * CAP + slot, pl.ds(a * TILES, TILES), :] = v
    add_pair(3)
    for way in range(2):
        last_copy(way).wait_recv()

    def add_last(i, carry):
        rows = pl.ds(pl.multiple_of(i * 16, 16), 16)
        for j in range(TILES):
            near = last_in[1, j, rows, :] if j < TILES // 2 else last_in[0, j - TILES // 2, rows, :]
            total[pl.ds(pl.multiple_of(j * ROWS + i * 16, 16), 16), :] = sums[3, j, rows, :] + near
        return carry

    lax.fori_loop(0, ROWS // 16, add_last, 0)

    all_here = recv.at[pl.ds(0, (DEVICES - 1) * CAP)]
    pltpu.make_async_copy(all_here, all_here, packet_recv).wait()

    def update(row, carry):
        slot = row_s[0, row]
        master, moment, second = [recv[slot, pl.ds(a * TILES, TILES), :] for a in range(3)]
        live = second >= 0.0
        second = jnp.where(live, second, 0.0)
        grad = jnp.where(live, total[pl.ds(row, TILES, stride=ROWS), :], 0.0)
        new_moment = beta_one * moment + (1.0 - beta_one) * grad
        new_second = beta_two * second + (1.0 - beta_two) * grad * grad
        moment_hat = new_moment / (1.0 - beta_one**step_count)
        second_hat = new_second / (1.0 - beta_two**step_count)
        new_master = master - learn_rate * (
            moment_hat / (jnp.sqrt(second_hat) + epsilon) + decay_weight * master
        )
        for a, v in enumerate((new_master, new_moment, new_second)):
            out[a, pl.ds(row, TILES, stride=ROWS), :] = v
        return carry

    for part in range(PARTS):
        for way in range(2):
            acc_copy(way, part).wait_recv()
        for j in range(TILES):
            total[pl.ds(j * ROWS + part * CHUNK, CHUNK), :] += acc_in[j, pl.ds(part * CHUNK, CHUNK), :]
        lax.fori_loop(part * CHUNK, (part + 1) * CHUNK, update, 0, unroll=4)

    all_sent = send.at[pl.ds(1, DEVICES - 1)]
    pltpu.make_async_copy(all_sent, all_sent, packet_send).wait()
    for step in range(4):
        pair_copy(step).wait_send()
    for way in range(2):
        for part in range(PARTS):
            acc_copy(way, part).wait_send()


def write_out(updated, master_hbm, moment_hbm, second_hbm, sem):
    stores = []
    for a, target in enumerate((master_hbm, moment_hbm, second_hbm)):
        for j in range(TILES):
            stores.append(
                pltpu.make_async_copy(
                    updated.at[a, pl.ds(j * ROWS, ROWS)], target.at[:, pl.ds(j * LANES, LANES)], sem.at[a, j]
                )
            )
    for store in stores:
        store.start()
    for store in stores:
        store.wait()


def local(old_master, old_moment, old_second, frag_list, pair_counts, grad_partial):
    anywhere = pl.BlockSpec(memory_space=pl.ANY)
    on_chip = pl.BlockSpec(memory_space=pltpu.VMEM)
    shape = jax.ShapeDtypeStruct((ROWS, FRAG), jnp.float32)
    f32, i32 = jnp.float32, jnp.int32
    dma = pltpu.SemaphoreType.DMA
    arguments = (old_master, old_moment, old_second, frag_list, pair_counts.reshape(1, DEVICES), grad_partial)
    updated = pl.pallas_call(
        kernel,
        out_shape=pltpu.VMEM((3, TILES * ROWS, LANES), f32),
        in_specs=[anywhere] * 6,
        out_specs=on_chip,
        scratch_shapes=[
            pltpu.VMEM((3, TILES * ROWS, LANES), f32),
            pltpu.VMEM((3, ROWS), i32),
            pltpu.VMEM((1, DEVICES), i32),
            pltpu.VMEM((8, DEVICES * CAP), i32),
            pltpu.VMEM((8, ROWS), i32),
            pltpu.SMEM((3, ROWS), i32),
            pltpu.SMEM((8, DEVICES * CAP), i32),
            pltpu.SMEM((8, ROWS), i32),
            pltpu.VMEM((DEVICES, CAP, 3 * TILES, LANES), f32),
            pltpu.VMEM((DEVICES * CAP, 3 * TILES, LANES), f32),
            pltpu.VMEM((2, 4, ROWS, FRAG), jnp.bfloat16),
            pltpu.VMEM((4, TILES, ROWS, LANES), f32),
            pltpu.VMEM((4, TILES, ROWS, LANES), f32),
            pltpu.VMEM((4, TILES, ROWS, LANES), f32),
            pltpu.VMEM((2, TILES // 2, ROWS, LANES), f32),
            pltpu.VMEM((2, TILES // 2, ROWS, LANES), f32),
            pltpu.VMEM((TILES, ROWS, LANES), f32),
            pltpu.VMEM((TILES * ROWS, LANES), f32),
            dma((3, TILES)),
            dma((5,)),
            dma((2, 4)),
            dma,
            dma,
            dma((4,)),
            dma((4,)),
            dma((2,)),
            dma((2,)),
            dma((2,)),
            dma((2,)),
            dma((2, PARTS)),
            dma((2, PARTS)),
            pltpu.SemaphoreType.REGULAR,
            pltpu.SemaphoreType.REGULAR,
        ],
        compiler_params=pltpu.CompilerParams(
            collective_id=0, has_side_effects=True, vmem_limit_bytes=48 * 1024 * 1024
        ),
    )(*[pltpu.with_memory_space_constraint(a, pltpu.HBM) for a in arguments])
    return pl.pallas_call(
        write_out,
        out_shape=(shape, shape, shape),
        in_specs=[on_chip],
        out_specs=(anywhere, anywhere, anywhere),
        scratch_shapes=[dma((3, TILES))],
    )(updated)


def solution(mesh):
    return jax.shard_map(
        local,
        mesh=mesh,
        in_specs=(
            P(("ctx", "fsdp"), None),
            P(("ctx", "fsdp"), None),
            P(("ctx", "fsdp"), None),
            P(None, ("ctx", "fsdp")),
            P(None, ("ctx", "fsdp")),
            P("ctx", None, "fsdp", None, None),
        ),
        out_specs=(P(("ctx", "fsdp"), None), P(("ctx", "fsdp"), None), P(("ctx", "fsdp"), None)),
        check_vma=False,
    )
```

```python
import functools

import jax
import jax.numpy as jnp
from jax import lax
from jax.experimental import pallas as pl
from jax.experimental.pallas import tpu as pltpu
from jax.sharding import PartitionSpec as P

MESH = pl.DeviceIdType.MESH

beta_one = 0.9
beta_two = 0.95
learn_rate = 0.0003
decay_weight = 0.1
epsilon = 1e-08
step_count = 1001.0

ROWS = 128
FRAG = 1024
TILES = 8
LANES = 128
N_CTX = 8
N_FSDP = 16
DEVICES = 128
CAP = 2


def place():
    ctx, fsdp = lax.axis_index("ctx"), lax.axis_index("fsdp")
    return ctx // 2, ctx % 2, fsdp // 4, fsdp % 4


def partner(dx, dy, dz, dcore):
    x, core, z, y = place()
    return ((x + dx) % 4) * 2 + (core + dcore) % 2, ((z + dz) % 4) * 4 + (y + dy) % 4


def kernel(
    master_hbm, moment_hbm, second_hbm, frag_hbm, counts_hbm, grad_hbm,
    out,
    state, frag_v, counts_v, slot_v, row_v, frag_s, slot_s, row_s,
    send, recv, terms, pair_out, pair_in, sums, hop_in, last_in, acc_in, total,
    state_sem, small_sem, terms_sem,
    packet_send, packet_recv, pair_send, pair_recv, hop_send, hop_recv, last_send, last_recv, acc_send, acc_recv,
    y_sem, z_sem,
):
    ctx, fsdp = lax.axis_index("ctx"), lax.axis_index("fsdp")
    x, core, z, y = place()
    me = ctx * N_FSDP + fsdp
    order = [(x + 2) % 4, (x + 1) % 4, (x + 3) % 4, x]

    def term_load(side, step):
        block = order[step] * 2 + (core + side) % 2
        return pltpu.make_async_copy(grad_hbm.at[0, block, 0], terms.at[side, step], terms_sem.at[side, step])

    def y_peer(k):
        return ctx, z * 4 + (y + k) % 4

    def z_peer(k):
        return ctx, ((z + k) % 4) * 4 + y

    barrier = pltpu.get_barrier_semaphore()
    for k in range(1, N_CTX):
        pl.semaphore_signal(barrier, inc=1, device_id=((ctx + k) % N_CTX, fsdp), device_id_type=MESH)
    for k in range(1, 4):
        pl.semaphore_signal(barrier, inc=1, device_id=y_peer(k), device_id_type=MESH)
    for k in range(1, 4):
        pl.semaphore_signal(barrier, inc=1, device_id=z_peer(k), device_id_type=MESH)

    for step in range(4):
        term_load(1, step).start()
    frag_load = pltpu.make_async_copy(frag_hbm, frag_v, small_sem.at[0])
    frag_load_s = pltpu.make_async_copy(frag_hbm, frag_s, small_sem.at[1])
    counts_load = pltpu.make_async_copy(counts_hbm, counts_v, small_sem.at[2])
    frag_load.start()
    frag_load_s.start()
    counts_load.start()
    for step in range(4):
        term_load(0, step).start()
    state_loads = []
    for a, source in enumerate((master_hbm, moment_hbm, second_hbm)):
        for j in range(TILES):
            state_loads.append(
                pltpu.make_async_copy(
                    source.at[:, pl.ds(j * LANES, LANES)],
                    state.at[a, pl.ds(j * ROWS, ROWS)],
                    state_sem.at[a, j],
                )
            )
    for load in state_loads:
        load.start()

    for step in range(4):
        term_load(1, step).wait()

        def widen(i, carry, step=step):
            rows = pl.ds(pl.multiple_of(i * 16, 16), 16)
            for j in range(TILES):
                pair_out[step, j, rows, :] = terms[1, step, rows, pl.ds(j * LANES, LANES)].astype(jnp.float32)
            return carry

        lax.fori_loop(0, ROWS // 16, widen, 0)

    frag_load.wait()
    counts_load.wait()
    owners, offsets = frag_v[pl.ds(0, 1), :], frag_v[pl.ds(1, 1), :]
    slot_of_row = owners * CAP + offsets
    slot_ids = lax.broadcasted_iota(jnp.int32, (DEVICES * CAP, ROWS), 0)
    hit = jnp.where(slot_ids == slot_of_row, 1.0, 0.0)
    row_ids = lax.broadcasted_iota(jnp.int32, (8, ROWS), 1).astype(jnp.float32)
    row_of_slot = lax.dot_general(row_ids, hit, (((1,), (1,)), ((), ())), preferred_element_type=jnp.float32)
    slot_v[...] = jnp.clip(row_of_slot.astype(jnp.int32), 0, ROWS - 1)
    counts = jnp.broadcast_to(counts_v[...].astype(jnp.float32), (8, DEVICES))
    earlier = jnp.where(
        lax.broadcasted_iota(jnp.int32, (DEVICES, DEVICES), 0) < lax.broadcasted_iota(jnp.int32, (DEVICES, DEVICES), 1),
        1.0, 0.0,
    )
    before = lax.dot_general(counts, earlier, (((1,), (0,)), ((), ())), preferred_element_type=jnp.float32)[0:1, :]
    rows_down = lax.broadcasted_iota(jnp.int32, (ROWS, DEVICES), 0).astype(jnp.float32)
    owner_ids = lax.broadcasted_iota(jnp.int32, (ROWS, DEVICES), 1).astype(jnp.float32)
    offset = rows_down - before
    from_owner = (offset >= 0.0) & (offset < counts[0:1, :])
    slot_here = jnp.where(from_owner, owner_ids * CAP + offset, 0.0)
    slot_of_new = lax.dot_general(
        jnp.ones((8, DEVICES), jnp.float32), slot_here, (((1,), (1,)), ((), ())), preferred_element_type=jnp.float32
    )
    row_v[...] = jnp.clip(slot_of_new.astype(jnp.int32), 0, DEVICES * CAP - 1)
    slot_copy = pltpu.make_async_copy(slot_v, slot_s, small_sem.at[3])
    row_copy = pltpu.make_async_copy(row_v, row_s, small_sem.at[4])
    slot_copy.start()
    row_copy.start()

    def pair_copy(step):
        return pltpu.make_async_remote_copy(
            src_ref=pair_out.at[step], dst_ref=pair_in.at[step], send_sem=pair_send.at[step],
            recv_sem=pair_recv.at[step], device_id=(x * 2 + 1 - core, fsdp), device_id_type=MESH,
        )

    def along_x(way):
        return ((x + (1 if way == 0 else 3)) % 4) * 2 + core, fsdp

    half = (pl.ds(0, TILES // 2), pl.ds(TILES // 2, TILES // 2))

    def hop_copy(way):
        return pltpu.make_async_remote_copy(
            src_ref=sums.at[0, half[way]], dst_ref=hop_in.at[way], send_sem=hop_send.at[way],
            recv_sem=hop_recv.at[way], device_id=along_x(way), device_id_type=MESH,
        )

    def last_copy(way):
        return pltpu.make_async_remote_copy(
            src_ref=sums.at[1 + way, half[1 - way]], dst_ref=last_in.at[way], send_sem=last_send.at[way],
            recv_sem=last_recv.at[way], device_id=along_x(way), device_id_type=MESH,
        )

    def acc_copy(way):
        return pltpu.make_async_remote_copy(
            src_ref=sums.at[1 + way, half[way]], dst_ref=acc_in.at[half[way]],
            send_sem=acc_send.at[way], recv_sem=acc_recv.at[way],
            device_id=along_x(way), device_id_type=MESH,
        )

    def add_pair(step):
        term_load(0, step).wait()
        pair_copy(step).wait_recv()

        def add(i, carry):
            rows = pl.ds(pl.multiple_of(i * 16, 16), 16)
            for j in range(TILES):
                own = terms[0, step, rows, pl.ds(j * LANES, LANES)].astype(jnp.float32)
                sums[step, j, rows, :] = own + pair_in[step, j, rows, :]
            return carry

        lax.fori_loop(0, ROWS // 16, add, 0)

    place_in_row = (
        lax.broadcasted_iota(jnp.int32, (TILES, LANES), 0) * LANES + lax.broadcasted_iota(jnp.int32, (TILES, LANES), 1)
    )

    def pack(device, slot):
        row = slot_s[0, device * CAP + slot]
        live = place_in_row < frag_s[2, row]
        values = [state[a, pl.ds(row, TILES, stride=ROWS), :] for a in range(3)]
        return [jnp.where(live, v, 0.0 if a < 2 else -1.0) for a, v in enumerate(values)]

    def post(dx, dy, dz, dcore):
        target = partner(dx, dy, dz, dcore)
        device, k = target[0] * N_FSDP + target[1], dx + 4 * dy + 16 * dz + 64 * dcore
        for slot in range(CAP):
            for a, v in enumerate(pack(device, slot)):
                send[k, slot, pl.ds(a * TILES, TILES), :] = v
        pltpu.make_async_remote_copy(
            src_ref=send.at[k], dst_ref=recv.at[pl.ds(me * CAP, CAP)],
            send_sem=packet_send, recv_sem=packet_recv, device_id=target, device_id_type=MESH,
        ).start()

    def post_line(i, carry):
        post(i % 4, 0, 0, i // 4)
        return carry

    def post_plane(i, carry):
        dx, k = i % 4, i // 4
        post(dx, 1 + (dx + k) % 3, 0, k // 3)
        return carry

    def post_rest(i, carry):
        dx, k = i % 4, i // 4
        post(dx, (dx + k) % 4, 1 + (dx + k // 4) % 3, k // 12)
        return carry

    for load in state_loads:
        load.wait()
    frag_load_s.wait()
    slot_copy.wait()
    row_copy.wait()
    pl.semaphore_wait(barrier, N_CTX - 1 + 6)
    for step in range(4):
        pair_copy(step).start()
    for k in range(1, 4):
        pl.semaphore_signal(y_sem, inc=1, device_id=y_peer(k), device_id_type=MESH)
    lax.fori_loop(1, N_CTX, post_line, 0)
    pl.semaphore_wait(y_sem, 3)
    for k in range(1, 4):
        pl.semaphore_signal(z_sem, inc=1, device_id=z_peer(k), device_id_type=MESH)
    add_pair(0)
    hop_copy(0).start()
    hop_copy(1).start()
    lax.fori_loop(0, 24, post_plane, 0)
    for way in range(2):
        add_pair(1 + way)
        last_copy(way).start()
    pl.semaphore_wait(z_sem, 3)
    lax.fori_loop(0, 96, post_rest, 0)

    for way in range(2):
        hop_copy(way).wait()

        def add_hop(i, carry, way=way):
            rows = pl.ds(pl.multiple_of(i * 16, 16), 16)
            for j in range(TILES // 2):
                sums[1 + way, way * (TILES // 2) + j, rows, :] += hop_in[way, j, rows, :]
            return carry

        lax.fori_loop(0, ROWS // 16, add_hop, 0)
        last_copy(way).wait_send()
        acc_copy(way).start()

    for slot in range(CAP):
        for a, v in enumerate(pack(me, slot)):
            recv[me * CAP + slot, pl.ds(a * TILES, TILES), :] = v
    add_pair(3)
    for way in range(2):
        last_copy(way).wait_recv()
    for way in range(2):
        acc_copy(way).wait_recv()

    def add_last(i, carry):
        rows = pl.ds(pl.multiple_of(i * 16, 16), 16)
        for j in range(TILES):
            near = last_in[1, j, rows, :] if j < TILES // 2 else last_in[0, j - TILES // 2, rows, :]
            total[pl.ds(pl.multiple_of(j * ROWS + i * 16, 16), 16), :] = (
                sums[3, j, rows, :] + near + acc_in[j, rows, :]
            )
        return carry

    lax.fori_loop(0, ROWS // 16, add_last, 0)

    all_here = recv.at[pl.ds(0, (DEVICES - 1) * CAP)]
    pltpu.make_async_copy(all_here, all_here, packet_recv).wait()

    def update(row, carry):
        slot = row_s[0, row]
        master, moment, second = [recv[slot, pl.ds(a * TILES, TILES), :] for a in range(3)]
        live = second >= 0.0
        second = jnp.where(live, second, 0.0)
        grad = jnp.where(live, total[pl.ds(row, TILES, stride=ROWS), :], 0.0)
        new_moment = beta_one * moment + (1.0 - beta_one) * grad
        new_second = beta_two * second + (1.0 - beta_two) * grad * grad
        moment_hat = new_moment / (1.0 - beta_one**step_count)
        second_hat = new_second / (1.0 - beta_two**step_count)
        new_master = master - learn_rate * (
            moment_hat / (jnp.sqrt(second_hat) + epsilon) + decay_weight * master
        )
        for a, v in enumerate((new_master, new_moment, new_second)):
            out[a, pl.ds(row, TILES, stride=ROWS), :] = v
        return carry

    lax.fori_loop(0, ROWS, update, 0, unroll=8)

    all_sent = send.at[pl.ds(1, DEVICES - 1)]
    pltpu.make_async_copy(all_sent, all_sent, packet_send).wait()
    for step in range(4):
        pair_copy(step).wait_send()
    for way in range(2):
        acc_copy(way).wait_send()


def write_out(updated, master_hbm, moment_hbm, second_hbm, sem):
    stores = []
    for a, target in enumerate((master_hbm, moment_hbm, second_hbm)):
        for j in range(TILES):
            stores.append(
                pltpu.make_async_copy(
                    updated.at[a, pl.ds(j * ROWS, ROWS)], target.at[:, pl.ds(j * LANES, LANES)], sem.at[a, j]
                )
            )
    for store in stores:
        store.start()
    for store in stores:
        store.wait()


def local(old_master, old_moment, old_second, frag_list, pair_counts, grad_partial):
    anywhere = pl.BlockSpec(memory_space=pl.ANY)
    on_chip = pl.BlockSpec(memory_space=pltpu.VMEM)
    shape = jax.ShapeDtypeStruct((ROWS, FRAG), jnp.float32)
    f32, i32 = jnp.float32, jnp.int32
    dma = pltpu.SemaphoreType.DMA
    arguments = (old_master, old_moment, old_second, frag_list, pair_counts.reshape(1, DEVICES), grad_partial)
    updated = pl.pallas_call(
        kernel,
        out_shape=pltpu.VMEM((3, TILES * ROWS, LANES), f32),
        in_specs=[anywhere] * 6,
        out_specs=on_chip,
        scratch_shapes=[
            pltpu.VMEM((3, TILES * ROWS, LANES), f32),
            pltpu.VMEM((3, ROWS), i32),
            pltpu.VMEM((1, DEVICES), i32),
            pltpu.VMEM((8, DEVICES * CAP), i32),
            pltpu.VMEM((8, ROWS), i32),
            pltpu.SMEM((3, ROWS), i32),
            pltpu.SMEM((8, DEVICES * CAP), i32),
            pltpu.SMEM((8, ROWS), i32),
            pltpu.VMEM((DEVICES, CAP, 3 * TILES, LANES), f32),
            pltpu.VMEM((DEVICES * CAP, 3 * TILES, LANES), f32),
            pltpu.VMEM((2, 4, ROWS, FRAG), jnp.bfloat16),
            pltpu.VMEM((4, TILES, ROWS, LANES), f32),
            pltpu.VMEM((4, TILES, ROWS, LANES), f32),
            pltpu.VMEM((4, TILES, ROWS, LANES), f32),
            pltpu.VMEM((2, TILES // 2, ROWS, LANES), f32),
            pltpu.VMEM((2, TILES // 2, ROWS, LANES), f32),
            pltpu.VMEM((TILES, ROWS, LANES), f32),
            pltpu.VMEM((TILES * ROWS, LANES), f32),
            dma((3, TILES)),
            dma((5,)),
            dma((2, 4)),
            dma,
            dma,
            dma((4,)),
            dma((4,)),
            dma((2,)),
            dma((2,)),
            dma((2,)),
            dma((2,)),
            dma((2,)),
            dma((2,)),
            pltpu.SemaphoreType.REGULAR,
            pltpu.SemaphoreType.REGULAR,
        ],
        compiler_params=pltpu.CompilerParams(
            collective_id=0, has_side_effects=True, vmem_limit_bytes=48 * 1024 * 1024
        ),
    )(*[pltpu.with_memory_space_constraint(a, pltpu.HBM) for a in arguments])
    return pl.pallas_call(
        write_out,
        out_shape=(shape, shape, shape),
        in_specs=[anywhere],
        out_specs=(anywhere, anywhere, anywhere),
        scratch_shapes=[dma((3, TILES))],
        compiler_params=pltpu.CompilerParams(vmem_limit_bytes=1024 * 1024),
    )(pltpu.with_memory_space_constraint(updated, pltpu.VMEM))


def solution(mesh):
    return jax.shard_map(
        local,
        mesh=mesh,
        in_specs=(
            P(("ctx", "fsdp"), None),
            P(("ctx", "fsdp"), None),
            P(("ctx", "fsdp"), None),
            P(None, ("ctx", "fsdp")),
            P(None, ("ctx", "fsdp")),
            P("ctx", None, "fsdp", None, None),
        ),
        out_specs=(P(("ctx", "fsdp"), None), P(("ctx", "fsdp"), None), P(("ctx", "fsdp"), None)),
        check_vma=False,
    )
```

```python
import functools

import jax
import jax.numpy as jnp
from jax import lax
from jax.experimental import pallas as pl
from jax.experimental.pallas import tpu as pltpu
from jax.sharding import PartitionSpec as P

MESH = pl.DeviceIdType.MESH

beta_one = 0.9
beta_two = 0.95
learn_rate = 0.0003
decay_weight = 0.1
epsilon = 1e-08
step_count = 1001.0

ROWS = 128
FRAG = 1024
TILES = 8
LANES = 128
N_CTX = 8
N_FSDP = 16
DEVICES = 128
CAP = 2
COLUMN = 32
WIDE = COLUMN * CAP
ROOM = 48


def place():
    ctx, fsdp = lax.axis_index("ctx"), lax.axis_index("fsdp")
    return ctx // 2, ctx % 2, fsdp // 4, fsdp % 4


def partner(dx, dy, dz, dcore):
    x, core, z, y = place()
    return ((x + dx) % 4) * 2 + (core + dcore) % 2, ((z + dz) % 4) * 4 + (y + dy) % 4


def kernel(
    master_hbm, moment_hbm, second_hbm, frag_hbm, counts_hbm, grad_hbm,
    out,
    state, frag_v, counts_v, slot_v, row_v, frag_s, slot_s, row_s,
    send, recv, terms, pair_out, pair_in, sums, hop_in, last_in, acc_in, total,
    state_sem, small_sem, terms_sem,
    packet_send, packet_recv, pair_send, pair_recv, hop_send, hop_recv, last_send, last_recv, acc_send, acc_recv,
    y_sem, z_sem,
):
    ctx, fsdp = lax.axis_index("ctx"), lax.axis_index("fsdp")
    x, core, z, y = place()
    me = ctx * N_FSDP + fsdp
    order = [(x + 2) % 4, (x + 1) % 4, (x + 3) % 4, x]

    def term_load(side, step):
        block = order[step] * 2 + (core + side) % 2
        return pltpu.make_async_copy(grad_hbm.at[0, block, 0], terms.at[side, step], terms_sem.at[side, step])

    def y_peer(k):
        return ctx, z * 4 + (y + k) % 4

    def z_peer(k):
        return ctx, ((z + k) % 4) * 4 + y

    barrier = pltpu.get_barrier_semaphore()
    for k in range(1, N_CTX):
        pl.semaphore_signal(barrier, inc=1, device_id=((ctx + k) % N_CTX, fsdp), device_id_type=MESH)
    for k in range(1, 4):
        pl.semaphore_signal(barrier, inc=1, device_id=y_peer(k), device_id_type=MESH)
    for k in range(1, 4):
        pl.semaphore_signal(barrier, inc=1, device_id=z_peer(k), device_id_type=MESH)

    for step in range(4):
        term_load(1, step).start()
    frag_load = pltpu.make_async_copy(frag_hbm, frag_v, small_sem.at[0])
    frag_load_s = pltpu.make_async_copy(frag_hbm, frag_s, small_sem.at[1])
    counts_load = pltpu.make_async_copy(counts_hbm, counts_v, small_sem.at[2])
    frag_load.start()
    frag_load_s.start()
    counts_load.start()
    for step in range(4):
        term_load(0, step).start()
    state_loads = []
    for a, source in enumerate((master_hbm, moment_hbm, second_hbm)):
        for j in range(TILES):
            state_loads.append(
                pltpu.make_async_copy(
                    source.at[:, pl.ds(j * LANES, LANES)],
                    state.at[a, pl.ds(j * ROWS, ROWS)],
                    state_sem.at[a, j],
                )
            )
    for load in state_loads:
        load.start()

    for step in range(4):
        term_load(1, step).wait()

        def widen(i, carry, step=step):
            rows = pl.ds(pl.multiple_of(i * 16, 16), 16)
            for j in range(TILES):
                pair_out[step, j, rows, :] = terms[1, step, rows, pl.ds(j * LANES, LANES)].astype(jnp.float32)
            return carry

        lax.fori_loop(0, ROWS // 16, widen, 0)

    frag_load.wait()
    counts_load.wait()
    owners, offsets = frag_v[pl.ds(0, 1), :], frag_v[pl.ds(1, 1), :]
    slot_of_row = owners * CAP + offsets
    slot_ids = lax.broadcasted_iota(jnp.int32, (DEVICES * CAP, ROWS), 0)
    hit = jnp.where(slot_ids == slot_of_row, 1.0, 0.0)
    row_ids = lax.broadcasted_iota(jnp.int32, (8, ROWS), 1).astype(jnp.float32)
    row_of_slot = lax.dot_general(row_ids, hit, (((1,), (1,)), ((), ())), preferred_element_type=jnp.float32)
    slot_v[...] = jnp.clip(row_of_slot.astype(jnp.int32), 0, ROWS - 1)
    counts = jnp.broadcast_to(counts_v[...].astype(jnp.float32), (8, DEVICES))
    earlier = jnp.where(
        lax.broadcasted_iota(jnp.int32, (DEVICES, DEVICES), 0) < lax.broadcasted_iota(jnp.int32, (DEVICES, DEVICES), 1),
        1.0, 0.0,
    )
    before = lax.dot_general(counts, earlier, (((1,), (0,)), ((), ())), preferred_element_type=jnp.float32)[0:1, :]
    rows_down = lax.broadcasted_iota(jnp.int32, (ROWS, DEVICES), 0).astype(jnp.float32)
    owner_ids = lax.broadcasted_iota(jnp.int32, (ROWS, DEVICES), 1).astype(jnp.float32)
    offset = rows_down - before
    from_owner = (offset >= 0.0) & (offset < counts[0:1, :])
    slot_here = jnp.where(from_owner, owner_ids * CAP + offset, 0.0)
    slot_of_new = lax.dot_general(
        jnp.ones((8, DEVICES), jnp.float32), slot_here, (((1,), (1,)), ((), ())), preferred_element_type=jnp.float32
    )
    row_v[...] = jnp.clip(slot_of_new.astype(jnp.int32), 0, DEVICES * CAP - 1)
    slot_copy = pltpu.make_async_copy(slot_v, slot_s, small_sem.at[3])
    row_copy = pltpu.make_async_copy(row_v, row_s, small_sem.at[4])
    slot_copy.start()
    row_copy.start()

    def pair_copy(step):
        return pltpu.make_async_remote_copy(
            src_ref=pair_out.at[step], dst_ref=pair_in.at[step], send_sem=pair_send.at[step],
            recv_sem=pair_recv.at[step], device_id=(x * 2 + 1 - core, fsdp), device_id_type=MESH,
        )

    def along_x(way):
        return ((x + (1 if way == 0 else 3)) % 4) * 2 + core, fsdp

    half = (pl.ds(0, TILES // 2), pl.ds(TILES // 2, TILES // 2))

    def hop_copy(way):
        return pltpu.make_async_remote_copy(
            src_ref=sums.at[0, half[way]], dst_ref=hop_in.at[way], send_sem=hop_send.at[way],
            recv_sem=hop_recv.at[way], device_id=along_x(way), device_id_type=MESH,
        )

    def last_copy(way):
        return pltpu.make_async_remote_copy(
            src_ref=sums.at[1 + way, half[1 - way]], dst_ref=last_in.at[way], send_sem=last_send.at[way],
            recv_sem=last_recv.at[way], device_id=along_x(way), device_id_type=MESH,
        )

    def acc_copy(way):
        return pltpu.make_async_remote_copy(
            src_ref=sums.at[1 + way, half[way]], dst_ref=acc_in.at[half[way]],
            send_sem=acc_send.at[way], recv_sem=acc_recv.at[way],
            device_id=along_x(way), device_id_type=MESH,
        )

    def add_pair(step):
        term_load(0, step).wait()
        pair_copy(step).wait_recv()

        def add(i, carry):
            rows = pl.ds(pl.multiple_of(i * 16, 16), 16)
            for j in range(TILES):
                own = terms[0, step, rows, pl.ds(j * LANES, LANES)].astype(jnp.float32)
                sums[step, j, rows, :] = own + pair_in[step, j, rows, :]
            return carry

        lax.fori_loop(0, ROWS // 16, add, 0)

    place_in_row = (
        lax.broadcasted_iota(jnp.int32, (TILES, LANES), 0) * LANES + lax.broadcasted_iota(jnp.int32, (TILES, LANES), 1)
    )

    def pack(device, slot):
        row = slot_s[0, device * CAP + slot]
        live = place_in_row < frag_s[2, row]
        values = [state[a, pl.ds(row, TILES, stride=ROWS), :] for a in range(3)]
        return [jnp.where(live, v, 0.0 if a < 2 else -1.0) for a, v in enumerate(values)]

    def post(dx, dy, dz, dcore):
        target = partner(dx, dy, dz, dcore)
        device, k = target[0] * N_FSDP + target[1], dx + 4 * dy + 16 * dz + 64 * dcore
        for slot in range(CAP):
            for a, v in enumerate(pack(device, slot)):
                send[k, slot, pl.ds(a * TILES, TILES), :] = v
        pltpu.make_async_remote_copy(
            src_ref=send.at[k], dst_ref=recv.at[pl.ds(me * CAP, CAP)],
            send_sem=packet_send, recv_sem=packet_recv, device_id=target, device_id_type=MESH,
        ).start()

    def post_line(i, carry):
        post(i % 4, 0, 0, i // 4)
        return carry

    def post_plane(i, carry):
        dx, k = i % 4, i // 4
        post(dx, 1 + (dx + k) % 3, 0, k // 3)
        return carry

    def post_rest(i, carry):
        dx, k = i % 4, i // 4
        post(dx, (dx + k) % 4, 1 + (dx + k // 4) % 3, k // 12)
        return carry

    for load in state_loads:
        load.wait()
    frag_load_s.wait()
    slot_copy.wait()
    row_copy.wait()
    pl.semaphore_wait(barrier, N_CTX - 1 + 6)
    for step in range(4):
        pair_copy(step).start()
    for k in range(1, 4):
        pl.semaphore_signal(y_sem, inc=1, device_id=y_peer(k), device_id_type=MESH)
    lax.fori_loop(1, N_CTX, post_line, 0)
    pl.semaphore_wait(y_sem, 3)
    for k in range(1, 4):
        pl.semaphore_signal(z_sem, inc=1, device_id=z_peer(k), device_id_type=MESH)
    add_pair(0)
    hop_copy(0).start()
    hop_copy(1).start()
    lax.fori_loop(0, 24, post_plane, 0)
    for way in range(2):
        add_pair(1 + way)
        last_copy(way).start()
    pl.semaphore_wait(z_sem, 3)
    lax.fori_loop(0, 96, post_rest, 0)

    for way in range(2):
        hop_copy(way).wait()

        def add_hop(i, carry, way=way):
            rows = pl.ds(pl.multiple_of(i * 16, 16), 16)
            for j in range(TILES // 2):
                sums[1 + way, way * (TILES // 2) + j, rows, :] += hop_in[way, j, rows, :]
            return carry

        lax.fori_loop(0, ROWS // 16, add_hop, 0)
        last_copy(way).wait_send()
        acc_copy(way).start()

    for slot in range(CAP):
        for a, v in enumerate(pack(me, slot)):
            recv[me * CAP + slot, pl.ds(a * TILES, TILES), :] = v
    add_pair(3)
    for way in range(2):
        last_copy(way).wait_recv()
    for way in range(2):
        acc_copy(way).wait_recv()

    def add_last(i, carry):
        rows = pl.ds(pl.multiple_of(i * 16, 16), 16)
        for j in range(TILES):
            near = last_in[1, j, rows, :] if j < TILES // 2 else last_in[0, j - TILES // 2, rows, :]
            total[pl.ds(pl.multiple_of(j * ROWS + i * 16, 16), 16), :] = (
                sums[3, j, rows, :] + near + acc_in[j, rows, :]
            )
        return carry

    lax.fori_loop(0, ROWS // 16, add_last, 0)

    all_here = recv.at[pl.ds(0, (DEVICES - 1) * CAP)]
    pltpu.make_async_copy(all_here, all_here, packet_recv).wait()

    def update(row, carry):
        slot = row_s[0, row]
        master, moment, second = [recv[slot, pl.ds(a * TILES, TILES), :] for a in range(3)]
        live = second >= 0.0
        second = jnp.where(live, second, 0.0)
        grad = jnp.where(live, total[pl.ds(row, TILES, stride=ROWS), :], 0.0)
        new_moment = beta_one * moment + (1.0 - beta_one) * grad
        new_second = beta_two * second + (1.0 - beta_two) * grad * grad
        moment_hat = new_moment / (1.0 - beta_one**step_count)
        second_hat = new_second / (1.0 - beta_two**step_count)
        new_master = master - learn_rate * (
            moment_hat / (jnp.sqrt(second_hat) + epsilon) + decay_weight * master
        )
        for a, v in enumerate((new_master, new_moment, new_second)):
            out[a, pl.ds(row, TILES, stride=ROWS), :] = v
        return carry

    lax.fori_loop(0, ROWS, update, 0, unroll=8)

    all_sent = send.at[pl.ds(1, DEVICES - 1)]
    pltpu.make_async_copy(all_sent, all_sent, packet_send).wait()
    for step in range(4):
        pair_copy(step).wait_send()
    for way in range(2):
        acc_copy(way).wait_send()


def kernel_fast(
    master_hbm, moment_hbm, second_hbm, frag_hbm, counts_hbm, grad_hbm,
    out, flag_out,
    state, frag_v, counts_v, rank_v, meta_v, row_v, frag_s, rank_s, own_s, meta_s, row_s,
    x_out, x_in_0, x_in_1, x_in_2, meta_in, near_out, far_out, flag_mine, flag_in, recv, terms, pair_out, pair_in, sums, hop_in, last_in, acc_in, total,
    state_sem, small_sem, terms_sem,
    x_send, x_recv, meta_send, meta_recv, near_send, near_recv, far_send, far_recv, flag_send, flag_recv, pair_send, pair_recv, hop_send, hop_recv, last_send, last_recv, acc_send, acc_recv,
    y_sem, z_sem,
):
    ctx, fsdp = lax.axis_index("ctx"), lax.axis_index("fsdp")
    x, core, z, y = place()
    here = core * N_FSDP + fsdp
    x_in = (x_in_0, x_in_1, x_in_2)
    order = [(x + 2) % 4, (x + 1) % 4, (x + 3) % 4, x]

    def term_load(side, step):
        block = order[step] * 2 + (core + side) % 2
        return pltpu.make_async_copy(grad_hbm.at[0, block, 0], terms.at[side, step], terms_sem.at[side, step])

    def x_peer(k):
        return ((x + k) % 4) * 2 + core, fsdp

    def y_peer(k):
        return ctx, z * 4 + (y + k) % 4

    def z_peer(k):
        return ctx, ((z + k) % 4) * 4 + y

    barrier = pltpu.get_barrier_semaphore()
    pl.semaphore_signal(barrier, inc=1, device_id=(x * 2 + 1 - core, fsdp), device_id_type=MESH)
    for k in range(1, 4):
        pl.semaphore_signal(barrier, inc=1, device_id=x_peer(k), device_id_type=MESH)
    for k in range(1, 4):
        pl.semaphore_signal(barrier, inc=1, device_id=y_peer(k), device_id_type=MESH)
    for k in range(1, 4):
        pl.semaphore_signal(barrier, inc=1, device_id=z_peer(k), device_id_type=MESH)

    for step in range(4):
        term_load(1, step).start()
    frag_load = pltpu.make_async_copy(frag_hbm, frag_v, small_sem.at[0])
    frag_load_s = pltpu.make_async_copy(frag_hbm, frag_s, small_sem.at[1])
    counts_load = pltpu.make_async_copy(counts_hbm, counts_v, small_sem.at[2])
    frag_load.start()
    frag_load_s.start()
    counts_load.start()
    for step in range(4):
        term_load(0, step).start()
    state_loads = []
    for a, source in enumerate((master_hbm, moment_hbm, second_hbm)):
        for j in range(TILES):
            state_loads.append(
                pltpu.make_async_copy(
                    source.at[:, pl.ds(j * LANES, LANES)],
                    state.at[a, pl.ds(j * ROWS, ROWS)],
                    state_sem.at[a, j],
                )
            )
    for load in state_loads:
        load.start()

    frag_load.wait()
    counts_load.wait()
    owners, offsets = frag_v[pl.ds(0, 1), :], frag_v[pl.ds(1, 1), :]
    column = (owners // COLUMN - x + 4) % 4
    in_column = jnp.where(lax.broadcasted_iota(jnp.int32, (8, ROWS), 0) == column, 1.0, 0.0)
    earlier = jnp.where(
        lax.broadcasted_iota(jnp.int32, (DEVICES, DEVICES), 0) < lax.broadcasted_iota(jnp.int32, (DEVICES, DEVICES), 1),
        1.0, 0.0,
    )
    ranks = lax.dot_general(in_column, earlier, (((1,), (0,)), ((), ())), preferred_element_type=jnp.float32)
    rank = jnp.sum(in_column * ranks, axis=0, keepdims=True)
    over = jnp.max(jnp.where((rank >= ROOM) & (column > 0), 1.0, 0.0), axis=1, keepdims=True)
    place_ids = lax.broadcasted_iota(jnp.int32, (DEVICES * CAP, ROWS), 0)
    by_rank = jnp.where(place_ids == column * WIDE + rank.astype(jnp.int32), 1.0, 0.0)
    by_slot = jnp.where(place_ids == column * WIDE + (owners % COLUMN) * CAP + offsets, 1.0, 0.0)
    row_ids = lax.broadcasted_iota(jnp.int32, (8, ROWS), 1).astype(jnp.float32)
    which = lax.broadcasted_iota(jnp.int32, (8, ROWS), 0)
    row_of_rank = lax.dot_general(row_ids, by_rank, (((1,), (1,)), ((), ())), preferred_element_type=jnp.float32)
    rank_v[...] = jnp.clip(row_of_rank.astype(jnp.int32), 0, ROWS - 1)
    of_slot = lax.dot_general(
        jnp.where(which == 0, row_ids, rank), by_slot, (((1,), (1,)), ((), ())), preferred_element_type=jnp.float32
    )
    line = lax.broadcasted_iota(jnp.int32, (8, DEVICES * CAP), 0)
    top = jnp.where(line == 0, ROWS - 1, ROOM - 1)
    meta = jnp.clip(of_slot.astype(jnp.int32), 0, top)
    meta_v[...] = jnp.where(line == 2, over.astype(jnp.int32), meta)
    counts = jnp.broadcast_to(counts_v[...].astype(jnp.float32), (8, DEVICES))
    before = lax.dot_general(counts, earlier, (((1,), (0,)), ((), ())), preferred_element_type=jnp.float32)[0:1, :]
    rows_down = lax.broadcasted_iota(jnp.int32, (ROWS, DEVICES), 0).astype(jnp.float32)
    owner_ids = lax.broadcasted_iota(jnp.int32, (ROWS, DEVICES), 1)
    first = ((owner_ids % COLUMN) * 8 + ((owner_ids // COLUMN - x + 4) % 4) * CAP).astype(jnp.float32)
    offset = rows_down - before
    from_owner = (offset >= 0.0) & (offset < counts[0:1, :])
    slot_here = jnp.where(from_owner, first + offset, 0.0)
    slot_of_new = lax.dot_general(
        jnp.ones((8, DEVICES), jnp.float32), slot_here, (((1,), (1,)), ((), ())), preferred_element_type=jnp.float32
    )
    row_v[...] = jnp.clip(slot_of_new.astype(jnp.int32), 0, DEVICES * CAP - 1)
    table_copies = [
        pltpu.make_async_copy(source, target, small_sem.at[3 + i])
        for i, (source, target) in enumerate(((rank_v, rank_s), (meta_v, own_s), (row_v, row_s)))
    ]
    for copy in table_copies:
        copy.start()

    for step in range(4):
        term_load(1, step).wait()

        def widen(i, carry, step=step):
            rows = pl.ds(pl.multiple_of(i * 16, 16), 16)
            for j in range(TILES):
                pair_out[step, j, rows, :] = terms[1, step, rows, pl.ds(j * LANES, LANES)].astype(jnp.float32)
            return carry

        lax.fori_loop(0, ROWS // 16, widen, 0)

    def pair_copy(step):
        return pltpu.make_async_remote_copy(
            src_ref=pair_out.at[step], dst_ref=pair_in.at[step], send_sem=pair_send.at[step],
            recv_sem=pair_recv.at[step], device_id=(x * 2 + 1 - core, fsdp), device_id_type=MESH,
        )

    def along_x(way):
        return ((x + (1 if way == 0 else 3)) % 4) * 2 + core, fsdp

    half = (pl.ds(0, TILES // 2), pl.ds(TILES // 2, TILES // 2))

    def hop_copy(way):
        return pltpu.make_async_remote_copy(
            src_ref=sums.at[0, half[way]], dst_ref=hop_in.at[way], send_sem=hop_send.at[way],
            recv_sem=hop_recv.at[way], device_id=along_x(way), device_id_type=MESH,
        )

    def last_copy(way):
        return pltpu.make_async_remote_copy(
            src_ref=sums.at[1 + way, half[1 - way]], dst_ref=last_in.at[way], send_sem=last_send.at[way],
            recv_sem=last_recv.at[way], device_id=along_x(way), device_id_type=MESH,
        )

    def acc_copy(way):
        return pltpu.make_async_remote_copy(
            src_ref=sums.at[1 + way, half[way]], dst_ref=acc_in.at[half[way]],
            send_sem=acc_send.at[way], recv_sem=acc_recv.at[way],
            device_id=along_x(way), device_id_type=MESH,
        )

    def add_pair(step):
        term_load(0, step).wait()
        pair_copy(step).wait_recv()

        def add(i, carry):
            rows = pl.ds(pl.multiple_of(i * 16, 16), 16)
            for j in range(TILES):
                own = terms[0, step, rows, pl.ds(j * LANES, LANES)].astype(jnp.float32)
                sums[step, j, rows, :] = own + pair_in[step, j, rows, :]
            return carry

        lax.fori_loop(0, ROWS // 16, add, 0)

    place_in_row = (
        lax.broadcasted_iota(jnp.int32, (TILES, LANES), 0) * LANES + lax.broadcasted_iota(jnp.int32, (TILES, LANES), 1)
    )

    def masked(a, row):
        live = place_in_row < frag_s[2, row]
        return jnp.where(live, state[a, pl.ds(row, TILES, stride=ROWS), :], -1.0 if a == 2 else 0.0)

    def fill_x(a):
        def fill(i, carry):
            for k in range(1, 4):
                x_out[a, k - 1, i] = masked(a, rank_s[0, k * WIDE + i])
            return carry

        lax.fori_loop(0, ROOM, fill, 0, unroll=4)

    def x_copy(a, k):
        return pltpu.make_async_remote_copy(
            src_ref=x_out.at[a, k - 1], dst_ref=x_in[a].at[3 - k], send_sem=x_send.at[a, k - 1],
            recv_sem=x_recv.at[a, 3 - k], device_id=x_peer(k), device_id_type=MESH,
        )

    def meta_copy(k):
        return pltpu.make_async_remote_copy(
            src_ref=meta_v, dst_ref=meta_in.at[3 - k], send_sem=meta_send.at[k - 1],
            recv_sem=meta_recv.at[3 - k], device_id=x_peer(k), device_id_type=MESH,
        )

    def column_peer(i):
        return partner(0, i % 4, (i + i // 4) % 4, i // 16)

    def post_near(i, carry):
        target = column_peer(i)
        there = (target[0] % 2) * N_FSDP + target[1]
        for slot in range(CAP):
            row = own_s[0, there * CAP + slot]
            for a in range(3):
                near_out[i, a, slot] = masked(a, row)
        pltpu.make_async_remote_copy(
            src_ref=near_out.at[i], dst_ref=recv.at[:, pl.ds(here * 8, CAP)],
            send_sem=near_send, recv_sem=near_recv, device_id=target, device_id_type=MESH,
        ).start()
        return carry

    def moved(a, there, origin, slot):
        return x_in[a][origin - 1, meta_s[origin - 1, 1, (4 - origin) * WIDE + there * CAP + slot]]

    def post_far(a):
        def post(i, carry):
            target = column_peer(i)
            there = (target[0] % 2) * N_FSDP + target[1]
            for origin in range(1, 4):
                for slot in range(CAP):
                    far_out[a, i, (origin - 1) * CAP + slot] = moved(a, there, origin, slot)
            pltpu.make_async_remote_copy(
                src_ref=far_out.at[a, i], dst_ref=recv.at[a, pl.ds(here * 8 + CAP, 3 * CAP)],
                send_sem=far_send.at[a], recv_sem=far_recv.at[a], device_id=target, device_id_type=MESH,
            ).start()
            return carry

        for k in range(1, 4):
            x_copy(a, k).wait_recv()
        lax.fori_loop(1, COLUMN, post, 0)
        for origin in range(1, 4):
            for slot in range(CAP):
                recv[a, here * 8 + origin * CAP + slot] = moved(a, here, origin, slot)

    def post_flag(i, carry):
        pltpu.make_async_remote_copy(
            src_ref=flag_mine, dst_ref=flag_in.at[here], send_sem=flag_send, recv_sem=flag_recv,
            device_id=column_peer(i), device_id_type=MESH,
        ).start()
        return carry

    for load in state_loads:
        load.wait()
    frag_load_s.wait()
    for copy in table_copies:
        copy.wait()
    fill_x(0)
    pl.semaphore_wait(barrier, 10)
    for k in (1, 3, 2):
        meta_copy(k).start()
    for k in (1, 3, 2):
        x_copy(0, k).start()
    for step in range(4):
        pair_copy(step).start()
    for k in range(1, 4):
        pl.semaphore_signal(y_sem, inc=1, device_id=y_peer(k), device_id_type=MESH)
    fill_x(1)
    for k in (1, 3, 2):
        x_copy(1, k).start()
    fill_x(2)
    for k in (1, 3, 2):
        x_copy(2, k).start()
    pl.semaphore_wait(y_sem, 3)
    for k in range(1, 4):
        pl.semaphore_signal(z_sem, inc=1, device_id=z_peer(k), device_id_type=MESH)
    add_pair(0)
    hop_copy(0).start()
    hop_copy(1).start()
    for way in range(2):
        add_pair(1 + way)
        last_copy(way).start()
    pl.semaphore_wait(z_sem, 3)
    lax.fori_loop(1, COLUMN, post_near, 0)
    for slot in range(CAP):
        row = own_s[0, here * CAP + slot]
        for a in range(3):
            recv[a, here * 8 + slot] = masked(a, row)
    for k in range(1, 4):
        meta_copy(k).wait_recv()
    flag = meta_v[pl.ds(2, 1), pl.ds(0, LANES)]
    for origin in range(3):
        flag = jnp.maximum(flag, meta_in[origin, pl.ds(2, 1), pl.ds(0, LANES)])
    flag = jnp.broadcast_to(flag.astype(jnp.float32), (8, LANES))
    flag_mine[...] = flag
    flag_in[here] = flag
    meta_load = pltpu.make_async_copy(meta_in, meta_s, small_sem.at[6])
    meta_load.start()
    lax.fori_loop(1, COLUMN, post_flag, 0)
    meta_load.wait()
    for a in range(3):
        post_far(a)
    for way in range(2):
        hop_copy(way).wait()

        def add_hop(i, carry, way=way):
            rows = pl.ds(pl.multiple_of(i * 16, 16), 16)
            for j in range(TILES // 2):
                sums[1 + way, way * (TILES // 2) + j, rows, :] += hop_in[way, j, rows, :]
            return carry

        lax.fori_loop(0, ROWS // 16, add_hop, 0)
        last_copy(way).wait_send()
        acc_copy(way).start()

    add_pair(3)
    for way in range(2):
        last_copy(way).wait_recv()
    for way in range(2):
        acc_copy(way).wait_recv()

    def add_last(i, carry):
        rows = pl.ds(pl.multiple_of(i * 16, 16), 16)
        for j in range(TILES):
            near = last_in[1, j, rows, :] if j < TILES // 2 else last_in[0, j - TILES // 2, rows, :]
            total[pl.ds(pl.multiple_of(j * ROWS + i * 16, 16), 16), :] = (
                sums[3, j, rows, :] + near + acc_in[j, rows, :]
            )
        return carry

    lax.fori_loop(0, ROWS // 16, add_last, 0)

    others = COLUMN - 1
    near_here = recv.at[:, pl.ds(0, others * CAP)]
    pltpu.make_async_copy(near_here, near_here, near_recv).wait()
    for a in range(3):
        far_here = recv.at[a, pl.ds(0, others * 3 * CAP)]
        pltpu.make_async_copy(far_here, far_here, far_recv.at[a]).wait()
    flags_here = flag_in.at[pl.ds(0, others)]
    pltpu.make_async_copy(flags_here, flags_here, flag_recv).wait()
    flag_out[...] = jnp.max(flag_in[...], axis=0)

    def update(row, carry):
        slot = row_s[0, row]
        master, moment, second = [recv[a, slot] for a in range(3)]
        live = second >= 0.0
        second = jnp.where(live, second, 0.0)
        grad = jnp.where(live, total[pl.ds(row, TILES, stride=ROWS), :], 0.0)
        new_moment = beta_one * moment + (1.0 - beta_one) * grad
        new_second = beta_two * second + (1.0 - beta_two) * grad * grad
        moment_hat = new_moment / (1.0 - beta_one**step_count)
        second_hat = new_second / (1.0 - beta_two**step_count)
        new_master = master - learn_rate * (
            moment_hat / (jnp.sqrt(second_hat) + epsilon) + decay_weight * master
        )
        for a, v in enumerate((new_master, new_moment, new_second)):
            out[a, pl.ds(row, TILES, stride=ROWS), :] = v
        return carry

    lax.fori_loop(0, ROWS, update, 0, unroll=8)

    near_sent = near_out.at[pl.ds(1, others)]
    pltpu.make_async_copy(near_sent, near_sent, near_send).wait()
    for a in range(3):
        far_sent = far_out.at[a, pl.ds(1, others)]
        pltpu.make_async_copy(far_sent, far_sent, far_send.at[a]).wait()
    flags_sent = flag_in.at[pl.ds(0, others)]
    pltpu.make_async_copy(flags_sent, flags_sent, flag_send).wait()
    for k in range(1, 4):
        meta_copy(k).wait_send()
        for a in range(3):
            x_copy(a, k).wait_send()
    for step in range(4):
        pair_copy(step).wait_send()
    for way in range(2):
        acc_copy(way).wait_send()


def write_out(updated, master_hbm, moment_hbm, second_hbm, sem):
    stores = []
    for a, target in enumerate((master_hbm, moment_hbm, second_hbm)):
        for j in range(TILES):
            stores.append(
                pltpu.make_async_copy(
                    updated.at[a, pl.ds(j * ROWS, ROWS)], target.at[:, pl.ds(j * LANES, LANES)], sem.at[a, j]
                )
            )
    for store in stores:
        store.start()
    for store in stores:
        store.wait()


def local(old_master, old_moment, old_second, frag_list, pair_counts, grad_partial):
    anywhere = pl.BlockSpec(memory_space=pl.ANY)
    on_chip = pl.BlockSpec(memory_space=pltpu.VMEM)
    shape = jax.ShapeDtypeStruct((ROWS, FRAG), jnp.float32)
    f32, i32 = jnp.float32, jnp.int32
    dma = pltpu.SemaphoreType.DMA
    arguments = (old_master, old_moment, old_second, frag_list, pair_counts.reshape(1, DEVICES), grad_partial)
    updated, flag = pl.pallas_call(
        kernel_fast,
        out_shape=(pltpu.VMEM((3, TILES * ROWS, LANES), f32), jax.ShapeDtypeStruct((8,128),f32)),
        in_specs=[anywhere] * 6,
        out_specs=(on_chip,on_chip),
        scratch_shapes=[
            pltpu.VMEM((3, TILES * ROWS, LANES), f32),
            pltpu.VMEM((3, ROWS), i32),
            pltpu.VMEM((1, DEVICES), i32),
            pltpu.VMEM((8, DEVICES * CAP), i32),
            pltpu.VMEM((8, DEVICES * CAP), i32),
            pltpu.VMEM((8, ROWS), i32),
            pltpu.SMEM((3, ROWS), i32),
            pltpu.SMEM((8, DEVICES * CAP), i32),
            pltpu.SMEM((8, DEVICES * CAP), i32),
            pltpu.SMEM((3, 8, DEVICES * CAP), i32),
            pltpu.SMEM((8, ROWS), i32),
            pltpu.VMEM((3, 3, ROOM, TILES, LANES), f32),
            pltpu.VMEM((3, ROOM, TILES, LANES), f32),
            pltpu.VMEM((3, ROOM, TILES, LANES), f32),
            pltpu.VMEM((3, ROOM, TILES, LANES), f32),
            pltpu.VMEM((3, 8, DEVICES * CAP), i32),
            pltpu.VMEM((COLUMN, 3, CAP, TILES, LANES), f32),
            pltpu.VMEM((3, COLUMN, 3 * CAP, TILES, LANES), f32),
            pltpu.VMEM((8, LANES), f32),
            pltpu.VMEM((COLUMN, 8, LANES), f32),
            pltpu.VMEM((3, DEVICES * CAP, TILES, LANES), f32),
            pltpu.VMEM((2, 4, ROWS, FRAG), jnp.bfloat16),
            pltpu.VMEM((4, TILES, ROWS, LANES), f32),
            pltpu.VMEM((4, TILES, ROWS, LANES), f32),
            pltpu.VMEM((4, TILES, ROWS, LANES), f32),
            pltpu.VMEM((2, TILES // 2, ROWS, LANES), f32),
            pltpu.VMEM((2, TILES // 2, ROWS, LANES), f32),
            pltpu.VMEM((TILES, ROWS, LANES), f32),
            pltpu.VMEM((TILES * ROWS, LANES), f32),
            dma((3, TILES)),
            dma((7,)),
            dma((2, 4)),
            dma((3, 3)),
            dma((3, 3)),
            dma((3,)),
            dma((3,)),
            dma,
            dma,
            dma((3,)),
            dma((3,)),
            dma,
            dma,
            dma((4,)),
            dma((4,)),
            dma((2,)),
            dma((2,)),
            dma((2,)),
            dma((2,)),
            dma((2,)),
            dma((2,)),
            pltpu.SemaphoreType.REGULAR,
            pltpu.SemaphoreType.REGULAR,
        ],
        compiler_params=pltpu.CompilerParams(
            collective_id=0, has_side_effects=True, vmem_limit_bytes=48 * 1024 * 1024
        ),
    )(*[pltpu.with_memory_space_constraint(a, pltpu.HBM) for a in arguments])

    def slow():
        return pl.pallas_call(
            kernel,
            out_shape=pltpu.VMEM((3, TILES * ROWS, LANES), f32),
            in_specs=[anywhere] * 6,
            out_specs=on_chip,
            scratch_shapes=[
                pltpu.VMEM((3, TILES * ROWS, LANES), f32),
                pltpu.VMEM((3, ROWS), i32),
                pltpu.VMEM((1, DEVICES), i32),
                pltpu.VMEM((8, DEVICES * CAP), i32),
                pltpu.VMEM((8, ROWS), i32),
                pltpu.SMEM((3, ROWS), i32),
                pltpu.SMEM((8, DEVICES * CAP), i32),
                pltpu.SMEM((8, ROWS), i32),
                pltpu.VMEM((DEVICES, CAP, 3 * TILES, LANES), f32),
                pltpu.VMEM((DEVICES * CAP, 3 * TILES, LANES), f32),
                pltpu.VMEM((2, 4, ROWS, FRAG), jnp.bfloat16),
                pltpu.VMEM((4, TILES, ROWS, LANES), f32),
                pltpu.VMEM((4, TILES, ROWS, LANES), f32),
                pltpu.VMEM((4, TILES, ROWS, LANES), f32),
                pltpu.VMEM((2, TILES // 2, ROWS, LANES), f32),
                pltpu.VMEM((2, TILES // 2, ROWS, LANES), f32),
                pltpu.VMEM((TILES, ROWS, LANES), f32),
                pltpu.VMEM((TILES * ROWS, LANES), f32),
                dma((3, TILES)),
                dma((5,)),
                dma((2, 4)),
                dma,
                dma,
                dma((4,)),
                dma((4,)),
                dma((2,)),
                dma((2,)),
                dma((2,)),
                dma((2,)),
                dma((2,)),
                dma((2,)),
                pltpu.SemaphoreType.REGULAR,
                pltpu.SemaphoreType.REGULAR,
            ],
            compiler_params=pltpu.CompilerParams(
                collective_id=1, has_side_effects=True, vmem_limit_bytes=48 * 1024 * 1024
            ),
        )(*[pltpu.with_memory_space_constraint(a, pltpu.HBM) for a in arguments])

    def write(updated):
        return pl.pallas_call(
            write_out,
            out_shape=(shape, shape, shape),
            in_specs=[anywhere],
            out_specs=(anywhere, anywhere, anywhere),
            scratch_shapes=[dma((3, TILES))],
            compiler_params=pltpu.CompilerParams(vmem_limit_bytes=1024 * 1024),
        )(pltpu.with_memory_space_constraint(updated, pltpu.VMEM))

    return lax.cond(flag[0, 0] > 0.0, lambda: write(slow()), lambda: write(updated))


def solution(mesh):
    return jax.shard_map(
        local,
        mesh=mesh,
        in_specs=(
            P(("ctx", "fsdp"), None),
            P(("ctx", "fsdp"), None),
            P(("ctx", "fsdp"), None),
            P(None, ("ctx", "fsdp")),
            P(None, ("ctx", "fsdp")),
            P("ctx", None, "fsdp", None, None),
        ),
        out_specs=(P(("ctx", "fsdp"), None), P(("ctx", "fsdp"), None), P(("ctx", "fsdp"), None)),
        check_vma=False,
    )
```

```python
import functools

import jax
import jax.numpy as jnp
from jax import lax
from jax.experimental import pallas as pl
from jax.experimental.pallas import tpu as pltpu
from jax.sharding import PartitionSpec as P

MESH = pl.DeviceIdType.MESH

beta_one = 0.9
beta_two = 0.95
learn_rate = 0.0003
decay_weight = 0.1
epsilon = 1e-08
step_count = 1001.0

ROWS = 128
FRAG = 1024
TILES = 8
LANES = 128
N_CTX = 8
N_FSDP = 16
DEVICES = 128
CAP = 2
PARTS = 4
CHUNK = ROWS // PARTS
COLUMN = 32
WIDE = COLUMN * CAP
ROOM = 48


def place():
    ctx, fsdp = lax.axis_index("ctx"), lax.axis_index("fsdp")
    return ctx // 2, ctx % 2, fsdp // 4, fsdp % 4


def partner(dx, dy, dz, dcore):
    x, core, z, y = place()
    return ((x + dx) % 4) * 2 + (core + dcore) % 2, ((z + dz) % 4) * 4 + (y + dy) % 4


def kernel(
    master_hbm, moment_hbm, second_hbm, frag_hbm, counts_hbm, grad_hbm,
    out,
    state, frag_v, counts_v, slot_v, row_v, frag_s, slot_s, row_s,
    send, recv, terms, pair_out, pair_in, sums, hop_in, last_in, acc_in, total,
    state_sem, small_sem, terms_sem,
    packet_send, packet_recv, pair_send, pair_recv, hop_send, hop_recv, last_send, last_recv, acc_send, acc_recv,
    y_sem, z_sem,
):
    ctx, fsdp = lax.axis_index("ctx"), lax.axis_index("fsdp")
    x, core, z, y = place()
    me = ctx * N_FSDP + fsdp
    order = [(x + 2) % 4, (x + 1) % 4, (x + 3) % 4, x]

    def term_load(side, step):
        block = order[step] * 2 + (core + side) % 2
        return pltpu.make_async_copy(grad_hbm.at[0, block, 0], terms.at[side, step], terms_sem.at[side, step])

    def y_peer(k):
        return ctx, z * 4 + (y + k) % 4

    def z_peer(k):
        return ctx, ((z + k) % 4) * 4 + y

    barrier = pltpu.get_barrier_semaphore()
    for k in range(1, N_CTX):
        pl.semaphore_signal(barrier, inc=1, device_id=((ctx + k) % N_CTX, fsdp), device_id_type=MESH)
    for k in range(1, 4):
        pl.semaphore_signal(barrier, inc=1, device_id=y_peer(k), device_id_type=MESH)
    for k in range(1, 4):
        pl.semaphore_signal(barrier, inc=1, device_id=z_peer(k), device_id_type=MESH)

    for step in range(4):
        term_load(1, step).start()
    frag_load = pltpu.make_async_copy(frag_hbm, frag_v, small_sem.at[0])
    frag_load_s = pltpu.make_async_copy(frag_hbm, frag_s, small_sem.at[1])
    counts_load = pltpu.make_async_copy(counts_hbm, counts_v, small_sem.at[2])
    frag_load.start()
    frag_load_s.start()
    counts_load.start()
    for step in range(4):
        term_load(0, step).start()
    state_loads = []
    for a, source in enumerate((master_hbm, moment_hbm, second_hbm)):
        for j in range(TILES):
            state_loads.append(
                pltpu.make_async_copy(
                    source.at[:, pl.ds(j * LANES, LANES)],
                    state.at[a, pl.ds(j * ROWS, ROWS)],
                    state_sem.at[a, j],
                )
            )
    for load in state_loads:
        load.start()

    for step in range(4):
        term_load(1, step).wait()

        def widen(i, carry, step=step):
            rows = pl.ds(pl.multiple_of(i * 16, 16), 16)
            for j in range(TILES):
                pair_out[step, j, rows, :] = terms[1, step, rows, pl.ds(j * LANES, LANES)].astype(jnp.float32)
            return carry

        lax.fori_loop(0, ROWS // 16, widen, 0)

    frag_load.wait()
    counts_load.wait()
    owners, offsets = frag_v[pl.ds(0, 1), :], frag_v[pl.ds(1, 1), :]
    slot_of_row = owners * CAP + offsets
    slot_ids = lax.broadcasted_iota(jnp.int32, (DEVICES * CAP, ROWS), 0)
    hit = jnp.where(slot_ids == slot_of_row, 1.0, 0.0)
    row_ids = lax.broadcasted_iota(jnp.int32, (8, ROWS), 1).astype(jnp.float32)
    row_of_slot = lax.dot_general(row_ids, hit, (((1,), (1,)), ((), ())), preferred_element_type=jnp.float32)
    slot_v[...] = jnp.clip(row_of_slot.astype(jnp.int32), 0, ROWS - 1)
    counts = jnp.broadcast_to(counts_v[...].astype(jnp.float32), (8, DEVICES))
    earlier = jnp.where(
        lax.broadcasted_iota(jnp.int32, (DEVICES, DEVICES), 0) < lax.broadcasted_iota(jnp.int32, (DEVICES, DEVICES), 1),
        1.0, 0.0,
    )
    before = lax.dot_general(counts, earlier, (((1,), (0,)), ((), ())), preferred_element_type=jnp.float32)[0:1, :]
    rows_down = lax.broadcasted_iota(jnp.int32, (ROWS, DEVICES), 0).astype(jnp.float32)
    owner_ids = lax.broadcasted_iota(jnp.int32, (ROWS, DEVICES), 1).astype(jnp.float32)
    offset = rows_down - before
    from_owner = (offset >= 0.0) & (offset < counts[0:1, :])
    slot_here = jnp.where(from_owner, owner_ids * CAP + offset, 0.0)
    slot_of_new = lax.dot_general(
        jnp.ones((8, DEVICES), jnp.float32), slot_here, (((1,), (1,)), ((), ())), preferred_element_type=jnp.float32
    )
    row_v[...] = jnp.clip(slot_of_new.astype(jnp.int32), 0, DEVICES * CAP - 1)
    slot_copy = pltpu.make_async_copy(slot_v, slot_s, small_sem.at[3])
    row_copy = pltpu.make_async_copy(row_v, row_s, small_sem.at[4])
    slot_copy.start()
    row_copy.start()

    def pair_copy(step):
        return pltpu.make_async_remote_copy(
            src_ref=pair_out.at[step], dst_ref=pair_in.at[step], send_sem=pair_send.at[step],
            recv_sem=pair_recv.at[step], device_id=(x * 2 + 1 - core, fsdp), device_id_type=MESH,
        )

    def along_x(way):
        return ((x + (1 if way == 0 else 3)) % 4) * 2 + core, fsdp

    half = (pl.ds(0, TILES // 2), pl.ds(TILES // 2, TILES // 2))

    def hop_copy(way):
        return pltpu.make_async_remote_copy(
            src_ref=sums.at[0, half[way]], dst_ref=hop_in.at[way], send_sem=hop_send.at[way],
            recv_sem=hop_recv.at[way], device_id=along_x(way), device_id_type=MESH,
        )

    def last_copy(way):
        return pltpu.make_async_remote_copy(
            src_ref=sums.at[1 + way, half[1 - way]], dst_ref=last_in.at[way], send_sem=last_send.at[way],
            recv_sem=last_recv.at[way], device_id=along_x(way), device_id_type=MESH,
        )

    def acc_copy(way):
        return pltpu.make_async_remote_copy(
            src_ref=sums.at[1 + way, half[way]], dst_ref=acc_in.at[half[way]],
            send_sem=acc_send.at[way], recv_sem=acc_recv.at[way],
            device_id=along_x(way), device_id_type=MESH,
        )

    def add_pair(step):
        term_load(0, step).wait()
        pair_copy(step).wait_recv()

        def add(i, carry):
            rows = pl.ds(pl.multiple_of(i * 16, 16), 16)
            for j in range(TILES):
                own = terms[0, step, rows, pl.ds(j * LANES, LANES)].astype(jnp.float32)
                sums[step, j, rows, :] = own + pair_in[step, j, rows, :]
            return carry

        lax.fori_loop(0, ROWS // 16, add, 0)

    place_in_row = (
        lax.broadcasted_iota(jnp.int32, (TILES, LANES), 0) * LANES + lax.broadcasted_iota(jnp.int32, (TILES, LANES), 1)
    )

    def pack(device, slot):
        row = slot_s[0, device * CAP + slot]
        live = place_in_row < frag_s[2, row]
        values = [state[a, pl.ds(row, TILES, stride=ROWS), :] for a in range(3)]
        return [jnp.where(live, v, 0.0 if a < 2 else -1.0) for a, v in enumerate(values)]

    def post(dx, dy, dz, dcore):
        target = partner(dx, dy, dz, dcore)
        device, k = target[0] * N_FSDP + target[1], dx + 4 * dy + 16 * dz + 64 * dcore
        for slot in range(CAP):
            for a, v in enumerate(pack(device, slot)):
                send[k, slot, pl.ds(a * TILES, TILES), :] = v
        pltpu.make_async_remote_copy(
            src_ref=send.at[k], dst_ref=recv.at[pl.ds(me * CAP, CAP)],
            send_sem=packet_send, recv_sem=packet_recv, device_id=target, device_id_type=MESH,
        ).start()

    def post_line(i, carry):
        post(i % 4, 0, 0, i // 4)
        return carry

    def post_plane(i, carry):
        dx, k = i % 4, i // 4
        post(dx, 1 + (dx + k) % 3, 0, k // 3)
        return carry

    def post_rest(i, carry):
        dx, k = i % 4, i // 4
        post(dx, (dx + k) % 4, 1 + (dx + k // 4) % 3, k // 12)
        return carry

    for load in state_loads:
        load.wait()
    frag_load_s.wait()
    slot_copy.wait()
    row_copy.wait()
    pl.semaphore_wait(barrier, N_CTX - 1 + 6)
    for step in range(4):
        pair_copy(step).start()
    for k in range(1, 4):
        pl.semaphore_signal(y_sem, inc=1, device_id=y_peer(k), device_id_type=MESH)
    lax.fori_loop(1, N_CTX, post_line, 0)
    pl.semaphore_wait(y_sem, 3)
    for k in range(1, 4):
        pl.semaphore_signal(z_sem, inc=1, device_id=z_peer(k), device_id_type=MESH)
    add_pair(0)
    hop_copy(0).start()
    hop_copy(1).start()
    lax.fori_loop(0, 24, post_plane, 0)
    for way in range(2):
        add_pair(1 + way)
        last_copy(way).start()
    pl.semaphore_wait(z_sem, 3)
    lax.fori_loop(0, 96, post_rest, 0)

    for way in range(2):
        hop_copy(way).wait()

        def add_hop(i, carry, way=way):
            rows = pl.ds(pl.multiple_of(i * 16, 16), 16)
            for j in range(TILES // 2):
                sums[1 + way, way * (TILES // 2) + j, rows, :] += hop_in[way, j, rows, :]
            return carry

        lax.fori_loop(0, ROWS // 16, add_hop, 0)
        last_copy(way).wait_send()
        acc_copy(way).start()

    for slot in range(CAP):
        for a, v in enumerate(pack(me, slot)):
            recv[me * CAP + slot, pl.ds(a * TILES, TILES), :] = v
    add_pair(3)
    for way in range(2):
        last_copy(way).wait_recv()
    for way in range(2):
        acc_copy(way).wait_recv()

    def add_last(i, carry):
        rows = pl.ds(pl.multiple_of(i * 16, 16), 16)
        for j in range(TILES):
            near = last_in[1, j, rows, :] if j < TILES // 2 else last_in[0, j - TILES // 2, rows, :]
            total[pl.ds(pl.multiple_of(j * ROWS + i * 16, 16), 16), :] = (
                sums[3, j, rows, :] + near + acc_in[j, rows, :]
            )
        return carry

    lax.fori_loop(0, ROWS // 16, add_last, 0)

    all_here = recv.at[pl.ds(0, (DEVICES - 1) * CAP)]
    pltpu.make_async_copy(all_here, all_here, packet_recv).wait()

    def update(row, carry):
        slot = row_s[0, row]
        master, moment, second = [recv[slot, pl.ds(a * TILES, TILES), :] for a in range(3)]
        live = second >= 0.0
        second = jnp.where(live, second, 0.0)
        grad = jnp.where(live, total[pl.ds(row, TILES, stride=ROWS), :], 0.0)
        new_moment = beta_one * moment + (1.0 - beta_one) * grad
        new_second = beta_two * second + (1.0 - beta_two) * grad * grad
        moment_hat = new_moment / (1.0 - beta_one**step_count)
        second_hat = new_second / (1.0 - beta_two**step_count)
        new_master = master - learn_rate * (
            moment_hat / (jnp.sqrt(second_hat) + epsilon) + decay_weight * master
        )
        for a, v in enumerate((new_master, new_moment, new_second)):
            out[a, pl.ds(row, TILES, stride=ROWS), :] = v
        return carry

    lax.fori_loop(0, ROWS, update, 0, unroll=8)

    all_sent = send.at[pl.ds(1, DEVICES - 1)]
    pltpu.make_async_copy(all_sent, all_sent, packet_send).wait()
    for step in range(4):
        pair_copy(step).wait_send()
    for way in range(2):
        acc_copy(way).wait_send()


def kernel_fast(
    master_hbm, moment_hbm, second_hbm, frag_hbm, counts_hbm, grad_hbm,
    out, flag_out,
    state, frag_v, counts_v, rank_v, meta_v, row_v, frag_s, rank_s, own_s, meta_s, row_s,
    x_out, x_in_0, x_in_1, x_in_2, meta_in, near_out, far_out, flag_mine, flag_in, recv, recv_one, step_size, terms, pair_out, pair_in, sums, hop_in, last_in, acc_in, total,
    state_sem, small_sem, terms_sem,
    x_send, x_recv, meta_send, meta_recv, near_send, near_recv, one_send, one_recv, far_send, far_recv, flag_send, flag_recv, pair_send, pair_recv, hop_send, hop_recv, last_send, last_recv, acc_send, acc_recv,
    y_sem, z_sem,
):
    ctx, fsdp = lax.axis_index("ctx"), lax.axis_index("fsdp")
    x, core, z, y = place()
    here = core * N_FSDP + fsdp
    x_in = (x_in_0, x_in_1, x_in_2)
    order_of_arrays = (1, 2, 0)

    def arrivals(a):
        return recv_one if a == 0 else recv.at[a - 1]

    order = [(x + 2) % 4, (x + 1) % 4, (x + 3) % 4, x]

    def term_load(side, step):
        block = order[step] * 2 + (core + side) % 2
        return pltpu.make_async_copy(grad_hbm.at[0, block, 0], terms.at[side, step], terms_sem.at[side, step])

    def x_peer(k):
        return ((x + k) % 4) * 2 + core, fsdp

    def y_peer(k):
        return ctx, z * 4 + (y + k) % 4

    def z_peer(k):
        return ctx, ((z + k) % 4) * 4 + y

    barrier = pltpu.get_barrier_semaphore()
    pl.semaphore_signal(barrier, inc=1, device_id=(x * 2 + 1 - core, fsdp), device_id_type=MESH)
    for k in range(1, 4):
        pl.semaphore_signal(barrier, inc=1, device_id=x_peer(k), device_id_type=MESH)
    for k in range(1, 4):
        pl.semaphore_signal(barrier, inc=1, device_id=y_peer(k), device_id_type=MESH)
    for k in range(1, 4):
        pl.semaphore_signal(barrier, inc=1, device_id=z_peer(k), device_id_type=MESH)

    for step in range(4):
        term_load(1, step).start()
    frag_load = pltpu.make_async_copy(frag_hbm, frag_v, small_sem.at[0])
    frag_load_s = pltpu.make_async_copy(frag_hbm, frag_s, small_sem.at[1])
    counts_load = pltpu.make_async_copy(counts_hbm, counts_v, small_sem.at[2])
    frag_load.start()
    frag_load_s.start()
    counts_load.start()
    for step in range(4):
        term_load(0, step).start()
    state_loads = []
    for a, source in enumerate((master_hbm, moment_hbm, second_hbm)):
        for j in range(TILES):
            state_loads.append(
                pltpu.make_async_copy(
                    source.at[:, pl.ds(j * LANES, LANES)],
                    state.at[a, pl.ds(j * ROWS, ROWS)],
                    state_sem.at[a, j],
                )
            )
    for load in state_loads:
        load.start()

    frag_load.wait()
    counts_load.wait()
    owners, offsets = frag_v[pl.ds(0, 1), :], frag_v[pl.ds(1, 1), :]
    column = (owners // COLUMN - x + 4) % 4
    in_column = jnp.where(lax.broadcasted_iota(jnp.int32, (8, ROWS), 0) == column, 1.0, 0.0)
    earlier = jnp.where(
        lax.broadcasted_iota(jnp.int32, (DEVICES, DEVICES), 0) < lax.broadcasted_iota(jnp.int32, (DEVICES, DEVICES), 1),
        1.0, 0.0,
    )
    ranks = lax.dot_general(in_column, earlier, (((1,), (0,)), ((), ())), preferred_element_type=jnp.float32)
    rank = jnp.sum(in_column * ranks, axis=0, keepdims=True)
    over = jnp.max(jnp.where((rank >= ROOM) & (column > 0), 1.0, 0.0), axis=1, keepdims=True)
    place_ids = lax.broadcasted_iota(jnp.int32, (DEVICES * CAP, ROWS), 0)
    by_rank = jnp.where(place_ids == column * WIDE + rank.astype(jnp.int32), 1.0, 0.0)
    by_slot = jnp.where(place_ids == column * WIDE + (owners % COLUMN) * CAP + offsets, 1.0, 0.0)
    row_ids = lax.broadcasted_iota(jnp.int32, (8, ROWS), 1).astype(jnp.float32)
    which = lax.broadcasted_iota(jnp.int32, (8, ROWS), 0)
    row_of_rank = lax.dot_general(row_ids, by_rank, (((1,), (1,)), ((), ())), preferred_element_type=jnp.float32)
    rank_v[...] = jnp.clip(row_of_rank.astype(jnp.int32), 0, ROWS - 1)
    of_slot = lax.dot_general(
        jnp.where(which == 0, row_ids, rank), by_slot, (((1,), (1,)), ((), ())), preferred_element_type=jnp.float32
    )
    line = lax.broadcasted_iota(jnp.int32, (8, DEVICES * CAP), 0)
    top = jnp.where(line == 0, ROWS - 1, ROOM - 1)
    meta = jnp.clip(of_slot.astype(jnp.int32), 0, top)
    meta_v[...] = jnp.where(line == 2, over.astype(jnp.int32), meta)
    counts = jnp.broadcast_to(counts_v[...].astype(jnp.float32), (8, DEVICES))
    before = lax.dot_general(counts, earlier, (((1,), (0,)), ((), ())), preferred_element_type=jnp.float32)[0:1, :]
    rows_down = lax.broadcasted_iota(jnp.int32, (ROWS, DEVICES), 0).astype(jnp.float32)
    owner_ids = lax.broadcasted_iota(jnp.int32, (ROWS, DEVICES), 1)
    first = ((owner_ids % COLUMN) * 8 + ((owner_ids // COLUMN - x + 4) % 4) * CAP).astype(jnp.float32)
    offset = rows_down - before
    from_owner = (offset >= 0.0) & (offset < counts[0:1, :])
    slot_here = jnp.where(from_owner, first + offset, 0.0)
    slot_of_new = lax.dot_general(
        jnp.ones((8, DEVICES), jnp.float32), slot_here, (((1,), (1,)), ((), ())), preferred_element_type=jnp.float32
    )
    row_v[...] = jnp.clip(slot_of_new.astype(jnp.int32), 0, DEVICES * CAP - 1)
    table_copies = [
        pltpu.make_async_copy(source, target, small_sem.at[3 + i])
        for i, (source, target) in enumerate(((rank_v, rank_s), (meta_v, own_s), (row_v, row_s)))
    ]
    for copy in table_copies:
        copy.start()

    def pair_copy(step):
        return pltpu.make_async_remote_copy(
            src_ref=pair_out.at[step], dst_ref=pair_in.at[step], send_sem=pair_send.at[step],
            recv_sem=pair_recv.at[step], device_id=(x * 2 + 1 - core, fsdp), device_id_type=MESH,
        )

    def along_x(way):
        return ((x + (1 if way == 0 else 3)) % 4) * 2 + core, fsdp

    half = (pl.ds(0, TILES // 2), pl.ds(TILES // 2, TILES // 2))

    def hop_copy(way):
        return pltpu.make_async_remote_copy(
            src_ref=sums.at[0, half[way]], dst_ref=hop_in.at[way], send_sem=hop_send.at[way],
            recv_sem=hop_recv.at[way], device_id=along_x(way), device_id_type=MESH,
        )

    def last_copy(way):
        return pltpu.make_async_remote_copy(
            src_ref=sums.at[1 + way, half[1 - way]], dst_ref=last_in.at[way], send_sem=last_send.at[way],
            recv_sem=last_recv.at[way], device_id=along_x(way), device_id_type=MESH,
        )

    def acc_copy(way, part):
        rows = pl.ds(part * CHUNK, CHUNK)
        return pltpu.make_async_remote_copy(
            src_ref=sums.at[1 + way, half[way], rows], dst_ref=acc_in.at[half[way], rows],
            send_sem=acc_send.at[way, part], recv_sem=acc_recv.at[way, part],
            device_id=along_x(way), device_id_type=MESH,
        )

    def add_pair(step):
        term_load(0, step).wait()
        pair_copy(step).wait_recv()

        def add(i, carry):
            rows = pl.ds(pl.multiple_of(i * 16, 16), 16)
            for j in range(TILES):
                own = terms[0, step, rows, pl.ds(j * LANES, LANES)].astype(jnp.float32)
                sums[step, j, rows, :] = own + pair_in[step, j, rows, :]
            return carry

        lax.fori_loop(0, ROWS // 16, add, 0)

    place_in_row = (
        lax.broadcasted_iota(jnp.int32, (TILES, LANES), 0) * LANES + lax.broadcasted_iota(jnp.int32, (TILES, LANES), 1)
    )

    def masked(a, row):
        live = place_in_row < frag_s[2, row]
        return jnp.where(live, state[a, pl.ds(row, TILES, stride=ROWS), :], -1.0 if a == 2 else 0.0)

    def fill_x(a):
        def fill(i, carry):
            for k in range(1, 4):
                x_out[a, k - 1, i] = masked(a, rank_s[0, k * WIDE + i])
            return carry

        lax.fori_loop(0, ROOM, fill, 0, unroll=4)

    def x_copy(a, k):
        return pltpu.make_async_remote_copy(
            src_ref=x_out.at[a, k - 1], dst_ref=x_in[a].at[3 - k], send_sem=x_send.at[a, k - 1],
            recv_sem=x_recv.at[a, 3 - k], device_id=x_peer(k), device_id_type=MESH,
        )

    def meta_copy(k):
        return pltpu.make_async_remote_copy(
            src_ref=meta_v, dst_ref=meta_in.at[3 - k], send_sem=meta_send.at[k - 1],
            recv_sem=meta_recv.at[3 - k], device_id=x_peer(k), device_id_type=MESH,
        )

    def column_peer(i):
        return partner(0, i % 4, (i + i // 4) % 4, i // 16)

    def post_near(dy, dz, dcore):
        target = partner(0, dy, dz, dcore)
        there, i = (target[0] % 2) * N_FSDP + target[1], dy + 4 * dz + 16 * dcore
        for slot in range(CAP):
            row = own_s[0, there * CAP + slot]
            for a in range(3):
                near_out[i, a, slot] = masked(a, row)
        pltpu.make_async_remote_copy(
            src_ref=near_out.at[i, pl.ds(1, 2)], dst_ref=recv.at[:, pl.ds(here * 8, CAP)],
            send_sem=near_send, recv_sem=near_recv, device_id=target, device_id_type=MESH,
        ).start()
        pltpu.make_async_remote_copy(
            src_ref=near_out.at[i, 0], dst_ref=recv_one.at[pl.ds(here * 8, CAP)],
            send_sem=one_send, recv_sem=one_recv, device_id=target, device_id_type=MESH,
        ).start()

    def post_line(i, carry):
        post_near((1 + i // 2) * (i % 2), (1 + i // 2) * ((i + 1) % 2), 0)
        return carry

    def post_plane(i, carry):
        post_near(1 + i % 3, 1 + (i + i // 3) % 3, 0)
        return carry

    def post_core(i, carry):
        post_near(i % 4, (i + i // 4) % 4, 1)
        return carry

    def moved(a, there, origin, slot):
        return x_in[a][origin - 1, meta_s[origin - 1, 1, (4 - origin) * WIDE + there * CAP + slot]]

    def post_far(a):
        def post(i, carry):
            target = column_peer(i)
            there = (target[0] % 2) * N_FSDP + target[1]
            for origin in range(1, 4):
                for slot in range(CAP):
                    far_out[a, i, (origin - 1) * CAP + slot] = moved(a, there, origin, slot)
            pltpu.make_async_remote_copy(
                src_ref=far_out.at[a, i], dst_ref=arrivals(a).at[pl.ds(here * 8 + CAP, 3 * CAP)],
                send_sem=far_send.at[a], recv_sem=far_recv.at[a], device_id=target, device_id_type=MESH,
            ).start()
            return carry

        for k in range(1, 4):
            x_copy(a, k).wait_recv()
        lax.fori_loop(1, COLUMN, post, 0)
        for origin in range(1, 4):
            for slot in range(CAP):
                arrivals(a)[here * 8 + origin * CAP + slot] = moved(a, here, origin, slot)

    def post_flag(i, carry):
        pltpu.make_async_remote_copy(
            src_ref=flag_mine, dst_ref=flag_in.at[here], send_sem=flag_send, recv_sem=flag_recv,
            device_id=column_peer(i), device_id_type=MESH,
        ).start()
        return carry

    for load in state_loads:
        load.wait()
    frag_load_s.wait()
    for copy in table_copies:
        copy.wait()
    fill_x(1)
    pl.semaphore_wait(barrier, 10)
    for k in range(1, 4):
        pl.semaphore_signal(y_sem, inc=1, device_id=y_peer(k), device_id_type=MESH)
    for k in (1, 3, 2):
        x_copy(1, k).start()
    for k in (1, 3, 2):
        meta_copy(k).start()
    fill_x(2)
    for k in (1, 3, 2):
        x_copy(2, k).start()
    pl.semaphore_wait(y_sem, 3)
    for k in range(1, 4):
        pl.semaphore_signal(z_sem, inc=1, device_id=z_peer(k), device_id_type=MESH)
    lax.fori_loop(0, 6, post_line, 0)
    fill_x(0)
    for k in (1, 3, 2):
        x_copy(0, k).start()
    pl.semaphore_wait(z_sem, 3)
    lax.fori_loop(0, 9, post_plane, 0)
    lax.fori_loop(0, 16, post_core, 0)
    for step in range(4):
        term_load(1, step).wait()

        def widen(i, carry, step=step):
            rows = pl.ds(pl.multiple_of(i * 16, 16), 16)
            for j in range(TILES):
                pair_out[step, j, rows, :] = terms[1, step, rows, pl.ds(j * LANES, LANES)].astype(jnp.float32)
            return carry

        lax.fori_loop(0, ROWS // 16, widen, 0)
        pair_copy(step).start()
    for slot in range(CAP):
        row = own_s[0, here * CAP + slot]
        for a in range(3):
            arrivals(a)[here * 8 + slot] = masked(a, row)
    add_pair(0)
    hop_copy(0).start()
    hop_copy(1).start()
    for way in range(2):
        add_pair(1 + way)
        last_copy(way).start()
    add_pair(3)
    for k in range(1, 4):
        meta_copy(k).wait_recv()
    flag = meta_v[pl.ds(2, 1), pl.ds(0, LANES)]
    for origin in range(3):
        flag = jnp.maximum(flag, meta_in[origin, pl.ds(2, 1), pl.ds(0, LANES)])
    flag = jnp.broadcast_to(flag.astype(jnp.float32), (8, LANES))
    flag_mine[...] = flag
    flag_in[here] = flag
    meta_load = pltpu.make_async_copy(meta_in, meta_s, small_sem.at[6])
    meta_load.start()
    lax.fori_loop(1, COLUMN, post_flag, 0)
    meta_load.wait()
    for a in order_of_arrays:
        post_far(a)
    for way in range(2):
        hop_copy(way).wait()

        def add_hop(i, carry, way=way):
            rows = pl.ds(pl.multiple_of(i * 16, 16), 16)
            for j in range(TILES // 2):
                sums[1 + way, way * (TILES // 2) + j, rows, :] += hop_in[way, j, rows, :]
            return carry

        lax.fori_loop(0, ROWS // 16, add_hop, 0)
    for part in range(PARTS):
        for way in range(2):
            acc_copy(way, part).start()
    for way in range(2):
        last_copy(way).wait()

    def add_last(i, carry):
        rows = pl.ds(pl.multiple_of(i * 16, 16), 16)
        for j in range(TILES):
            near = last_in[1, j, rows, :] if j < TILES // 2 else last_in[0, j - TILES // 2, rows, :]
            total[pl.ds(pl.multiple_of(j * ROWS + i * 16, 16), 16), :] = sums[3, j, rows, :] + near
        return carry

    lax.fori_loop(0, ROWS // 16, add_last, 0)

    others = COLUMN - 1
    near_here = recv.at[:, pl.ds(0, others * CAP)]
    pltpu.make_async_copy(near_here, near_here, near_recv).wait()
    for a in (1, 2):
        far_here = recv.at[a - 1, pl.ds(0, others * 3 * CAP)]
        pltpu.make_async_copy(far_here, far_here, far_recv.at[a]).wait()
    def update_moments(row, carry):
        slot = row_s[0, row]
        moment, second = recv[0, slot], recv[1, slot]
        live = second >= 0.0
        second = jnp.where(live, second, 0.0)
        grad = jnp.where(live, total[pl.ds(row, TILES, stride=ROWS), :], 0.0)
        new_moment = beta_one * moment + (1.0 - beta_one) * grad
        new_second = beta_two * second + (1.0 - beta_two) * grad * grad
        moment_hat = new_moment / (1.0 - beta_one**step_count)
        second_hat = new_second / (1.0 - beta_two**step_count)
        step_size[row] = moment_hat / (jnp.sqrt(second_hat) + epsilon)
        out[1, pl.ds(row, TILES, stride=ROWS), :] = new_moment
        out[2, pl.ds(row, TILES, stride=ROWS), :] = new_second
        return carry

    def update_master(row, carry):
        master = recv_one[row_s[0, row]]
        out[0, pl.ds(row, TILES, stride=ROWS), :] = master - learn_rate * (step_size[row] + decay_weight * master)
        return carry

    for part in range(PARTS):
        for way in range(2):
            acc_copy(way, part).wait_recv()
        for j in range(TILES):
            total[pl.ds(j * ROWS + part * CHUNK, CHUNK), :] += acc_in[j, pl.ds(part * CHUNK, CHUNK), :]
        lax.fori_loop(part * CHUNK, (part + 1) * CHUNK, update_moments, 0, unroll=8)
    flags_here = flag_in.at[pl.ds(0, others)]
    pltpu.make_async_copy(flags_here, flags_here, flag_recv).wait()
    flag_out[0] = jnp.max(flag_in[...]).astype(jnp.int32)
    one_here = recv_one.at[pl.ds(0, others * CAP)]
    pltpu.make_async_copy(one_here, one_here, one_recv).wait()
    far_here = recv_one.at[pl.ds(0, others * 3 * CAP)]
    pltpu.make_async_copy(far_here, far_here, far_recv.at[0]).wait()
    lax.fori_loop(0, ROWS, update_master, 0, unroll=8)

    near_sent = near_out.at[pl.ds(1, others), pl.ds(1, 2)]
    pltpu.make_async_copy(near_sent, near_sent, near_send).wait()
    one_sent = near_out.at[pl.ds(1, others), 0]
    pltpu.make_async_copy(one_sent, one_sent, one_send).wait()
    for a in range(3):
        far_sent = far_out.at[a, pl.ds(1, others)]
        pltpu.make_async_copy(far_sent, far_sent, far_send.at[a]).wait()
    flags_sent = flag_in.at[pl.ds(0, others)]
    pltpu.make_async_copy(flags_sent, flags_sent, flag_send).wait()
    for k in range(1, 4):
        meta_copy(k).wait_send()
        for a in range(3):
            x_copy(a, k).wait_send()
    for step in range(4):
        pair_copy(step).wait_send()
    for way in range(2):
        for part in range(PARTS):
            acc_copy(way, part).wait_send()


def write_out(updated, master_hbm, moment_hbm, second_hbm, sem):
    stores = []
    for a, target in enumerate((master_hbm, moment_hbm, second_hbm)):
        for j in range(TILES):
            stores.append(
                pltpu.make_async_copy(
                    updated.at[a, pl.ds(j * ROWS, ROWS)], target.at[:, pl.ds(j * LANES, LANES)], sem.at[a, j]
                )
            )
    for store in stores:
        store.start()
    for store in stores:
        store.wait()


def local(old_master, old_moment, old_second, frag_list, pair_counts, grad_partial):
    anywhere = pl.BlockSpec(memory_space=pl.ANY)
    on_chip = pl.BlockSpec(memory_space=pltpu.VMEM)
    shape = jax.ShapeDtypeStruct((ROWS, FRAG), jnp.float32)
    f32, i32 = jnp.float32, jnp.int32
    dma = pltpu.SemaphoreType.DMA
    arguments = (old_master, old_moment, old_second, frag_list, pair_counts.reshape(1, DEVICES), grad_partial)
    updated, flag = pl.pallas_call(
        kernel_fast,
        out_shape=(pltpu.VMEM((3, TILES * ROWS, LANES), f32), jax.ShapeDtypeStruct((1,), i32)),
        in_specs=[anywhere] * 6,
        out_specs=(on_chip, pl.BlockSpec(memory_space=pltpu.SMEM)),
        scratch_shapes=[
            pltpu.VMEM((3, TILES * ROWS, LANES), f32),
            pltpu.VMEM((3, ROWS), i32),
            pltpu.VMEM((1, DEVICES), i32),
            pltpu.VMEM((8, DEVICES * CAP), i32),
            pltpu.VMEM((8, DEVICES * CAP), i32),
            pltpu.VMEM((8, ROWS), i32),
            pltpu.SMEM((3, ROWS), i32),
            pltpu.SMEM((8, DEVICES * CAP), i32),
            pltpu.SMEM((8, DEVICES * CAP), i32),
            pltpu.SMEM((3, 8, DEVICES * CAP), i32),
            pltpu.SMEM((8, ROWS), i32),
            pltpu.VMEM((3, 3, ROOM, TILES, LANES), f32),
            pltpu.VMEM((3, ROOM, TILES, LANES), f32),
            pltpu.VMEM((3, ROOM, TILES, LANES), f32),
            pltpu.VMEM((3, ROOM, TILES, LANES), f32),
            pltpu.VMEM((3, 8, DEVICES * CAP), i32),
            pltpu.VMEM((COLUMN, 3, CAP, TILES, LANES), f32),
            pltpu.VMEM((3, COLUMN, 3 * CAP, TILES, LANES), f32),
            pltpu.VMEM((8, LANES), f32),
            pltpu.VMEM((COLUMN, 8, LANES), f32),
            pltpu.VMEM((2, DEVICES * CAP, TILES, LANES), f32),
            pltpu.VMEM((DEVICES * CAP, TILES, LANES), f32),
            pltpu.VMEM((ROWS, TILES, LANES), f32),
            pltpu.VMEM((2, 4, ROWS, FRAG), jnp.bfloat16),
            pltpu.VMEM((4, TILES, ROWS, LANES), f32),
            pltpu.VMEM((4, TILES, ROWS, LANES), f32),
            pltpu.VMEM((4, TILES, ROWS, LANES), f32),
            pltpu.VMEM((2, TILES // 2, ROWS, LANES), f32),
            pltpu.VMEM((2, TILES // 2, ROWS, LANES), f32),
            pltpu.VMEM((TILES, ROWS, LANES), f32),
            pltpu.VMEM((TILES * ROWS, LANES), f32),
            dma((3, TILES)),
            dma((7,)),
            dma((2, 4)),
            dma((3, 3)),
            dma((3, 3)),
            dma((3,)),
            dma((3,)),
            dma,
            dma,
            dma,
            dma,
            dma((3,)),
            dma((3,)),
            dma,
            dma,
            dma((4,)),
            dma((4,)),
            dma((2,)),
            dma((2,)),
            dma((2,)),
            dma((2,)),
            dma((2, PARTS)),
            dma((2, PARTS)),
            pltpu.SemaphoreType.REGULAR,
            pltpu.SemaphoreType.REGULAR,
        ],
        compiler_params=pltpu.CompilerParams(
            collective_id=0, has_side_effects=True, vmem_limit_bytes=48 * 1024 * 1024
        ),
    )(*[pltpu.with_memory_space_constraint(a, pltpu.HBM) for a in arguments])

    def slow():
        return pl.pallas_call(
            kernel,
            out_shape=pltpu.VMEM((3, TILES * ROWS, LANES), f32),
            in_specs=[anywhere] * 6,
            out_specs=on_chip,
            scratch_shapes=[
                pltpu.VMEM((3, TILES * ROWS, LANES), f32),
                pltpu.VMEM((3, ROWS), i32),
                pltpu.VMEM((1, DEVICES), i32),
                pltpu.VMEM((8, DEVICES * CAP), i32),
                pltpu.VMEM((8, ROWS), i32),
                pltpu.SMEM((3, ROWS), i32),
                pltpu.SMEM((8, DEVICES * CAP), i32),
                pltpu.SMEM((8, ROWS), i32),
                pltpu.VMEM((DEVICES, CAP, 3 * TILES, LANES), f32),
                pltpu.VMEM((DEVICES * CAP, 3 * TILES, LANES), f32),
                pltpu.VMEM((2, 4, ROWS, FRAG), jnp.bfloat16),
                pltpu.VMEM((4, TILES, ROWS, LANES), f32),
                pltpu.VMEM((4, TILES, ROWS, LANES), f32),
                pltpu.VMEM((4, TILES, ROWS, LANES), f32),
                pltpu.VMEM((2, TILES // 2, ROWS, LANES), f32),
                pltpu.VMEM((2, TILES // 2, ROWS, LANES), f32),
                pltpu.VMEM((TILES, ROWS, LANES), f32),
                pltpu.VMEM((TILES * ROWS, LANES), f32),
                dma((3, TILES)),
                dma((5,)),
                dma((2, 4)),
                dma,
                dma,
                dma((4,)),
                dma((4,)),
                dma((2,)),
                dma((2,)),
                dma((2,)),
                dma((2,)),
                dma((2,)),
                dma((2,)),
                pltpu.SemaphoreType.REGULAR,
                pltpu.SemaphoreType.REGULAR,
            ],
            compiler_params=pltpu.CompilerParams(
                collective_id=1, has_side_effects=True, vmem_limit_bytes=48 * 1024 * 1024
            ),
        )(*[pltpu.with_memory_space_constraint(a, pltpu.HBM) for a in arguments])

    def write(updated):
        return pl.pallas_call(
            write_out,
            out_shape=(shape, shape, shape),
            in_specs=[anywhere],
            out_specs=(anywhere, anywhere, anywhere),
            scratch_shapes=[dma((3, TILES))],
            compiler_params=pltpu.CompilerParams(vmem_limit_bytes=1024 * 1024),
        )(pltpu.with_memory_space_constraint(updated, pltpu.VMEM))

    return lax.cond(flag[0] > 0, lambda: write(slow()), lambda: write(updated))


def solution(mesh):
    return jax.shard_map(
        local,
        mesh=mesh,
        in_specs=(
            P(("ctx", "fsdp"), None),
            P(("ctx", "fsdp"), None),
            P(("ctx", "fsdp"), None),
            P(None, ("ctx", "fsdp")),
            P(None, ("ctx", "fsdp")),
            P("ctx", None, "fsdp", None, None),
        ),
        out_specs=(P(("ctx", "fsdp"), None), P(("ctx", "fsdp"), None), P(("ctx", "fsdp"), None)),
        check_vma=False,
    )
```

```python
import functools

import jax
import jax.numpy as jnp
from jax import lax
from jax.experimental import pallas as pl
from jax.experimental.pallas import tpu as pltpu
from jax.sharding import PartitionSpec as P

MESH = pl.DeviceIdType.MESH

beta_one = 0.9
beta_two = 0.95
learn_rate = 0.0003
decay_weight = 0.1
epsilon = 1e-08
step_count = 1001.0

ROWS = 128
FRAG = 1024
TILES = 8
LANES = 128
N_CTX = 8
N_FSDP = 16
DEVICES = 128
CAP = 2
PARTS = 4
CHUNK = ROWS // PARTS
COLUMN = 32
WIDE = COLUMN * CAP
ROOM = 48


def place():
    ctx, fsdp = lax.axis_index("ctx"), lax.axis_index("fsdp")
    return ctx // 2, ctx % 2, fsdp // 4, fsdp % 4


def partner(dx, dy, dz, dcore):
    x, core, z, y = place()
    return ((x + dx) % 4) * 2 + (core + dcore) % 2, ((z + dz) % 4) * 4 + (y + dy) % 4


def kernel(
    master_hbm, moment_hbm, second_hbm, frag_hbm, counts_hbm, grad_hbm,
    out,
    state, frag_v, counts_v, slot_v, row_v, frag_s, slot_s, row_s,
    send, recv, terms, pair_out, pair_in, sums, hop_in, last_in, acc_in, total,
    state_sem, small_sem, terms_sem,
    packet_send, packet_recv, pair_send, pair_recv, hop_send, hop_recv, last_send, last_recv, acc_send, acc_recv,
    y_sem, z_sem,
):
    ctx, fsdp = lax.axis_index("ctx"), lax.axis_index("fsdp")
    x, core, z, y = place()
    me = ctx * N_FSDP + fsdp
    order = [(x + 2) % 4, (x + 1) % 4, (x + 3) % 4, x]

    def term_load(side, step):
        block = order[step] * 2 + (core + side) % 2
        return pltpu.make_async_copy(grad_hbm.at[0, block, 0], terms.at[side, step], terms_sem.at[side, step])

    def y_peer(k):
        return ctx, z * 4 + (y + k) % 4

    def z_peer(k):
        return ctx, ((z + k) % 4) * 4 + y

    barrier = pltpu.get_barrier_semaphore()
    for k in range(1, N_CTX):
        pl.semaphore_signal(barrier, inc=1, device_id=((ctx + k) % N_CTX, fsdp), device_id_type=MESH)
    for k in range(1, 4):
        pl.semaphore_signal(barrier, inc=1, device_id=y_peer(k), device_id_type=MESH)
    for k in range(1, 4):
        pl.semaphore_signal(barrier, inc=1, device_id=z_peer(k), device_id_type=MESH)

    for step in range(4):
        term_load(1, step).start()
    frag_load = pltpu.make_async_copy(frag_hbm, frag_v, small_sem.at[0])
    frag_load_s = pltpu.make_async_copy(frag_hbm, frag_s, small_sem.at[1])
    counts_load = pltpu.make_async_copy(counts_hbm, counts_v, small_sem.at[2])
    frag_load.start()
    frag_load_s.start()
    counts_load.start()
    for step in range(4):
        term_load(0, step).start()
    state_loads = []
    for a, source in enumerate((master_hbm, moment_hbm, second_hbm)):
        for j in range(TILES):
            state_loads.append(
                pltpu.make_async_copy(
                    source.at[:, pl.ds(j * LANES, LANES)],
                    state.at[a, pl.ds(j * ROWS, ROWS)],
                    state_sem.at[a, j],
                )
            )
    for load in state_loads:
        load.start()

    for step in range(4):
        term_load(1, step).wait()

        def widen(i, carry, step=step):
            rows = pl.ds(pl.multiple_of(i * 16, 16), 16)
            for j in range(TILES):
                pair_out[step, j, rows, :] = terms[1, step, rows, pl.ds(j * LANES, LANES)].astype(jnp.float32)
            return carry

        lax.fori_loop(0, ROWS // 16, widen, 0)

    frag_load.wait()
    counts_load.wait()
    owners, offsets = frag_v[pl.ds(0, 1), :], frag_v[pl.ds(1, 1), :]
    slot_of_row = owners * CAP + offsets
    slot_ids = lax.broadcasted_iota(jnp.int32, (DEVICES * CAP, ROWS), 0)
    hit = jnp.where(slot_ids == slot_of_row, 1.0, 0.0)
    row_ids = lax.broadcasted_iota(jnp.int32, (8, ROWS), 1).astype(jnp.float32)
    row_of_slot = lax.dot_general(row_ids, hit, (((1,), (1,)), ((), ())), preferred_element_type=jnp.float32)
    slot_v[...] = jnp.clip(row_of_slot.astype(jnp.int32), 0, ROWS - 1)
    counts = jnp.broadcast_to(counts_v[...].astype(jnp.float32), (8, DEVICES))
    earlier = jnp.where(
        lax.broadcasted_iota(jnp.int32, (DEVICES, DEVICES), 0) < lax.broadcasted_iota(jnp.int32, (DEVICES, DEVICES), 1),
        1.0, 0.0,
    )
    before = lax.dot_general(counts, earlier, (((1,), (0,)), ((), ())), preferred_element_type=jnp.float32)[0:1, :]
    rows_down = lax.broadcasted_iota(jnp.int32, (ROWS, DEVICES), 0).astype(jnp.float32)
    owner_ids = lax.broadcasted_iota(jnp.int32, (ROWS, DEVICES), 1).astype(jnp.float32)
    offset = rows_down - before
    from_owner = (offset >= 0.0) & (offset < counts[0:1, :])
    slot_here = jnp.where(from_owner, owner_ids * CAP + offset, 0.0)
    slot_of_new = lax.dot_general(
        jnp.ones((8, DEVICES), jnp.float32), slot_here, (((1,), (1,)), ((), ())), preferred_element_type=jnp.float32
    )
    row_v[...] = jnp.clip(slot_of_new.astype(jnp.int32), 0, DEVICES * CAP - 1)
    slot_copy = pltpu.make_async_copy(slot_v, slot_s, small_sem.at[3])
    row_copy = pltpu.make_async_copy(row_v, row_s, small_sem.at[4])
    slot_copy.start()
    row_copy.start()

    def pair_copy(step):
        return pltpu.make_async_remote_copy(
            src_ref=pair_out.at[step], dst_ref=pair_in.at[step], send_sem=pair_send.at[step],
            recv_sem=pair_recv.at[step], device_id=(x * 2 + 1 - core, fsdp), device_id_type=MESH,
        )

    def along_x(way):
        return ((x + (1 if way == 0 else 3)) % 4) * 2 + core, fsdp

    half = (pl.ds(0, TILES // 2), pl.ds(TILES // 2, TILES // 2))

    def hop_copy(way):
        return pltpu.make_async_remote_copy(
            src_ref=sums.at[0, half[way]], dst_ref=hop_in.at[way], send_sem=hop_send.at[way],
            recv_sem=hop_recv.at[way], device_id=along_x(way), device_id_type=MESH,
        )

    def last_copy(way):
        return pltpu.make_async_remote_copy(
            src_ref=sums.at[1 + way, half[1 - way]], dst_ref=last_in.at[way], send_sem=last_send.at[way],
            recv_sem=last_recv.at[way], device_id=along_x(way), device_id_type=MESH,
        )

    def acc_copy(way):
        return pltpu.make_async_remote_copy(
            src_ref=sums.at[1 + way, half[way]], dst_ref=acc_in.at[half[way]],
            send_sem=acc_send.at[way], recv_sem=acc_recv.at[way],
            device_id=along_x(way), device_id_type=MESH,
        )

    def add_pair(step):
        term_load(0, step).wait()
        pair_copy(step).wait_recv()

        def add(i, carry):
            rows = pl.ds(pl.multiple_of(i * 16, 16), 16)
            for j in range(TILES):
                own = terms[0, step, rows, pl.ds(j * LANES, LANES)].astype(jnp.float32)
                sums[step, j, rows, :] = own + pair_in[step, j, rows, :]
            return carry

        lax.fori_loop(0, ROWS // 16, add, 0)

    place_in_row = (
        lax.broadcasted_iota(jnp.int32, (TILES, LANES), 0) * LANES + lax.broadcasted_iota(jnp.int32, (TILES, LANES), 1)
    )

    def pack(device, slot):
        row = slot_s[0, device * CAP + slot]
        live = place_in_row < frag_s[2, row]
        values = [state[a, pl.ds(row, TILES, stride=ROWS), :] for a in range(3)]
        return [jnp.where(live, v, 0.0 if a < 2 else -1.0) for a, v in enumerate(values)]

    def post(dx, dy, dz, dcore):
        target = partner(dx, dy, dz, dcore)
        device, k = target[0] * N_FSDP + target[1], dx + 4 * dy + 16 * dz + 64 * dcore
        for slot in range(CAP):
            for a, v in enumerate(pack(device, slot)):
                send[k, slot, pl.ds(a * TILES, TILES), :] = v
        pltpu.make_async_remote_copy(
            src_ref=send.at[k], dst_ref=recv.at[pl.ds(me * CAP, CAP)],
            send_sem=packet_send, recv_sem=packet_recv, device_id=target, device_id_type=MESH,
        ).start()

    def post_line(i, carry):
        post(i % 4, 0, 0, i // 4)
        return carry

    def post_plane(i, carry):
        dx, k = i % 4, i // 4
        post(dx, 1 + (dx + k) % 3, 0, k // 3)
        return carry

    def post_rest(i, carry):
        dx, k = i % 4, i // 4
        post(dx, (dx + k) % 4, 1 + (dx + k // 4) % 3, k // 12)
        return carry

    for load in state_loads:
        load.wait()
    frag_load_s.wait()
    slot_copy.wait()
    row_copy.wait()
    pl.semaphore_wait(barrier, N_CTX - 1 + 6)
    for step in range(4):
        pair_copy(step).start()
    for k in range(1, 4):
        pl.semaphore_signal(y_sem, inc=1, device_id=y_peer(k), device_id_type=MESH)
    lax.fori_loop(1, N_CTX, post_line, 0)
    pl.semaphore_wait(y_sem, 3)
    for k in range(1, 4):
        pl.semaphore_signal(z_sem, inc=1, device_id=z_peer(k), device_id_type=MESH)
    add_pair(0)
    hop_copy(0).start()
    hop_copy(1).start()
    lax.fori_loop(0, 24, post_plane, 0)
    for way in range(2):
        add_pair(1 + way)
        last_copy(way).start()
    pl.semaphore_wait(z_sem, 3)
    lax.fori_loop(0, 96, post_rest, 0)

    for way in range(2):
        hop_copy(way).wait()

        def add_hop(i, carry, way=way):
            rows = pl.ds(pl.multiple_of(i * 16, 16), 16)
            for j in range(TILES // 2):
                sums[1 + way, way * (TILES // 2) + j, rows, :] += hop_in[way, j, rows, :]
            return carry

        lax.fori_loop(0, ROWS // 16, add_hop, 0)
        last_copy(way).wait_send()
        acc_copy(way).start()

    for slot in range(CAP):
        for a, v in enumerate(pack(me, slot)):
            recv[me * CAP + slot, pl.ds(a * TILES, TILES), :] = v
    add_pair(3)
    for way in range(2):
        last_copy(way).wait_recv()
    for way in range(2):
        acc_copy(way).wait_recv()

    def add_last(i, carry):
        rows = pl.ds(pl.multiple_of(i * 16, 16), 16)
        for j in range(TILES):
            near = last_in[1, j, rows, :] if j < TILES // 2 else last_in[0, j - TILES // 2, rows, :]
            total[pl.ds(pl.multiple_of(j * ROWS + i * 16, 16), 16), :] = (
                sums[3, j, rows, :] + near + acc_in[j, rows, :]
            )
        return carry

    lax.fori_loop(0, ROWS // 16, add_last, 0)

    all_here = recv.at[pl.ds(0, (DEVICES - 1) * CAP)]
    pltpu.make_async_copy(all_here, all_here, packet_recv).wait()

    def update(row, carry):
        slot = row_s[0, row]
        master, moment, second = [recv[slot, pl.ds(a * TILES, TILES), :] for a in range(3)]
        live = second >= 0.0
        second = jnp.where(live, second, 0.0)
        grad = jnp.where(live, total[pl.ds(row, TILES, stride=ROWS), :], 0.0)
        new_moment = beta_one * moment + (1.0 - beta_one) * grad
        new_second = beta_two * second + (1.0 - beta_two) * grad * grad
        moment_hat = new_moment / (1.0 - beta_one**step_count)
        second_hat = new_second / (1.0 - beta_two**step_count)
        new_master = master - learn_rate * (
            moment_hat / (jnp.sqrt(second_hat) + epsilon) + decay_weight * master
        )
        for a, v in enumerate((new_master, new_moment, new_second)):
            out[a, pl.ds(row, TILES, stride=ROWS), :] = v
        return carry

    lax.fori_loop(0, ROWS, update, 0, unroll=8)

    all_sent = send.at[pl.ds(1, DEVICES - 1)]
    pltpu.make_async_copy(all_sent, all_sent, packet_send).wait()
    for step in range(4):
        pair_copy(step).wait_send()
    for way in range(2):
        acc_copy(way).wait_send()


def kernel_fast(
    master_hbm, moment_hbm, second_hbm, frag_hbm, counts_hbm, grad_hbm,
    out, flag_out,
    state, frag_v, counts_v, rank_v, meta_v, row_v, frag_s, rank_s, own_s, meta_s, row_s,
    x_out, x_in_0, x_in_1, x_in_2, meta_in, near_out, far_out, flag_mine, flag_in, recv, recv_one, step_size, terms, pair_out, pair_in, sums, hop_in, last_in, acc_in, total,
    state_sem, small_sem, terms_sem,
    x_send, x_recv, meta_send, meta_recv, near_send, near_recv, one_send, one_recv, far_send, far_recv, flag_send, flag_recv, pair_send, pair_recv, hop_send, hop_recv, last_send, last_recv, acc_send, acc_recv,
    y_sem, z_sem,
):
    ctx, fsdp = lax.axis_index("ctx"), lax.axis_index("fsdp")
    x, core, z, y = place()
    here = core * N_FSDP + fsdp
    x_in = (x_in_0, x_in_1, x_in_2)
    order_of_arrays = (1, 2, 0)

    def arrivals(a):
        return recv_one if a == 0 else recv.at[a - 1]

    order = [(x + 2) % 4, (x + 1) % 4, (x + 3) % 4, x]

    def term_load(side, step):
        block = order[step] * 2 + (core + side) % 2
        return pltpu.make_async_copy(grad_hbm.at[0, block, 0], terms.at[side, step], terms_sem.at[side, step])

    def x_peer(k):
        return ((x + k) % 4) * 2 + core, fsdp

    def y_peer(k):
        return ctx, z * 4 + (y + k) % 4

    def z_peer(k):
        return ctx, ((z + k) % 4) * 4 + y

    barrier = pltpu.get_barrier_semaphore()
    pl.semaphore_signal(barrier, inc=1, device_id=(x * 2 + 1 - core, fsdp), device_id_type=MESH)
    for k in range(1, 4):
        pl.semaphore_signal(barrier, inc=1, device_id=x_peer(k), device_id_type=MESH)
    for k in range(1, 4):
        pl.semaphore_signal(barrier, inc=1, device_id=y_peer(k), device_id_type=MESH)
    for k in range(1, 4):
        pl.semaphore_signal(barrier, inc=1, device_id=z_peer(k), device_id_type=MESH)

    for step in range(4):
        term_load(1, step).start()
    frag_load = pltpu.make_async_copy(frag_hbm, frag_v, small_sem.at[0])
    frag_load_s = pltpu.make_async_copy(frag_hbm, frag_s, small_sem.at[1])
    counts_load = pltpu.make_async_copy(counts_hbm, counts_v, small_sem.at[2])
    frag_load.start()
    frag_load_s.start()
    counts_load.start()
    for step in range(4):
        term_load(0, step).start()
    state_loads = []
    for a, source in enumerate((master_hbm, moment_hbm, second_hbm)):
        for j in range(TILES):
            state_loads.append(
                pltpu.make_async_copy(
                    source.at[:, pl.ds(j * LANES, LANES)],
                    state.at[a, pl.ds(j * ROWS, ROWS)],
                    state_sem.at[a, j],
                )
            )
    for load in state_loads:
        load.start()

    frag_load.wait()
    counts_load.wait()
    owners, offsets = frag_v[pl.ds(0, 1), :], frag_v[pl.ds(1, 1), :]
    column = (owners // COLUMN - x + 4) % 4
    in_column = jnp.where(lax.broadcasted_iota(jnp.int32, (8, ROWS), 0) == column, 1.0, 0.0)
    earlier = jnp.where(
        lax.broadcasted_iota(jnp.int32, (DEVICES, DEVICES), 0) < lax.broadcasted_iota(jnp.int32, (DEVICES, DEVICES), 1),
        1.0, 0.0,
    )
    ranks = lax.dot_general(in_column, earlier, (((1,), (0,)), ((), ())), preferred_element_type=jnp.float32)
    rank = jnp.sum(in_column * ranks, axis=0, keepdims=True)
    over = jnp.max(jnp.where((rank >= ROOM) & (column > 0), 1.0, 0.0), axis=1, keepdims=True)
    place_ids = lax.broadcasted_iota(jnp.int32, (DEVICES * CAP, ROWS), 0)
    by_rank = jnp.where(place_ids == column * WIDE + rank.astype(jnp.int32), 1.0, 0.0)
    by_slot = jnp.where(place_ids == column * WIDE + (owners % COLUMN) * CAP + offsets, 1.0, 0.0)
    row_ids = lax.broadcasted_iota(jnp.int32, (8, ROWS), 1).astype(jnp.float32)
    which = lax.broadcasted_iota(jnp.int32, (8, ROWS), 0)
    row_of_rank = lax.dot_general(row_ids, by_rank, (((1,), (1,)), ((), ())), preferred_element_type=jnp.float32)
    rank_v[...] = jnp.clip(row_of_rank.astype(jnp.int32), 0, ROWS - 1)
    of_slot = lax.dot_general(
        jnp.where(which == 0, row_ids, rank), by_slot, (((1,), (1,)), ((), ())), preferred_element_type=jnp.float32
    )
    line = lax.broadcasted_iota(jnp.int32, (8, DEVICES * CAP), 0)
    top = jnp.where(line == 0, ROWS - 1, ROOM - 1)
    meta = jnp.clip(of_slot.astype(jnp.int32), 0, top)
    meta_v[...] = jnp.where(line == 2, over.astype(jnp.int32), meta)
    counts = jnp.broadcast_to(counts_v[...].astype(jnp.float32), (8, DEVICES))
    before = lax.dot_general(counts, earlier, (((1,), (0,)), ((), ())), preferred_element_type=jnp.float32)[0:1, :]
    rows_down = lax.broadcasted_iota(jnp.int32, (ROWS, DEVICES), 0).astype(jnp.float32)
    owner_ids = lax.broadcasted_iota(jnp.int32, (ROWS, DEVICES), 1)
    first = ((owner_ids % COLUMN) * 8 + ((owner_ids // COLUMN - x + 4) % 4) * CAP).astype(jnp.float32)
    offset = rows_down - before
    from_owner = (offset >= 0.0) & (offset < counts[0:1, :])
    slot_here = jnp.where(from_owner, first + offset, 0.0)
    slot_of_new = lax.dot_general(
        jnp.ones((8, DEVICES), jnp.float32), slot_here, (((1,), (1,)), ((), ())), preferred_element_type=jnp.float32
    )
    row_v[...] = jnp.clip(slot_of_new.astype(jnp.int32), 0, DEVICES * CAP - 1)
    table_copies = [
        pltpu.make_async_copy(source, target, small_sem.at[3 + i])
        for i, (source, target) in enumerate(((rank_v, rank_s), (meta_v, own_s), (row_v, row_s)))
    ]
    for copy in table_copies:
        copy.start()

    def pair_copy(step):
        return pltpu.make_async_remote_copy(
            src_ref=pair_out.at[step], dst_ref=pair_in.at[step], send_sem=pair_send.at[step],
            recv_sem=pair_recv.at[step], device_id=(x * 2 + 1 - core, fsdp), device_id_type=MESH,
        )

    def along_x(way):
        return ((x + (1 if way == 0 else 3)) % 4) * 2 + core, fsdp

    half = (pl.ds(0, TILES // 2), pl.ds(TILES // 2, TILES // 2))

    def hop_copy(way):
        return pltpu.make_async_remote_copy(
            src_ref=sums.at[0, half[way]], dst_ref=hop_in.at[way], send_sem=hop_send.at[way],
            recv_sem=hop_recv.at[way], device_id=along_x(way), device_id_type=MESH,
        )

    def last_copy(way):
        return pltpu.make_async_remote_copy(
            src_ref=sums.at[1 + way, half[1 - way]], dst_ref=last_in.at[way], send_sem=last_send.at[way],
            recv_sem=last_recv.at[way], device_id=along_x(way), device_id_type=MESH,
        )

    def acc_copy(way, part):
        rows = pl.ds(part * CHUNK, CHUNK)
        return pltpu.make_async_remote_copy(
            src_ref=sums.at[1 + way, half[way], rows], dst_ref=acc_in.at[half[way], rows],
            send_sem=acc_send.at[way, part], recv_sem=acc_recv.at[way, part],
            device_id=along_x(way), device_id_type=MESH,
        )

    def add_pair(step):
        term_load(0, step).wait()
        pair_copy(step).wait_recv()

        def add(i, carry):
            rows = pl.ds(pl.multiple_of(i * 16, 16), 16)
            for j in range(TILES):
                own = terms[0, step, rows, pl.ds(j * LANES, LANES)].astype(jnp.float32)
                sums[step, j, rows, :] = own + pair_in[step, j, rows, :]
            return carry

        lax.fori_loop(0, ROWS // 16, add, 0)

    place_in_row = (
        lax.broadcasted_iota(jnp.int32, (TILES, LANES), 0) * LANES + lax.broadcasted_iota(jnp.int32, (TILES, LANES), 1)
    )

    def masked(a, row):
        live = place_in_row < frag_s[2, row]
        return jnp.where(live, state[a, pl.ds(row, TILES, stride=ROWS), :], -1.0 if a == 2 else 0.0)

    def fill_x(a):
        def fill(i, carry):
            for k in range(1, 4):
                x_out[a, k - 1, i] = masked(a, rank_s[0, k * WIDE + i])
            return carry

        lax.fori_loop(0, ROOM, fill, 0, unroll=4)

    def x_copy(a, k):
        return pltpu.make_async_remote_copy(
            src_ref=x_out.at[a, k - 1], dst_ref=x_in[a].at[3 - k], send_sem=x_send.at[a, k - 1],
            recv_sem=x_recv.at[a, 3 - k], device_id=x_peer(k), device_id_type=MESH,
        )

    def meta_copy(k):
        return pltpu.make_async_remote_copy(
            src_ref=meta_v, dst_ref=meta_in.at[3 - k], send_sem=meta_send.at[k - 1],
            recv_sem=meta_recv.at[3 - k], device_id=x_peer(k), device_id_type=MESH,
        )

    def column_peer(i):
        return partner(0, i % 4, (i // 4) % 4, i // 16)

    def post_near(dy, dz, dcore):
        target = partner(0, dy, dz, dcore)
        there, i = (target[0] % 2) * N_FSDP + target[1], dy + 4 * dz + 16 * dcore
        for slot in range(CAP):
            row = own_s[0, there * CAP + slot]
            for a in range(3):
                near_out[i, a, slot] = masked(a, row)
        pltpu.make_async_remote_copy(
            src_ref=near_out.at[i, pl.ds(1, 2)], dst_ref=recv.at[:, pl.ds(here * 8, CAP)],
            send_sem=near_send, recv_sem=near_recv, device_id=target, device_id_type=MESH,
        ).start()
        pltpu.make_async_remote_copy(
            src_ref=near_out.at[i, 0], dst_ref=recv_one.at[pl.ds(here * 8, CAP)],
            send_sem=one_send, recv_sem=one_recv, device_id=target, device_id_type=MESH,
        ).start()

    def post_line(i, carry):
        post_near((1 + i // 2) * (i % 2), (1 + i // 2) * ((i + 1) % 2), 0)
        return carry

    def post_plane(i, carry):
        post_near(1 + i % 3, 1 + (i + i // 3) % 3, 0)
        return carry

    def post_core(i, carry):
        post_near(i % 4, (i + i // 4) % 4, 1)
        return carry

    def moved(a, there, origin, slot):
        return x_in[a][origin - 1, meta_s[origin - 1, 1, (4 - origin) * WIDE + there * CAP + slot]]

    def post_far(a):
        def post(i, carry):
            target = column_peer(i)
            there = (target[0] % 2) * N_FSDP + target[1]
            for origin in range(1, 4):
                for slot in range(CAP):
                    far_out[a, i, (origin - 1) * CAP + slot] = moved(a, there, origin, slot)
            pltpu.make_async_remote_copy(
                src_ref=far_out.at[a, i], dst_ref=arrivals(a).at[pl.ds(here * 8 + CAP, 3 * CAP)],
                send_sem=far_send.at[a], recv_sem=far_recv.at[a], device_id=target, device_id_type=MESH,
            ).start()
            return carry

        for k in range(1, 4):
            x_copy(a, k).wait_recv()
        lax.fori_loop(1, COLUMN, post, 0)
        for origin in range(1, 4):
            for slot in range(CAP):
                arrivals(a)[here * 8 + origin * CAP + slot] = moved(a, here, origin, slot)

    def post_flag(i, carry):
        pltpu.make_async_remote_copy(
            src_ref=flag_mine, dst_ref=flag_in.at[here], send_sem=flag_send, recv_sem=flag_recv,
            device_id=column_peer(i), device_id_type=MESH,
        ).start()
        return carry

    for load in state_loads:
        load.wait()
    frag_load_s.wait()
    for copy in table_copies:
        copy.wait()
    fill_x(1)
    pl.semaphore_wait(barrier, 10)
    for k in range(1, 4):
        pl.semaphore_signal(y_sem, inc=1, device_id=y_peer(k), device_id_type=MESH)
    for k in (1, 3, 2):
        x_copy(1, k).start()
    for k in (1, 3, 2):
        meta_copy(k).start()
    fill_x(2)
    for k in (1, 3, 2):
        x_copy(2, k).start()
    pl.semaphore_wait(y_sem, 3)
    for k in range(1, 4):
        pl.semaphore_signal(z_sem, inc=1, device_id=z_peer(k), device_id_type=MESH)
    lax.fori_loop(0, 6, post_line, 0)
    fill_x(0)
    for k in (1, 3, 2):
        x_copy(0, k).start()
    pl.semaphore_wait(z_sem, 3)
    lax.fori_loop(0, 9, post_plane, 0)
    lax.fori_loop(0, 16, post_core, 0)
    for step in range(4):
        term_load(1, step).wait()

        def widen(i, carry, step=step):
            rows = pl.ds(pl.multiple_of(i * 16, 16), 16)
            for j in range(TILES):
                pair_out[step, j, rows, :] = terms[1, step, rows, pl.ds(j * LANES, LANES)].astype(jnp.float32)
            return carry

        lax.fori_loop(0, ROWS // 16, widen, 0)
        pair_copy(step).start()
    for slot in range(CAP):
        row = own_s[0, here * CAP + slot]
        for a in range(3):
            arrivals(a)[here * 8 + slot] = masked(a, row)
    add_pair(0)
    hop_copy(0).start()
    hop_copy(1).start()
    for way in range(2):
        add_pair(1 + way)
        last_copy(way).start()
    add_pair(3)
    for k in range(1, 4):
        meta_copy(k).wait_recv()
    flag = meta_v[pl.ds(2, 1), pl.ds(0, LANES)]
    for origin in range(3):
        flag = jnp.maximum(flag, meta_in[origin, pl.ds(2, 1), pl.ds(0, LANES)])
    flag = jnp.broadcast_to(flag.astype(jnp.float32), (8, LANES))
    flag_mine[...] = flag
    flag_in[here] = flag
    meta_load = pltpu.make_async_copy(meta_in, meta_s, small_sem.at[6])
    meta_load.start()
    lax.fori_loop(1, COLUMN, post_flag, 0)
    meta_load.wait()
    for a in order_of_arrays:
        post_far(a)
    for way in range(2):
        hop_copy(way).wait()

        def add_hop(i, carry, way=way):
            rows = pl.ds(pl.multiple_of(i * 16, 16), 16)
            for j in range(TILES // 2):
                sums[1 + way, way * (TILES // 2) + j, rows, :] += hop_in[way, j, rows, :]
            return carry

        lax.fori_loop(0, ROWS // 16, add_hop, 0)
    for part in range(PARTS):
        for way in range(2):
            acc_copy(way, part).start()
    for way in range(2):
        last_copy(way).wait()

    def add_last(i, carry):
        rows = pl.ds(pl.multiple_of(i * 16, 16), 16)
        for j in range(TILES):
            near = last_in[1, j, rows, :] if j < TILES // 2 else last_in[0, j - TILES // 2, rows, :]
            total[pl.ds(pl.multiple_of(j * ROWS + i * 16, 16), 16), :] = sums[3, j, rows, :] + near
        return carry

    lax.fori_loop(0, ROWS // 16, add_last, 0)

    others = COLUMN - 1
    near_here = recv.at[:, pl.ds(0, others * CAP)]
    pltpu.make_async_copy(near_here, near_here, near_recv).wait()
    for a in (1, 2):
        far_here = recv.at[a - 1, pl.ds(0, others * 3 * CAP)]
        pltpu.make_async_copy(far_here, far_here, far_recv.at[a]).wait()
    def update_moments(row, carry):
        slot = row_s[0, row]
        moment, second = recv[0, slot], recv[1, slot]
        live = second >= 0.0
        second = jnp.where(live, second, 0.0)
        grad = jnp.where(live, total[pl.ds(row, TILES, stride=ROWS), :], 0.0)
        new_moment = beta_one * moment + (1.0 - beta_one) * grad
        new_second = beta_two * second + (1.0 - beta_two) * grad * grad
        moment_hat = new_moment / (1.0 - beta_one**step_count)
        second_hat = new_second / (1.0 - beta_two**step_count)
        step_size[row] = moment_hat / (jnp.sqrt(second_hat) + epsilon)
        out[1, pl.ds(row, TILES, stride=ROWS), :] = new_moment
        out[2, pl.ds(row, TILES, stride=ROWS), :] = new_second
        return carry

    def update_master(row, carry):
        master = recv_one[row_s[0, row]]
        out[0, pl.ds(row, TILES, stride=ROWS), :] = master - learn_rate * (step_size[row] + decay_weight * master)
        return carry

    for part in range(PARTS):
        for way in range(2):
            acc_copy(way, part).wait_recv()
        for j in range(TILES):
            total[pl.ds(j * ROWS + part * CHUNK, CHUNK), :] += acc_in[j, pl.ds(part * CHUNK, CHUNK), :]
        lax.fori_loop(part * CHUNK, (part + 1) * CHUNK, update_moments, 0, unroll=8)
    flags_here = flag_in.at[pl.ds(0, others)]
    pltpu.make_async_copy(flags_here, flags_here, flag_recv).wait()
    flag_out[0] = jnp.max(flag_in[...]).astype(jnp.int32)
    one_here = recv_one.at[pl.ds(0, others * CAP)]
    pltpu.make_async_copy(one_here, one_here, one_recv).wait()
    far_here = recv_one.at[pl.ds(0, others * 3 * CAP)]
    pltpu.make_async_copy(far_here, far_here, far_recv.at[0]).wait()
    lax.fori_loop(0, ROWS, update_master, 0, unroll=8)

    near_sent = near_out.at[pl.ds(1, others), pl.ds(1, 2)]
    pltpu.make_async_copy(near_sent, near_sent, near_send).wait()
    one_sent = near_out.at[pl.ds(1, others), 0]
    pltpu.make_async_copy(one_sent, one_sent, one_send).wait()
    for a in range(3):
        far_sent = far_out.at[a, pl.ds(1, others)]
        pltpu.make_async_copy(far_sent, far_sent, far_send.at[a]).wait()
    flags_sent = flag_in.at[pl.ds(0, others)]
    pltpu.make_async_copy(flags_sent, flags_sent, flag_send).wait()
    for k in range(1, 4):
        meta_copy(k).wait_send()
        for a in range(3):
            x_copy(a, k).wait_send()
    for step in range(4):
        pair_copy(step).wait_send()
    for way in range(2):
        for part in range(PARTS):
            acc_copy(way, part).wait_send()


def write_out(updated, master_hbm, moment_hbm, second_hbm, sem):
    stores = []
    for a, target in enumerate((master_hbm, moment_hbm, second_hbm)):
        for j in range(TILES):
            stores.append(
                pltpu.make_async_copy(
                    updated.at[a, pl.ds(j * ROWS, ROWS)], target.at[:, pl.ds(j * LANES, LANES)], sem.at[a, j]
                )
            )
    for store in stores:
        store.start()
    for store in stores:
        store.wait()


def local(old_master, old_moment, old_second, frag_list, pair_counts, grad_partial):
    anywhere = pl.BlockSpec(memory_space=pl.ANY)
    on_chip = pl.BlockSpec(memory_space=pltpu.VMEM)
    shape = jax.ShapeDtypeStruct((ROWS, FRAG), jnp.float32)
    f32, i32 = jnp.float32, jnp.int32
    dma = pltpu.SemaphoreType.DMA
    arguments = (old_master, old_moment, old_second, frag_list, pair_counts.reshape(1, DEVICES), grad_partial)
    updated, flag = pl.pallas_call(
        kernel_fast,
        out_shape=(pltpu.VMEM((3, TILES * ROWS, LANES), f32), pltpu.SMEM((1,), i32)),
        in_specs=[anywhere] * 6,
        out_specs=(on_chip, pl.BlockSpec(memory_space=pltpu.SMEM)),
        scratch_shapes=[
            pltpu.VMEM((3, TILES * ROWS, LANES), f32),
            pltpu.VMEM((3, ROWS), i32),
            pltpu.VMEM((1, DEVICES), i32),
            pltpu.VMEM((8, DEVICES * CAP), i32),
            pltpu.VMEM((8, DEVICES * CAP), i32),
            pltpu.VMEM((8, ROWS), i32),
            pltpu.SMEM((3, ROWS), i32),
            pltpu.SMEM((8, DEVICES * CAP), i32),
            pltpu.SMEM((8, DEVICES * CAP), i32),
            pltpu.SMEM((3, 8, DEVICES * CAP), i32),
            pltpu.SMEM((8, ROWS), i32),
            pltpu.VMEM((3, 3, ROOM, TILES, LANES), f32),
            pltpu.VMEM((3, ROOM, TILES, LANES), f32),
            pltpu.VMEM((3, ROOM, TILES, LANES), f32),
            pltpu.VMEM((3, ROOM, TILES, LANES), f32),
            pltpu.VMEM((3, 8, DEVICES * CAP), i32),
            pltpu.VMEM((COLUMN, 3, CAP, TILES, LANES), f32),
            pltpu.VMEM((3, COLUMN, 3 * CAP, TILES, LANES), f32),
            pltpu.VMEM((8, LANES), f32),
            pltpu.VMEM((COLUMN, 8, LANES), f32),
            pltpu.VMEM((2, DEVICES * CAP, TILES, LANES), f32),
            pltpu.VMEM((DEVICES * CAP, TILES, LANES), f32),
            pltpu.VMEM((ROWS, TILES, LANES), f32),
            pltpu.VMEM((2, 4, ROWS, FRAG), jnp.bfloat16),
            pltpu.VMEM((4, TILES, ROWS, LANES), f32),
            pltpu.VMEM((4, TILES, ROWS, LANES), f32),
            pltpu.VMEM((4, TILES, ROWS, LANES), f32),
            pltpu.VMEM((2, TILES // 2, ROWS, LANES), f32),
            pltpu.VMEM((2, TILES // 2, ROWS, LANES), f32),
            pltpu.VMEM((TILES, ROWS, LANES), f32),
            pltpu.VMEM((TILES * ROWS, LANES), f32),
            dma((3, TILES)),
            dma((7,)),
            dma((2, 4)),
            dma((3, 3)),
            dma((3, 3)),
            dma((3,)),
            dma((3,)),
            dma,
            dma,
            dma,
            dma,
            dma((3,)),
            dma((3,)),
            dma,
            dma,
            dma((4,)),
            dma((4,)),
            dma((2,)),
            dma((2,)),
            dma((2,)),
            dma((2,)),
            dma((2, PARTS)),
            dma((2, PARTS)),
            pltpu.SemaphoreType.REGULAR,
            pltpu.SemaphoreType.REGULAR,
        ],
        compiler_params=pltpu.CompilerParams(
            collective_id=0, has_side_effects=True, vmem_limit_bytes=48 * 1024 * 1024
        ),
    )(*[pltpu.with_memory_space_constraint(a, pltpu.HBM) for a in arguments])

    def slow():
        return pl.pallas_call(
            kernel,
            out_shape=pltpu.VMEM((3, TILES * ROWS, LANES), f32),
            in_specs=[anywhere] * 6,
            out_specs=on_chip,
            scratch_shapes=[
                pltpu.VMEM((3, TILES * ROWS, LANES), f32),
                pltpu.VMEM((3, ROWS), i32),
                pltpu.VMEM((1, DEVICES), i32),
                pltpu.VMEM((8, DEVICES * CAP), i32),
                pltpu.VMEM((8, ROWS), i32),
                pltpu.SMEM((3, ROWS), i32),
                pltpu.SMEM((8, DEVICES * CAP), i32),
                pltpu.SMEM((8, ROWS), i32),
                pltpu.VMEM((DEVICES, CAP, 3 * TILES, LANES), f32),
                pltpu.VMEM((DEVICES * CAP, 3 * TILES, LANES), f32),
                pltpu.VMEM((2, 4, ROWS, FRAG), jnp.bfloat16),
                pltpu.VMEM((4, TILES, ROWS, LANES), f32),
                pltpu.VMEM((4, TILES, ROWS, LANES), f32),
                pltpu.VMEM((4, TILES, ROWS, LANES), f32),
                pltpu.VMEM((2, TILES // 2, ROWS, LANES), f32),
                pltpu.VMEM((2, TILES // 2, ROWS, LANES), f32),
                pltpu.VMEM((TILES, ROWS, LANES), f32),
                pltpu.VMEM((TILES * ROWS, LANES), f32),
                dma((3, TILES)),
                dma((5,)),
                dma((2, 4)),
                dma,
                dma,
                dma((4,)),
                dma((4,)),
                dma((2,)),
                dma((2,)),
                dma((2,)),
                dma((2,)),
                dma((2,)),
                dma((2,)),
                pltpu.SemaphoreType.REGULAR,
                pltpu.SemaphoreType.REGULAR,
            ],
            compiler_params=pltpu.CompilerParams(
                collective_id=1, has_side_effects=True, vmem_limit_bytes=48 * 1024 * 1024
            ),
        )(*[pltpu.with_memory_space_constraint(a, pltpu.HBM) for a in arguments])

    def write(updated):
        return pl.pallas_call(
            write_out,
            out_shape=(shape, shape, shape),
            in_specs=[anywhere],
            out_specs=(anywhere, anywhere, anywhere),
            scratch_shapes=[dma((3, TILES))],
            compiler_params=pltpu.CompilerParams(vmem_limit_bytes=1024 * 1024),
        )(pltpu.with_memory_space_constraint(updated, pltpu.VMEM))

    return lax.cond(flag[0] > 0, lambda: write(slow()), lambda: write(updated))


def solution(mesh):
    return jax.shard_map(
        local,
        mesh=mesh,
        in_specs=(
            P(("ctx", "fsdp"), None),
            P(("ctx", "fsdp"), None),
            P(("ctx", "fsdp"), None),
            P(None, ("ctx", "fsdp")),
            P(None, ("ctx", "fsdp")),
            P("ctx", None, "fsdp", None, None),
        ),
        out_specs=(P(("ctx", "fsdp"), None), P(("ctx", "fsdp"), None), P(("ctx", "fsdp"), None)),
        check_vma=False,
    )
```

```python
import functools

import jax
import jax.numpy as jnp
from jax import lax
from jax.experimental import pallas as pl
from jax.experimental.pallas import tpu as pltpu
from jax.sharding import PartitionSpec as P

MESH = pl.DeviceIdType.MESH

beta_one = 0.9
beta_two = 0.95
learn_rate = 0.0003
decay_weight = 0.1
epsilon = 1e-08
step_count = 1001.0

ROWS = 128
FRAG = 1024
TILES = 8
LANES = 128
N_CTX = 8
N_FSDP = 16
DEVICES = 128
CAP = 2
PARTS = 4
CHUNK = ROWS // PARTS
COLUMN = 32
WIDE = COLUMN * CAP
ROOM = 48


def place():
    ctx, fsdp = lax.axis_index("ctx"), lax.axis_index("fsdp")
    return ctx // 2, ctx % 2, fsdp // 4, fsdp % 4


def partner(dx, dy, dz, dcore):
    x, core, z, y = place()
    return ((x + dx) % 4) * 2 + (core + dcore) % 2, ((z + dz) % 4) * 4 + (y + dy) % 4


def kernel(
    master_hbm, moment_hbm, second_hbm, frag_hbm, counts_hbm, grad_hbm,
    out,
    state, frag_v, counts_v, slot_v, row_v, frag_s, slot_s, row_s,
    send, recv, terms, pair_out, pair_in, sums, hop_in, last_in, acc_in, total,
    state_sem, small_sem, terms_sem,
    packet_send, packet_recv, pair_send, pair_recv, hop_send, hop_recv, last_send, last_recv, acc_send, acc_recv,
    y_sem, z_sem,
):
    ctx, fsdp = lax.axis_index("ctx"), lax.axis_index("fsdp")
    x, core, z, y = place()
    me = ctx * N_FSDP + fsdp
    order = [(x + 2) % 4, (x + 1) % 4, (x + 3) % 4, x]

    def term_load(side, step):
        block = order[step] * 2 + (core + side) % 2
        return pltpu.make_async_copy(grad_hbm.at[0, block, 0], terms.at[side, step], terms_sem.at[side, step])

    def y_peer(k):
        return ctx, z * 4 + (y + k) % 4

    def z_peer(k):
        return ctx, ((z + k) % 4) * 4 + y

    barrier = pltpu.get_barrier_semaphore()
    for k in range(1, N_CTX):
        pl.semaphore_signal(barrier, inc=1, device_id=((ctx + k) % N_CTX, fsdp), device_id_type=MESH)
    for k in range(1, 4):
        pl.semaphore_signal(barrier, inc=1, device_id=y_peer(k), device_id_type=MESH)
    for k in range(1, 4):
        pl.semaphore_signal(barrier, inc=1, device_id=z_peer(k), device_id_type=MESH)

    for step in range(4):
        term_load(1, step).start()
    frag_load = pltpu.make_async_copy(frag_hbm, frag_v, small_sem.at[0])
    frag_load_s = pltpu.make_async_copy(frag_hbm, frag_s, small_sem.at[1])
    counts_load = pltpu.make_async_copy(counts_hbm, counts_v, small_sem.at[2])
    frag_load.start()
    frag_load_s.start()
    counts_load.start()
    for step in range(4):
        term_load(0, step).start()
    state_loads = []
    for a, source in enumerate((master_hbm, moment_hbm, second_hbm)):
        for j in range(TILES):
            state_loads.append(
                pltpu.make_async_copy(
                    source.at[:, pl.ds(j * LANES, LANES)],
                    state.at[a, pl.ds(j * ROWS, ROWS)],
                    state_sem.at[a, j],
                )
            )
    for load in state_loads:
        load.start()

    for step in range(4):
        term_load(1, step).wait()

        def widen(i, carry, step=step):
            rows = pl.ds(pl.multiple_of(i * 16, 16), 16)
            for j in range(TILES):
                pair_out[step, j, rows, :] = terms[1, step, rows, pl.ds(j * LANES, LANES)].astype(jnp.float32)
            return carry

        lax.fori_loop(0, ROWS // 16, widen, 0)

    frag_load.wait()
    counts_load.wait()
    owners, offsets = frag_v[pl.ds(0, 1), :], frag_v[pl.ds(1, 1), :]
    slot_of_row = owners * CAP + offsets
    slot_ids = lax.broadcasted_iota(jnp.int32, (DEVICES * CAP, ROWS), 0)
    hit = jnp.where(slot_ids == slot_of_row, 1.0, 0.0)
    row_ids = lax.broadcasted_iota(jnp.int32, (8, ROWS), 1).astype(jnp.float32)
    row_of_slot = lax.dot_general(row_ids, hit, (((1,), (1,)), ((), ())), preferred_element_type=jnp.float32)
    slot_v[...] = jnp.clip(row_of_slot.astype(jnp.int32), 0, ROWS - 1)
    counts = jnp.broadcast_to(counts_v[...].astype(jnp.float32), (8, DEVICES))
    earlier = jnp.where(
        lax.broadcasted_iota(jnp.int32, (DEVICES, DEVICES), 0) < lax.broadcasted_iota(jnp.int32, (DEVICES, DEVICES), 1),
        1.0, 0.0,
    )
    before = lax.dot_general(counts, earlier, (((1,), (0,)), ((), ())), preferred_element_type=jnp.float32)[0:1, :]
    rows_down = lax.broadcasted_iota(jnp.int32, (ROWS, DEVICES), 0).astype(jnp.float32)
    owner_ids = lax.broadcasted_iota(jnp.int32, (ROWS, DEVICES), 1).astype(jnp.float32)
    offset = rows_down - before
    from_owner = (offset >= 0.0) & (offset < counts[0:1, :])
    slot_here = jnp.where(from_owner, owner_ids * CAP + offset, 0.0)
    slot_of_new = lax.dot_general(
        jnp.ones((8, DEVICES), jnp.float32), slot_here, (((1,), (1,)), ((), ())), preferred_element_type=jnp.float32
    )
    row_v[...] = jnp.clip(slot_of_new.astype(jnp.int32), 0, DEVICES * CAP - 1)
    slot_copy = pltpu.make_async_copy(slot_v, slot_s, small_sem.at[3])
    row_copy = pltpu.make_async_copy(row_v, row_s, small_sem.at[4])
    slot_copy.start()
    row_copy.start()

    def pair_copy(step):
        return pltpu.make_async_remote_copy(
            src_ref=pair_out.at[step], dst_ref=pair_in.at[step], send_sem=pair_send.at[step],
            recv_sem=pair_recv.at[step], device_id=(x * 2 + 1 - core, fsdp), device_id_type=MESH,
        )

    def along_x(way):
        return ((x + (1 if way == 0 else 3)) % 4) * 2 + core, fsdp

    half = (pl.ds(0, TILES // 2), pl.ds(TILES // 2, TILES // 2))

    def hop_copy(way):
        return pltpu.make_async_remote_copy(
            src_ref=sums.at[0, half[way]], dst_ref=hop_in.at[way], send_sem=hop_send.at[way],
            recv_sem=hop_recv.at[way], device_id=along_x(way), device_id_type=MESH,
        )

    def last_copy(way):
        return pltpu.make_async_remote_copy(
            src_ref=sums.at[1 + way, half[1 - way]], dst_ref=last_in.at[way], send_sem=last_send.at[way],
            recv_sem=last_recv.at[way], device_id=along_x(way), device_id_type=MESH,
        )

    def acc_copy(way):
        return pltpu.make_async_remote_copy(
            src_ref=sums.at[1 + way, half[way]], dst_ref=acc_in.at[half[way]],
            send_sem=acc_send.at[way], recv_sem=acc_recv.at[way],
            device_id=along_x(way), device_id_type=MESH,
        )

    def add_pair(step):
        term_load(0, step).wait()
        pair_copy(step).wait_recv()

        def add(i, carry):
            rows = pl.ds(pl.multiple_of(i * 16, 16), 16)
            for j in range(TILES):
                own = terms[0, step, rows, pl.ds(j * LANES, LANES)].astype(jnp.float32)
                sums[step, j, rows, :] = own + pair_in[step, j, rows, :]
            return carry

        lax.fori_loop(0, ROWS // 16, add, 0)

    place_in_row = (
        lax.broadcasted_iota(jnp.int32, (TILES, LANES), 0) * LANES + lax.broadcasted_iota(jnp.int32, (TILES, LANES), 1)
    )

    def pack(device, slot):
        row = slot_s[0, device * CAP + slot]
        live = place_in_row < frag_s[2, row]
        values = [state[a, pl.ds(row, TILES, stride=ROWS), :] for a in range(3)]
        return [jnp.where(live, v, 0.0 if a < 2 else -1.0) for a, v in enumerate(values)]

    def post(dx, dy, dz, dcore):
        target = partner(dx, dy, dz, dcore)
        device, k = target[0] * N_FSDP + target[1], dx + 4 * dy + 16 * dz + 64 * dcore
        for slot in range(CAP):
            for a, v in enumerate(pack(device, slot)):
                send[k, slot, pl.ds(a * TILES, TILES), :] = v
        pltpu.make_async_remote_copy(
            src_ref=send.at[k], dst_ref=recv.at[pl.ds(me * CAP, CAP)],
            send_sem=packet_send, recv_sem=packet_recv, device_id=target, device_id_type=MESH,
        ).start()

    def post_line(i, carry):
        post(i % 4, 0, 0, i // 4)
        return carry

    def post_plane(i, carry):
        dx, k = i % 4, i // 4
        post(dx, 1 + (dx + k) % 3, 0, k // 3)
        return carry

    def post_rest(i, carry):
        dx, k = i % 4, i // 4
        post(dx, (dx + k) % 4, 1 + (dx + k // 4) % 3, k // 12)
        return carry

    for load in state_loads:
        load.wait()
    frag_load_s.wait()
    slot_copy.wait()
    row_copy.wait()
    pl.semaphore_wait(barrier, N_CTX - 1 + 6)
    for step in range(4):
        pair_copy(step).start()
    for k in range(1, 4):
        pl.semaphore_signal(y_sem, inc=1, device_id=y_peer(k), device_id_type=MESH)
    lax.fori_loop(1, N_CTX, post_line, 0)
    pl.semaphore_wait(y_sem, 3)
    for k in range(1, 4):
        pl.semaphore_signal(z_sem, inc=1, device_id=z_peer(k), device_id_type=MESH)
    add_pair(0)
    hop_copy(0).start()
    hop_copy(1).start()
    lax.fori_loop(0, 24, post_plane, 0)
    for way in range(2):
        add_pair(1 + way)
        last_copy(way).start()
    pl.semaphore_wait(z_sem, 3)
    lax.fori_loop(0, 96, post_rest, 0)

    for way in range(2):
        hop_copy(way).wait()

        def add_hop(i, carry, way=way):
            rows = pl.ds(pl.multiple_of(i * 16, 16), 16)
            for j in range(TILES // 2):
                sums[1 + way, way * (TILES // 2) + j, rows, :] += hop_in[way, j, rows, :]
            return carry

        lax.fori_loop(0, ROWS // 16, add_hop, 0)
        last_copy(way).wait_send()
        acc_copy(way).start()

    for slot in range(CAP):
        for a, v in enumerate(pack(me, slot)):
            recv[me * CAP + slot, pl.ds(a * TILES, TILES), :] = v
    add_pair(3)
    for way in range(2):
        last_copy(way).wait_recv()
    for way in range(2):
        acc_copy(way).wait_recv()

    def add_last(i, carry):
        rows = pl.ds(pl.multiple_of(i * 16, 16), 16)
        for j in range(TILES):
            near = last_in[1, j, rows, :] if j < TILES // 2 else last_in[0, j - TILES // 2, rows, :]
            total[pl.ds(pl.multiple_of(j * ROWS + i * 16, 16), 16), :] = (
                sums[3, j, rows, :] + near + acc_in[j, rows, :]
            )
        return carry

    lax.fori_loop(0, ROWS // 16, add_last, 0)

    all_here = recv.at[pl.ds(0, (DEVICES - 1) * CAP)]
    pltpu.make_async_copy(all_here, all_here, packet_recv).wait()

    def update(row, carry):
        slot = row_s[0, row]
        master, moment, second = [recv[slot, pl.ds(a * TILES, TILES), :] for a in range(3)]
        live = second >= 0.0
        second = jnp.where(live, second, 0.0)
        grad = jnp.where(live, total[pl.ds(row, TILES, stride=ROWS), :], 0.0)
        new_moment = beta_one * moment + (1.0 - beta_one) * grad
        new_second = beta_two * second + (1.0 - beta_two) * grad * grad
        moment_hat = new_moment / (1.0 - beta_one**step_count)
        second_hat = new_second / (1.0 - beta_two**step_count)
        new_master = master - learn_rate * (
            moment_hat / (jnp.sqrt(second_hat) + epsilon) + decay_weight * master
        )
        for a, v in enumerate((new_master, new_moment, new_second)):
            out[a, pl.ds(row, TILES, stride=ROWS), :] = v
        return carry

    lax.fori_loop(0, ROWS, update, 0, unroll=8)

    all_sent = send.at[pl.ds(1, DEVICES - 1)]
    pltpu.make_async_copy(all_sent, all_sent, packet_send).wait()
    for step in range(4):
        pair_copy(step).wait_send()
    for way in range(2):
        acc_copy(way).wait_send()


def kernel_fast(
    master_hbm, moment_hbm, second_hbm, frag_hbm, counts_hbm, grad_hbm,
    out, flag_out,
    state, frag_v, counts_v, rank_v, meta_v, row_v, frag_s, rank_s, own_s, meta_s, row_s,
    x_out, x_in_0, x_in_1, x_in_2, meta_in, near_out, far_out, flag_mine, flag_in, recv, recv_one, step_size, terms, pair_out, pair_in, sums, hop_in, last_in, acc_in, total,
    state_sem, small_sem, terms_sem,
    x_send, x_recv, meta_send, meta_recv, near_send, near_recv, one_send, one_recv, far_send, far_recv, flag_send, flag_recv, pair_send, pair_recv, hop_send, hop_recv, last_send, last_recv, acc_send, acc_recv,
    y_sem, z_sem,
):
    ctx, fsdp = lax.axis_index("ctx"), lax.axis_index("fsdp")
    x, core, z, y = place()
    here = core * N_FSDP + fsdp
    x_in = (x_in_0, x_in_1, x_in_2)
    order_of_arrays = (1, 2, 0)

    def arrivals(a):
        return recv_one if a == 0 else recv.at[a - 1]

    order = [(x + 2) % 4, (x + 1) % 4, (x + 3) % 4, x]

    def term_load(side, step):
        block = order[step] * 2 + (core + side) % 2
        return pltpu.make_async_copy(grad_hbm.at[0, block, 0], terms.at[side, step], terms_sem.at[side, step])

    def x_peer(k):
        return ((x + k) % 4) * 2 + core, fsdp

    def y_peer(k):
        return ctx, z * 4 + (y + k) % 4

    def z_peer(k):
        return ctx, ((z + k) % 4) * 4 + y

    barrier = pltpu.get_barrier_semaphore()
    pl.semaphore_signal(barrier, inc=1, device_id=(x * 2 + 1 - core, fsdp), device_id_type=MESH)
    for k in range(1, 4):
        pl.semaphore_signal(barrier, inc=1, device_id=x_peer(k), device_id_type=MESH)
    for k in range(1, 4):
        pl.semaphore_signal(barrier, inc=1, device_id=y_peer(k), device_id_type=MESH)
    for k in range(1, 4):
        pl.semaphore_signal(barrier, inc=1, device_id=z_peer(k), device_id_type=MESH)

    for step in range(4):
        term_load(1, step).start()
    frag_load = pltpu.make_async_copy(frag_hbm, frag_v, small_sem.at[0])
    frag_load_s = pltpu.make_async_copy(frag_hbm, frag_s, small_sem.at[1])
    counts_load = pltpu.make_async_copy(counts_hbm, counts_v, small_sem.at[2])
    frag_load.start()
    frag_load_s.start()
    counts_load.start()
    for step in range(4):
        term_load(0, step).start()
    state_loads = []
    for a, source in enumerate((master_hbm, moment_hbm, second_hbm)):
        for j in range(TILES):
            state_loads.append(
                pltpu.make_async_copy(
                    source.at[:, pl.ds(j * LANES, LANES)],
                    state.at[a, pl.ds(j * ROWS, ROWS)],
                    state_sem.at[a, j],
                )
            )
    for load in state_loads:
        load.start()

    frag_load.wait()
    counts_load.wait()
    owners, offsets = frag_v[pl.ds(0, 1), :], frag_v[pl.ds(1, 1), :]
    column = (owners // COLUMN - x + 4) % 4
    in_column = jnp.where(lax.broadcasted_iota(jnp.int32, (8, ROWS), 0) == column, 1.0, 0.0)
    earlier = jnp.where(
        lax.broadcasted_iota(jnp.int32, (DEVICES, DEVICES), 0) < lax.broadcasted_iota(jnp.int32, (DEVICES, DEVICES), 1),
        1.0, 0.0,
    )
    ranks = lax.dot_general(in_column, earlier, (((1,), (0,)), ((), ())), preferred_element_type=jnp.float32)
    rank = jnp.sum(in_column * ranks, axis=0, keepdims=True)
    over = jnp.max(jnp.where((rank >= ROOM) & (column > 0), 1.0, 0.0), axis=1, keepdims=True)
    place_ids = lax.broadcasted_iota(jnp.int32, (DEVICES * CAP, ROWS), 0)
    by_rank = jnp.where(place_ids == column * WIDE + rank.astype(jnp.int32), 1.0, 0.0)
    by_slot = jnp.where(place_ids == column * WIDE + (owners % COLUMN) * CAP + offsets, 1.0, 0.0)
    row_ids = lax.broadcasted_iota(jnp.int32, (8, ROWS), 1).astype(jnp.float32)
    which = lax.broadcasted_iota(jnp.int32, (8, ROWS), 0)
    row_of_rank = lax.dot_general(row_ids, by_rank, (((1,), (1,)), ((), ())), preferred_element_type=jnp.float32)
    rank_v[...] = jnp.clip(row_of_rank.astype(jnp.int32), 0, ROWS - 1)
    of_slot = lax.dot_general(
        jnp.where(which == 0, row_ids, rank), by_slot, (((1,), (1,)), ((), ())), preferred_element_type=jnp.float32
    )
    line = lax.broadcasted_iota(jnp.int32, (8, DEVICES * CAP), 0)
    top = jnp.where(line == 0, ROWS - 1, ROOM - 1)
    meta = jnp.clip(of_slot.astype(jnp.int32), 0, top)
    meta_v[...] = jnp.where(line == 2, over.astype(jnp.int32), meta)
    counts = jnp.broadcast_to(counts_v[...].astype(jnp.float32), (8, DEVICES))
    before = lax.dot_general(counts, earlier, (((1,), (0,)), ((), ())), preferred_element_type=jnp.float32)[0:1, :]
    rows_down = lax.broadcasted_iota(jnp.int32, (ROWS, DEVICES), 0).astype(jnp.float32)
    owner_ids = lax.broadcasted_iota(jnp.int32, (ROWS, DEVICES), 1)
    first = ((owner_ids % COLUMN) * 8 + ((owner_ids // COLUMN - x + 4) % 4) * CAP).astype(jnp.float32)
    offset = rows_down - before
    from_owner = (offset >= 0.0) & (offset < counts[0:1, :])
    slot_here = jnp.where(from_owner, first + offset, 0.0)
    slot_of_new = lax.dot_general(
        jnp.ones((8, DEVICES), jnp.float32), slot_here, (((1,), (1,)), ((), ())), preferred_element_type=jnp.float32
    )
    row_v[...] = jnp.clip(slot_of_new.astype(jnp.int32), 0, DEVICES * CAP - 1)
    table_copies = [
        pltpu.make_async_copy(source, target, small_sem.at[3 + i])
        for i, (source, target) in enumerate(((rank_v, rank_s), (meta_v, own_s), (row_v, row_s)))
    ]
    for copy in table_copies:
        copy.start()

    def pair_copy(step):
        return pltpu.make_async_remote_copy(
            src_ref=pair_out.at[step], dst_ref=pair_in.at[step], send_sem=pair_send.at[step],
            recv_sem=pair_recv.at[step], device_id=(x * 2 + 1 - core, fsdp), device_id_type=MESH,
        )

    def along_x(way):
        return ((x + (1 if way == 0 else 3)) % 4) * 2 + core, fsdp

    half = (pl.ds(0, TILES // 2), pl.ds(TILES // 2, TILES // 2))

    def hop_copy(way):
        return pltpu.make_async_remote_copy(
            src_ref=sums.at[0, half[way]], dst_ref=hop_in.at[way], send_sem=hop_send.at[way],
            recv_sem=hop_recv.at[way], device_id=along_x(way), device_id_type=MESH,
        )

    def last_copy(way):
        return pltpu.make_async_remote_copy(
            src_ref=sums.at[1 + way, half[1 - way]], dst_ref=last_in.at[way], send_sem=last_send.at[way],
            recv_sem=last_recv.at[way], device_id=along_x(way), device_id_type=MESH,
        )

    def acc_copy(way, part):
        rows = pl.ds(part * CHUNK, CHUNK)
        return pltpu.make_async_remote_copy(
            src_ref=sums.at[1 + way, half[way], rows], dst_ref=acc_in.at[half[way], rows],
            send_sem=acc_send.at[way, part], recv_sem=acc_recv.at[way, part],
            device_id=along_x(way), device_id_type=MESH,
        )

    def add_pair(step):
        term_load(0, step).wait()
        pair_copy(step).wait_recv()

        def add(i, carry):
            rows = pl.ds(pl.multiple_of(i * 16, 16), 16)
            for j in range(TILES):
                own = terms[0, step, rows, pl.ds(j * LANES, LANES)].astype(jnp.float32)
                sums[step, j, rows, :] = own + pair_in[step, j, rows, :]
            return carry

        lax.fori_loop(0, ROWS // 16, add, 0)

    place_in_row = (
        lax.broadcasted_iota(jnp.int32, (TILES, LANES), 0) * LANES + lax.broadcasted_iota(jnp.int32, (TILES, LANES), 1)
    )

    def masked(a, row):
        live = place_in_row < frag_s[2, row]
        return jnp.where(live, state[a, pl.ds(row, TILES, stride=ROWS), :], -1.0 if a == 2 else 0.0)

    def fill_x(a):
        def fill(i, carry):
            for k in range(1, 4):
                x_out[a, k - 1, i] = masked(a, rank_s[0, k * WIDE + i])
            return carry

        lax.fori_loop(0, ROOM, fill, 0, unroll=4)

    def x_copy(a, k):
        return pltpu.make_async_remote_copy(
            src_ref=x_out.at[a, k - 1], dst_ref=x_in[a].at[3 - k], send_sem=x_send.at[a, k - 1],
            recv_sem=x_recv.at[a, 3 - k], device_id=x_peer(k), device_id_type=MESH,
        )

    def meta_copy(k):
        return pltpu.make_async_remote_copy(
            src_ref=meta_v, dst_ref=meta_in.at[3 - k], send_sem=meta_send.at[k - 1],
            recv_sem=meta_recv.at[3 - k], device_id=x_peer(k), device_id_type=MESH,
        )

    def column_peer(i):
        return partner(0, i % 4, (i // 4) % 4, i // 16)

    def post_near(dy, dz, dcore):
        target = partner(0, dy, dz, dcore)
        there, i = (target[0] % 2) * N_FSDP + target[1], dy + 4 * dz + 16 * dcore
        for slot in range(CAP):
            row = own_s[0, there * CAP + slot]
            for a in range(3):
                near_out[i, a, slot] = masked(a, row)
        pltpu.make_async_remote_copy(
            src_ref=near_out.at[i, pl.ds(1, 2)], dst_ref=recv.at[:, pl.ds(here * 8, CAP)],
            send_sem=near_send, recv_sem=near_recv, device_id=target, device_id_type=MESH,
        ).start()
        pltpu.make_async_remote_copy(
            src_ref=near_out.at[i, 0], dst_ref=recv_one.at[pl.ds(here * 8, CAP)],
            send_sem=one_send, recv_sem=one_recv, device_id=target, device_id_type=MESH,
        ).start()

    def post_line(i, carry):
        post_near((1 + i // 2) * (i % 2), (1 + i // 2) * ((i + 1) % 2), 0)
        return carry

    def post_plane(i, carry):
        post_near(1 + i % 3, 1 + (i + i // 3) % 3, 0)
        return carry

    def post_core(i, carry):
        post_near(i % 4, (i + i // 4) % 4, 1)
        return carry

    def moved(a, there, origin, slot):
        return x_in[a][origin - 1, meta_s[origin - 1, 1, (4 - origin) * WIDE + there * CAP + slot]]

    def post_far(a):
        def post(i, carry):
            target = column_peer(i)
            there = (target[0] % 2) * N_FSDP + target[1]
            for origin in range(1, 4):
                for slot in range(CAP):
                    far_out[a, i, (origin - 1) * CAP + slot] = moved(a, there, origin, slot)
            pltpu.make_async_remote_copy(
                src_ref=far_out.at[a, i], dst_ref=arrivals(a).at[pl.ds(here * 8 + CAP, 3 * CAP)],
                send_sem=far_send.at[a], recv_sem=far_recv.at[a], device_id=target, device_id_type=MESH,
            ).start()
            return carry

        for k in range(1, 4):
            x_copy(a, k).wait_recv()
        lax.fori_loop(1, COLUMN, post, 0, unroll=2)
        for origin in range(1, 4):
            for slot in range(CAP):
                arrivals(a)[here * 8 + origin * CAP + slot] = moved(a, here, origin, slot)

    def post_flag(i, carry):
        pltpu.make_async_remote_copy(
            src_ref=flag_mine, dst_ref=flag_in.at[here], send_sem=flag_send, recv_sem=flag_recv,
            device_id=column_peer(i), device_id_type=MESH,
        ).start()
        return carry

    for load in state_loads:
        load.wait()
    frag_load_s.wait()
    for copy in table_copies:
        copy.wait()
    fill_x(1)
    pl.semaphore_wait(barrier, 10)
    for k in range(1, 4):
        pl.semaphore_signal(y_sem, inc=1, device_id=y_peer(k), device_id_type=MESH)
    for k in (1, 3, 2):
        x_copy(1, k).start()
    for k in (1, 3, 2):
        meta_copy(k).start()
    fill_x(2)
    for k in (1, 3, 2):
        x_copy(2, k).start()
    pl.semaphore_wait(y_sem, 3)
    for k in range(1, 4):
        pl.semaphore_signal(z_sem, inc=1, device_id=z_peer(k), device_id_type=MESH)
    lax.fori_loop(0, 6, post_line, 0)
    fill_x(0)
    for k in (1, 3, 2):
        x_copy(0, k).start()
    pl.semaphore_wait(z_sem, 3)
    lax.fori_loop(0, 9, post_plane, 0)
    lax.fori_loop(0, 16, post_core, 0)
    for step in range(4):
        term_load(1, step).wait()

        def widen(i, carry, step=step):
            rows = pl.ds(pl.multiple_of(i * 16, 16), 16)
            for j in range(TILES):
                pair_out[step, j, rows, :] = terms[1, step, rows, pl.ds(j * LANES, LANES)].astype(jnp.float32)
            return carry

        lax.fori_loop(0, ROWS // 16, widen, 0)
        pair_copy(step).start()
    for slot in range(CAP):
        row = own_s[0, here * CAP + slot]
        for a in range(3):
            arrivals(a)[here * 8 + slot] = masked(a, row)
    add_pair(0)
    hop_copy(0).start()
    hop_copy(1).start()
    for way in range(2):
        add_pair(1 + way)
        last_copy(way).start()
    add_pair(3)
    for k in range(1, 4):
        meta_copy(k).wait_recv()
    flag = meta_v[pl.ds(2, 1), pl.ds(0, LANES)]
    for origin in range(3):
        flag = jnp.maximum(flag, meta_in[origin, pl.ds(2, 1), pl.ds(0, LANES)])
    flag = jnp.broadcast_to(flag.astype(jnp.float32), (8, LANES))
    flag_mine[...] = flag
    flag_in[here] = flag
    meta_load = pltpu.make_async_copy(meta_in, meta_s, small_sem.at[6])
    meta_load.start()
    lax.fori_loop(1, COLUMN, post_flag, 0)
    meta_load.wait()
    for a in order_of_arrays:
        post_far(a)
    for way in range(2):
        hop_copy(way).wait()

        def add_hop(i, carry, way=way):
            rows = pl.ds(pl.multiple_of(i * 16, 16), 16)
            for j in range(TILES // 2):
                sums[1 + way, way * (TILES // 2) + j, rows, :] += hop_in[way, j, rows, :]
            return carry

        lax.fori_loop(0, ROWS // 16, add_hop, 0)
    for part in range(PARTS):
        for way in range(2):
            acc_copy(way, part).start()
    for way in range(2):
        last_copy(way).wait()

    def add_last(i, carry):
        rows = pl.ds(pl.multiple_of(i * 16, 16), 16)
        for j in range(TILES):
            near = last_in[1, j, rows, :] if j < TILES // 2 else last_in[0, j - TILES // 2, rows, :]
            total[pl.ds(pl.multiple_of(j * ROWS + i * 16, 16), 16), :] = sums[3, j, rows, :] + near
        return carry

    lax.fori_loop(0, ROWS // 16, add_last, 0)

    others = COLUMN - 1
    near_here = recv.at[:, pl.ds(0, others * CAP)]
    pltpu.make_async_copy(near_here, near_here, near_recv).wait()
    for a in (1, 2):
        far_here = recv.at[a - 1, pl.ds(0, others * 3 * CAP)]
        pltpu.make_async_copy(far_here, far_here, far_recv.at[a]).wait()
    def update_moments(row, carry):
        slot = row_s[0, row]
        moment, second = recv[0, slot], recv[1, slot]
        live = second >= 0.0
        second = jnp.where(live, second, 0.0)
        grad = jnp.where(live, total[pl.ds(row, TILES, stride=ROWS), :], 0.0)
        new_moment = beta_one * moment + (1.0 - beta_one) * grad
        new_second = beta_two * second + (1.0 - beta_two) * grad * grad
        moment_hat = new_moment / (1.0 - beta_one**step_count)
        second_hat = new_second / (1.0 - beta_two**step_count)
        step_size[row] = moment_hat / (jnp.sqrt(second_hat) + epsilon)
        out[1, pl.ds(row, TILES, stride=ROWS), :] = new_moment
        out[2, pl.ds(row, TILES, stride=ROWS), :] = new_second
        return carry

    def update_master(row, carry):
        master = recv_one[row_s[0, row]]
        out[0, pl.ds(row, TILES, stride=ROWS), :] = master - learn_rate * (step_size[row] + decay_weight * master)
        return carry

    for part in range(PARTS):
        for way in range(2):
            acc_copy(way, part).wait_recv()
        for j in range(TILES):
            total[pl.ds(j * ROWS + part * CHUNK, CHUNK), :] += acc_in[j, pl.ds(part * CHUNK, CHUNK), :]
        lax.fori_loop(part * CHUNK, (part + 1) * CHUNK, update_moments, 0, unroll=8)
    flags_here = flag_in.at[pl.ds(0, others)]
    pltpu.make_async_copy(flags_here, flags_here, flag_recv).wait()
    flag_out[0] = jnp.max(flag_in[...]).astype(jnp.int32)
    one_here = recv_one.at[pl.ds(0, others * CAP)]
    pltpu.make_async_copy(one_here, one_here, one_recv).wait()
    far_here = recv_one.at[pl.ds(0, others * 3 * CAP)]
    pltpu.make_async_copy(far_here, far_here, far_recv.at[0]).wait()
    lax.fori_loop(0, ROWS, update_master, 0, unroll=8)

    near_sent = near_out.at[pl.ds(1, others), pl.ds(1, 2)]
    pltpu.make_async_copy(near_sent, near_sent, near_send).wait()
    one_sent = near_out.at[pl.ds(1, others), 0]
    pltpu.make_async_copy(one_sent, one_sent, one_send).wait()
    for a in range(3):
        far_sent = far_out.at[a, pl.ds(1, others)]
        pltpu.make_async_copy(far_sent, far_sent, far_send.at[a]).wait()
    flags_sent = flag_in.at[pl.ds(0, others)]
    pltpu.make_async_copy(flags_sent, flags_sent, flag_send).wait()
    for k in range(1, 4):
        meta_copy(k).wait_send()
        for a in range(3):
            x_copy(a, k).wait_send()
    for step in range(4):
        pair_copy(step).wait_send()
    for way in range(2):
        for part in range(PARTS):
            acc_copy(way, part).wait_send()


def write_out(updated, master_hbm, moment_hbm, second_hbm, sem):
    stores = []
    for a, target in enumerate((master_hbm, moment_hbm, second_hbm)):
        for j in range(TILES):
            stores.append(
                pltpu.make_async_copy(
                    updated.at[a, pl.ds(j * ROWS, ROWS)], target.at[:, pl.ds(j * LANES, LANES)], sem.at[a, j]
                )
            )
    for store in stores:
        store.start()
    for store in stores:
        store.wait()


def local(old_master, old_moment, old_second, frag_list, pair_counts, grad_partial):
    anywhere = pl.BlockSpec(memory_space=pl.ANY)
    on_chip = pl.BlockSpec(memory_space=pltpu.VMEM)
    shape = jax.ShapeDtypeStruct((ROWS, FRAG), jnp.float32)
    f32, i32 = jnp.float32, jnp.int32
    dma = pltpu.SemaphoreType.DMA
    arguments = (old_master, old_moment, old_second, frag_list, pair_counts.reshape(1, DEVICES), grad_partial)
    updated, flag = pl.pallas_call(
        kernel_fast,
        out_shape=(pltpu.VMEM((3, TILES * ROWS, LANES), f32), pltpu.SMEM((1,), i32)),
        in_specs=[anywhere] * 6,
        out_specs=(on_chip, pl.BlockSpec(memory_space=pltpu.SMEM)),
        scratch_shapes=[
            pltpu.VMEM((3, TILES * ROWS, LANES), f32),
            pltpu.VMEM((3, ROWS), i32),
            pltpu.VMEM((1, DEVICES), i32),
            pltpu.VMEM((8, DEVICES * CAP), i32),
            pltpu.VMEM((8, DEVICES * CAP), i32),
            pltpu.VMEM((8, ROWS), i32),
            pltpu.SMEM((3, ROWS), i32),
            pltpu.SMEM((8, DEVICES * CAP), i32),
            pltpu.SMEM((8, DEVICES * CAP), i32),
            pltpu.SMEM((3, 8, DEVICES * CAP), i32),
            pltpu.SMEM((8, ROWS), i32),
            pltpu.VMEM((3, 3, ROOM, TILES, LANES), f32),
            pltpu.VMEM((3, ROOM, TILES, LANES), f32),
            pltpu.VMEM((3, ROOM, TILES, LANES), f32),
            pltpu.VMEM((3, ROOM, TILES, LANES), f32),
            pltpu.VMEM((3, 8, DEVICES * CAP), i32),
            pltpu.VMEM((COLUMN, 3, CAP, TILES, LANES), f32),
            pltpu.VMEM((3, COLUMN, 3 * CAP, TILES, LANES), f32),
            pltpu.VMEM((8, LANES), f32),
            pltpu.VMEM((COLUMN, 8, LANES), f32),
            pltpu.VMEM((2, DEVICES * CAP, TILES, LANES), f32),
            pltpu.VMEM((DEVICES * CAP, TILES, LANES), f32),
            pltpu.VMEM((ROWS, TILES, LANES), f32),
            pltpu.VMEM((2, 4, ROWS, FRAG), jnp.bfloat16),
            pltpu.VMEM((4, TILES, ROWS, LANES), f32),
            pltpu.VMEM((4, TILES, ROWS, LANES), f32),
            pltpu.VMEM((4, TILES, ROWS, LANES), f32),
            pltpu.VMEM((2, TILES // 2, ROWS, LANES), f32),
            pltpu.VMEM((2, TILES // 2, ROWS, LANES), f32),
            pltpu.VMEM((TILES, ROWS, LANES), f32),
            pltpu.VMEM((TILES * ROWS, LANES), f32),
            dma((3, TILES)),
            dma((7,)),
            dma((2, 4)),
            dma((3, 3)),
            dma((3, 3)),
            dma((3,)),
            dma((3,)),
            dma,
            dma,
            dma,
            dma,
            dma((3,)),
            dma((3,)),
            dma,
            dma,
            dma((4,)),
            dma((4,)),
            dma((2,)),
            dma((2,)),
            dma((2,)),
            dma((2,)),
            dma((2, PARTS)),
            dma((2, PARTS)),
            pltpu.SemaphoreType.REGULAR,
            pltpu.SemaphoreType.REGULAR,
        ],
        compiler_params=pltpu.CompilerParams(
            collective_id=0, has_side_effects=True, vmem_limit_bytes=48 * 1024 * 1024
        ),
    )(*[pltpu.with_memory_space_constraint(a, pltpu.HBM) for a in arguments])

    def slow():
        return pl.pallas_call(
            kernel,
            out_shape=pltpu.VMEM((3, TILES * ROWS, LANES), f32),
            in_specs=[anywhere] * 6,
            out_specs=on_chip,
            scratch_shapes=[
                pltpu.VMEM((3, TILES * ROWS, LANES), f32),
                pltpu.VMEM((3, ROWS), i32),
                pltpu.VMEM((1, DEVICES), i32),
                pltpu.VMEM((8, DEVICES * CAP), i32),
                pltpu.VMEM((8, ROWS), i32),
                pltpu.SMEM((3, ROWS), i32),
                pltpu.SMEM((8, DEVICES * CAP), i32),
                pltpu.SMEM((8, ROWS), i32),
                pltpu.VMEM((DEVICES, CAP, 3 * TILES, LANES), f32),
                pltpu.VMEM((DEVICES * CAP, 3 * TILES, LANES), f32),
                pltpu.VMEM((2, 4, ROWS, FRAG), jnp.bfloat16),
                pltpu.VMEM((4, TILES, ROWS, LANES), f32),
                pltpu.VMEM((4, TILES, ROWS, LANES), f32),
                pltpu.VMEM((4, TILES, ROWS, LANES), f32),
                pltpu.VMEM((2, TILES // 2, ROWS, LANES), f32),
                pltpu.VMEM((2, TILES // 2, ROWS, LANES), f32),
                pltpu.VMEM((TILES, ROWS, LANES), f32),
                pltpu.VMEM((TILES * ROWS, LANES), f32),
                dma((3, TILES)),
                dma((5,)),
                dma((2, 4)),
                dma,
                dma,
                dma((4,)),
                dma((4,)),
                dma((2,)),
                dma((2,)),
                dma((2,)),
                dma((2,)),
                dma((2,)),
                dma((2,)),
                pltpu.SemaphoreType.REGULAR,
                pltpu.SemaphoreType.REGULAR,
            ],
            compiler_params=pltpu.CompilerParams(
                collective_id=1, has_side_effects=True, vmem_limit_bytes=48 * 1024 * 1024
            ),
        )(*[pltpu.with_memory_space_constraint(a, pltpu.HBM) for a in arguments])

    def write(updated):
        return pl.pallas_call(
            write_out,
            out_shape=(shape, shape, shape),
            in_specs=[anywhere],
            out_specs=(anywhere, anywhere, anywhere),
            scratch_shapes=[dma((3, TILES))],
            compiler_params=pltpu.CompilerParams(vmem_limit_bytes=1024 * 1024),
        )(pltpu.with_memory_space_constraint(updated, pltpu.VMEM))

    return lax.cond(flag[0] > 0, lambda: write(slow()), lambda: write(updated))


def solution(mesh):
    return jax.shard_map(
        local,
        mesh=mesh,
        in_specs=(
            P(("ctx", "fsdp"), None),
            P(("ctx", "fsdp"), None),
            P(("ctx", "fsdp"), None),
            P(None, ("ctx", "fsdp")),
            P(None, ("ctx", "fsdp")),
            P("ctx", None, "fsdp", None, None),
        ),
        out_specs=(P(("ctx", "fsdp"), None), P(("ctx", "fsdp"), None), P(("ctx", "fsdp"), None)),
        check_vma=False,
    )
```

```python
import functools

import jax
import jax.numpy as jnp
from jax import lax
from jax.experimental import pallas as pl
from jax.experimental.pallas import tpu as pltpu
from jax.sharding import PartitionSpec as P

MESH = pl.DeviceIdType.MESH

beta_one = 0.9
beta_two = 0.95
learn_rate = 0.0003
decay_weight = 0.1
epsilon = 1e-08
step_count = 1001.0

ROWS = 128
FRAG = 1024
TILES = 8
LANES = 128
N_CTX = 8
N_FSDP = 16
DEVICES = 128
CAP = 2
PARTS = 4
CHUNK = ROWS // PARTS
COLUMN = 32
WIDE = COLUMN * CAP
ROOM = 48


def place():
    ctx, fsdp = lax.axis_index("ctx"), lax.axis_index("fsdp")
    return ctx // 2, ctx % 2, fsdp // 4, fsdp % 4


def partner(dx, dy, dz, dcore):
    x, core, z, y = place()
    return ((x + dx) % 4) * 2 + (core + dcore) % 2, ((z + dz) % 4) * 4 + (y + dy) % 4


def kernel(
    master_hbm, moment_hbm, second_hbm, frag_hbm, counts_hbm, grad_hbm,
    out,
    state, frag_v, counts_v, slot_v, row_v, frag_s, slot_s, row_s,
    send, recv, terms, pair_out, pair_in, sums, hop_in, last_in, acc_in, total,
    state_sem, small_sem, terms_sem,
    packet_send, packet_recv, pair_send, pair_recv, hop_send, hop_recv, last_send, last_recv, acc_send, acc_recv,
    y_sem, z_sem,
):
    ctx, fsdp = lax.axis_index("ctx"), lax.axis_index("fsdp")
    x, core, z, y = place()
    me = ctx * N_FSDP + fsdp
    order = [(x + 2) % 4, (x + 1) % 4, (x + 3) % 4, x]

    def term_load(side, step):
        block = order[step] * 2 + (core + side) % 2
        return pltpu.make_async_copy(grad_hbm.at[0, block, 0], terms.at[side, step], terms_sem.at[side, step])

    def y_peer(k):
        return ctx, z * 4 + (y + k) % 4

    def z_peer(k):
        return ctx, ((z + k) % 4) * 4 + y

    barrier = pltpu.get_barrier_semaphore()
    for k in range(1, N_CTX):
        pl.semaphore_signal(barrier, inc=1, device_id=((ctx + k) % N_CTX, fsdp), device_id_type=MESH)
    for k in range(1, 4):
        pl.semaphore_signal(barrier, inc=1, device_id=y_peer(k), device_id_type=MESH)
    for k in range(1, 4):
        pl.semaphore_signal(barrier, inc=1, device_id=z_peer(k), device_id_type=MESH)

    for step in range(4):
        term_load(1, step).start()
    frag_load = pltpu.make_async_copy(frag_hbm, frag_v, small_sem.at[0])
    frag_load_s = pltpu.make_async_copy(frag_hbm, frag_s, small_sem.at[1])
    counts_load = pltpu.make_async_copy(counts_hbm, counts_v, small_sem.at[2])
    frag_load.start()
    frag_load_s.start()
    counts_load.start()
    for step in range(4):
        term_load(0, step).start()
    state_loads = []
    for a, source in enumerate((master_hbm, moment_hbm, second_hbm)):
        for j in range(TILES):
            state_loads.append(
                pltpu.make_async_copy(
                    source.at[:, pl.ds(j * LANES, LANES)],
                    state.at[a, pl.ds(j * ROWS, ROWS)],
                    state_sem.at[a, j],
                )
            )
    for load in state_loads:
        load.start()

    for step in range(4):
        term_load(1, step).wait()

        def widen(i, carry, step=step):
            rows = pl.ds(pl.multiple_of(i * 16, 16), 16)
            for j in range(TILES):
                pair_out[step, j, rows, :] = terms[1, step, rows, pl.ds(j * LANES, LANES)].astype(jnp.float32)
            return carry

        lax.fori_loop(0, ROWS // 16, widen, 0)

    frag_load.wait()
    counts_load.wait()
    owners, offsets = frag_v[pl.ds(0, 1), :], frag_v[pl.ds(1, 1), :]
    slot_of_row = owners * CAP + offsets
    slot_ids = lax.broadcasted_iota(jnp.int32, (DEVICES * CAP, ROWS), 0)
    hit = jnp.where(slot_ids == slot_of_row, 1.0, 0.0)
    row_ids = lax.broadcasted_iota(jnp.int32, (8, ROWS), 1).astype(jnp.float32)
    row_of_slot = lax.dot_general(row_ids, hit, (((1,), (1,)), ((), ())), preferred_element_type=jnp.float32)
    slot_v[...] = jnp.clip(row_of_slot.astype(jnp.int32), 0, ROWS - 1)
    counts = jnp.broadcast_to(counts_v[...].astype(jnp.float32), (8, DEVICES))
    earlier = jnp.where(
        lax.broadcasted_iota(jnp.int32, (DEVICES, DEVICES), 0) < lax.broadcasted_iota(jnp.int32, (DEVICES, DEVICES), 1),
        1.0, 0.0,
    )
    before = lax.dot_general(counts, earlier, (((1,), (0,)), ((), ())), preferred_element_type=jnp.float32)[0:1, :]
    rows_down = lax.broadcasted_iota(jnp.int32, (ROWS, DEVICES), 0).astype(jnp.float32)
    owner_ids = lax.broadcasted_iota(jnp.int32, (ROWS, DEVICES), 1).astype(jnp.float32)
    offset = rows_down - before
    from_owner = (offset >= 0.0) & (offset < counts[0:1, :])
    slot_here = jnp.where(from_owner, owner_ids * CAP + offset, 0.0)
    slot_of_new = lax.dot_general(
        jnp.ones((8, DEVICES), jnp.float32), slot_here, (((1,), (1,)), ((), ())), preferred_element_type=jnp.float32
    )
    row_v[...] = jnp.clip(slot_of_new.astype(jnp.int32), 0, DEVICES * CAP - 1)
    slot_copy = pltpu.make_async_copy(slot_v, slot_s, small_sem.at[3])
    row_copy = pltpu.make_async_copy(row_v, row_s, small_sem.at[4])
    slot_copy.start()
    row_copy.start()

    def pair_copy(step):
        return pltpu.make_async_remote_copy(
            src_ref=pair_out.at[step], dst_ref=pair_in.at[step], send_sem=pair_send.at[step],
            recv_sem=pair_recv.at[step], device_id=(x * 2 + 1 - core, fsdp), device_id_type=MESH,
        )

    def along_x(way):
        return ((x + (1 if way == 0 else 3)) % 4) * 2 + core, fsdp

    half = (pl.ds(0, TILES // 2), pl.ds(TILES // 2, TILES // 2))

    def hop_copy(way):
        return pltpu.make_async_remote_copy(
            src_ref=sums.at[0, half[way]], dst_ref=hop_in.at[way], send_sem=hop_send.at[way],
            recv_sem=hop_recv.at[way], device_id=along_x(way), device_id_type=MESH,
        )

    def last_copy(way):
        return pltpu.make_async_remote_copy(
            src_ref=sums.at[1 + way, half[1 - way]], dst_ref=last_in.at[way], send_sem=last_send.at[way],
            recv_sem=last_recv.at[way], device_id=along_x(way), device_id_type=MESH,
        )

    def acc_copy(way):
        return pltpu.make_async_remote_copy(
            src_ref=sums.at[1 + way, half[way]], dst_ref=acc_in.at[half[way]],
            send_sem=acc_send.at[way], recv_sem=acc_recv.at[way],
            device_id=along_x(way), device_id_type=MESH,
        )

    def add_pair(step):
        term_load(0, step).wait()
        pair_copy(step).wait_recv()

        def add(i, carry):
            rows = pl.ds(pl.multiple_of(i * 16, 16), 16)
            for j in range(TILES):
                own = terms[0, step, rows, pl.ds(j * LANES, LANES)].astype(jnp.float32)
                sums[step, j, rows, :] = own + pair_in[step, j, rows, :]
            return carry

        lax.fori_loop(0, ROWS // 16, add, 0)

    place_in_row = (
        lax.broadcasted_iota(jnp.int32, (TILES, LANES), 0) * LANES + lax.broadcasted_iota(jnp.int32, (TILES, LANES), 1)
    )

    def pack(device, slot):
        row = slot_s[0, device * CAP + slot]
        live = place_in_row < frag_s[2, row]
        values = [state[a, pl.ds(row, TILES, stride=ROWS), :] for a in range(3)]
        return [jnp.where(live, v, 0.0 if a < 2 else -1.0) for a, v in enumerate(values)]

    def post(dx, dy, dz, dcore):
        target = partner(dx, dy, dz, dcore)
        device, k = target[0] * N_FSDP + target[1], dx + 4 * dy + 16 * dz + 64 * dcore
        for slot in range(CAP):
            for a, v in enumerate(pack(device, slot)):
                send[k, slot, pl.ds(a * TILES, TILES), :] = v
        pltpu.make_async_remote_copy(
            src_ref=send.at[k], dst_ref=recv.at[pl.ds(me * CAP, CAP)],
            send_sem=packet_send, recv_sem=packet_recv, device_id=target, device_id_type=MESH,
        ).start()

    def post_line(i, carry):
        post(i % 4, 0, 0, i // 4)
        return carry

    def post_plane(i, carry):
        dx, k = i % 4, i // 4
        post(dx, 1 + (dx + k) % 3, 0, k // 3)
        return carry

    def post_rest(i, carry):
        dx, k = i % 4, i // 4
        post(dx, (dx + k) % 4, 1 + (dx + k // 4) % 3, k // 12)
        return carry

    for load in state_loads:
        load.wait()
    frag_load_s.wait()
    slot_copy.wait()
    row_copy.wait()
    pl.semaphore_wait(barrier, N_CTX - 1 + 6)
    for step in range(4):
        pair_copy(step).start()
    for k in range(1, 4):
        pl.semaphore_signal(y_sem, inc=1, device_id=y_peer(k), device_id_type=MESH)
    lax.fori_loop(1, N_CTX, post_line, 0)
    pl.semaphore_wait(y_sem, 3)
    for k in range(1, 4):
        pl.semaphore_signal(z_sem, inc=1, device_id=z_peer(k), device_id_type=MESH)
    add_pair(0)
    hop_copy(0).start()
    hop_copy(1).start()
    lax.fori_loop(0, 24, post_plane, 0)
    for way in range(2):
        add_pair(1 + way)
        last_copy(way).start()
    pl.semaphore_wait(z_sem, 3)
    lax.fori_loop(0, 96, post_rest, 0)

    for way in range(2):
        hop_copy(way).wait()

        def add_hop(i, carry, way=way):
            rows = pl.ds(pl.multiple_of(i * 16, 16), 16)
            for j in range(TILES // 2):
                sums[1 + way, way * (TILES // 2) + j, rows, :] += hop_in[way, j, rows, :]
            return carry

        lax.fori_loop(0, ROWS // 16, add_hop, 0)
        last_copy(way).wait_send()
        acc_copy(way).start()

    for slot in range(CAP):
        for a, v in enumerate(pack(me, slot)):
            recv[me * CAP + slot, pl.ds(a * TILES, TILES), :] = v
    add_pair(3)
    for way in range(2):
        last_copy(way).wait_recv()
    for way in range(2):
        acc_copy(way).wait_recv()

    def add_last(i, carry):
        rows = pl.ds(pl.multiple_of(i * 16, 16), 16)
        for j in range(TILES):
            near = last_in[1, j, rows, :] if j < TILES // 2 else last_in[0, j - TILES // 2, rows, :]
            total[pl.ds(pl.multiple_of(j * ROWS + i * 16, 16), 16), :] = (
                sums[3, j, rows, :] + near + acc_in[j, rows, :]
            )
        return carry

    lax.fori_loop(0, ROWS // 16, add_last, 0)

    all_here = recv.at[pl.ds(0, (DEVICES - 1) * CAP)]
    pltpu.make_async_copy(all_here, all_here, packet_recv).wait()

    def update(row, carry):
        slot = row_s[0, row]
        master, moment, second = [recv[slot, pl.ds(a * TILES, TILES), :] for a in range(3)]
        live = second >= 0.0
        second = jnp.where(live, second, 0.0)
        grad = jnp.where(live, total[pl.ds(row, TILES, stride=ROWS), :], 0.0)
        new_moment = beta_one * moment + (1.0 - beta_one) * grad
        new_second = beta_two * second + (1.0 - beta_two) * grad * grad
        moment_hat = new_moment / (1.0 - beta_one**step_count)
        second_hat = new_second / (1.0 - beta_two**step_count)
        new_master = master - learn_rate * (
            moment_hat / (jnp.sqrt(second_hat) + epsilon) + decay_weight * master
        )
        for a, v in enumerate((new_master, new_moment, new_second)):
            out[a, pl.ds(row, TILES, stride=ROWS), :] = v
        return carry

    lax.fori_loop(0, ROWS, update, 0, unroll=8)

    all_sent = send.at[pl.ds(1, DEVICES - 1)]
    pltpu.make_async_copy(all_sent, all_sent, packet_send).wait()
    for step in range(4):
        pair_copy(step).wait_send()
    for way in range(2):
        acc_copy(way).wait_send()


def kernel_fast(
    master_hbm, moment_hbm, second_hbm, frag_hbm, counts_hbm, grad_hbm,
    out, flag_out,
    state, frag_v, counts_v, rank_v, meta_v, row_v, frag_s, rank_s, own_s, meta_s, row_s,
    x_out, x_in_0, x_in_1, x_in_2, meta_in, near_out, far_out, flag_mine, flag_in, recv, recv_one, step_size, terms, pair_out, pair_in, sums, hop_in, last_in, acc_in, total,
    state_sem, small_sem, terms_sem,
    x_send, x_recv, meta_send, meta_recv, near_send, near_recv, one_send, one_recv, far_send, far_recv, flag_send, flag_recv, pair_send, pair_recv, hop_send, hop_recv, last_send, last_recv, acc_send, acc_recv,
    y_sem, z_sem,
):
    ctx, fsdp = lax.axis_index("ctx"), lax.axis_index("fsdp")
    x, core, z, y = place()
    here = core * N_FSDP + fsdp
    x_in = (x_in_0, x_in_1, x_in_2)
    order_of_arrays = (1, 2, 0)

    def arrivals(a):
        return recv_one if a == 0 else recv.at[a - 1]

    order = [(x + 2) % 4, (x + 1) % 4, (x + 3) % 4, x]

    def term_load(side, step):
        block = order[step] * 2 + (core + side) % 2
        return pltpu.make_async_copy(grad_hbm.at[0, block, 0], terms.at[side, step], terms_sem.at[side, step])

    def x_peer(k):
        return ((x + k) % 4) * 2 + core, fsdp

    def y_peer(k):
        return ctx, z * 4 + (y + k) % 4

    def z_peer(k):
        return ctx, ((z + k) % 4) * 4 + y

    barrier = pltpu.get_barrier_semaphore()
    pl.semaphore_signal(barrier, inc=1, device_id=(x * 2 + 1 - core, fsdp), device_id_type=MESH)
    for k in range(1, 4):
        pl.semaphore_signal(barrier, inc=1, device_id=x_peer(k), device_id_type=MESH)
    for k in range(1, 4):
        pl.semaphore_signal(barrier, inc=1, device_id=y_peer(k), device_id_type=MESH)
    for k in range(1, 4):
        pl.semaphore_signal(barrier, inc=1, device_id=z_peer(k), device_id_type=MESH)

    for step in range(4):
        term_load(1, step).start()
    frag_load = pltpu.make_async_copy(frag_hbm, frag_v, small_sem.at[0])
    frag_load_s = pltpu.make_async_copy(frag_hbm, frag_s, small_sem.at[1])
    counts_load = pltpu.make_async_copy(counts_hbm, counts_v, small_sem.at[2])
    frag_load.start()
    frag_load_s.start()
    counts_load.start()
    for step in range(4):
        term_load(0, step).start()
    state_loads = []
    for a, source in enumerate((master_hbm, moment_hbm, second_hbm)):
        for j in range(TILES):
            state_loads.append(
                pltpu.make_async_copy(
                    source.at[:, pl.ds(j * LANES, LANES)],
                    state.at[a, pl.ds(j * ROWS, ROWS)],
                    state_sem.at[a, j],
                )
            )
    for load in state_loads:
        load.start()

    frag_load.wait()
    counts_load.wait()
    owners, offsets = frag_v[pl.ds(0, 1), :], frag_v[pl.ds(1, 1), :]
    column = (owners // COLUMN - x + 4) % 4
    in_column = jnp.where(lax.broadcasted_iota(jnp.int32, (8, ROWS), 0) == column, 1.0, 0.0)
    earlier = jnp.where(
        lax.broadcasted_iota(jnp.int32, (DEVICES, DEVICES), 0) < lax.broadcasted_iota(jnp.int32, (DEVICES, DEVICES), 1),
        1.0, 0.0,
    )
    ranks = lax.dot_general(in_column, earlier, (((1,), (0,)), ((), ())), preferred_element_type=jnp.float32)
    rank = jnp.sum(in_column * ranks, axis=0, keepdims=True)
    over = jnp.max(jnp.where((rank >= ROOM) & (column > 0), 1.0, 0.0), axis=1, keepdims=True)
    place_ids = lax.broadcasted_iota(jnp.int32, (DEVICES * CAP, ROWS), 0)
    by_rank = jnp.where(place_ids == column * WIDE + rank.astype(jnp.int32), 1.0, 0.0)
    by_slot = jnp.where(place_ids == column * WIDE + (owners % COLUMN) * CAP + offsets, 1.0, 0.0)
    row_ids = lax.broadcasted_iota(jnp.int32, (8, ROWS), 1).astype(jnp.float32)
    which = lax.broadcasted_iota(jnp.int32, (8, ROWS), 0)
    row_of_rank = lax.dot_general(row_ids, by_rank, (((1,), (1,)), ((), ())), preferred_element_type=jnp.float32)
    rank_v[...] = jnp.clip(row_of_rank.astype(jnp.int32), 0, ROWS - 1)
    of_slot = lax.dot_general(
        jnp.where(which == 0, row_ids, rank), by_slot, (((1,), (1,)), ((), ())), preferred_element_type=jnp.float32
    )
    line = lax.broadcasted_iota(jnp.int32, (8, DEVICES * CAP), 0)
    top = jnp.where(line == 0, ROWS - 1, ROOM - 1)
    meta = jnp.clip(of_slot.astype(jnp.int32), 0, top)
    meta_v[...] = jnp.where(line == 2, over.astype(jnp.int32), meta)
    counts = jnp.broadcast_to(counts_v[...].astype(jnp.float32), (8, DEVICES))
    before = lax.dot_general(counts, earlier, (((1,), (0,)), ((), ())), preferred_element_type=jnp.float32)[0:1, :]
    rows_down = lax.broadcasted_iota(jnp.int32, (ROWS, DEVICES), 0).astype(jnp.float32)
    owner_ids = lax.broadcasted_iota(jnp.int32, (ROWS, DEVICES), 1)
    first = ((owner_ids % COLUMN) * 8 + ((owner_ids // COLUMN - x + 4) % 4) * CAP).astype(jnp.float32)
    offset = rows_down - before
    from_owner = (offset >= 0.0) & (offset < counts[0:1, :])
    slot_here = jnp.where(from_owner, first + offset, 0.0)
    slot_of_new = lax.dot_general(
        jnp.ones((8, DEVICES), jnp.float32), slot_here, (((1,), (1,)), ((), ())), preferred_element_type=jnp.float32
    )
    row_v[...] = jnp.clip(slot_of_new.astype(jnp.int32), 0, DEVICES * CAP - 1)
    table_copies = [
        pltpu.make_async_copy(source, target, small_sem.at[3 + i])
        for i, (source, target) in enumerate(((rank_v, rank_s), (meta_v, own_s), (row_v, row_s)))
    ]
    for copy in table_copies:
        copy.start()

    def pair_copy(step):
        return pltpu.make_async_remote_copy(
            src_ref=pair_out.at[step], dst_ref=pair_in.at[step], send_sem=pair_send.at[step],
            recv_sem=pair_recv.at[step], device_id=(x * 2 + 1 - core, fsdp), device_id_type=MESH,
        )

    def along_x(way):
        return ((x + (1 if way == 0 else 3)) % 4) * 2 + core, fsdp

    half = (pl.ds(0, TILES // 2), pl.ds(TILES // 2, TILES // 2))

    def hop_copy(way):
        return pltpu.make_async_remote_copy(
            src_ref=sums.at[0, half[way]], dst_ref=hop_in.at[way], send_sem=hop_send.at[way],
            recv_sem=hop_recv.at[way], device_id=along_x(way), device_id_type=MESH,
        )

    def last_copy(way):
        return pltpu.make_async_remote_copy(
            src_ref=sums.at[1 + way, half[1 - way]], dst_ref=last_in.at[way], send_sem=last_send.at[way],
            recv_sem=last_recv.at[way], device_id=along_x(way), device_id_type=MESH,
        )

    def acc_copy(way, part):
        rows = pl.ds(part * CHUNK, CHUNK)
        return pltpu.make_async_remote_copy(
            src_ref=sums.at[1 + way, half[way], rows], dst_ref=acc_in.at[half[way], rows],
            send_sem=acc_send.at[way, part], recv_sem=acc_recv.at[way, part],
            device_id=along_x(way), device_id_type=MESH,
        )

    def add_pair(step):
        term_load(0, step).wait()
        pair_copy(step).wait_recv()

        def add(i, carry):
            rows = pl.ds(pl.multiple_of(i * 16, 16), 16)
            for j in range(TILES):
                own = terms[0, step, rows, pl.ds(j * LANES, LANES)].astype(jnp.float32)
                sums[step, j, rows, :] = own + pair_in[step, j, rows, :]
            return carry

        lax.fori_loop(0, ROWS // 16, add, 0)

    place_in_row = (
        lax.broadcasted_iota(jnp.int32, (TILES, LANES), 0) * LANES + lax.broadcasted_iota(jnp.int32, (TILES, LANES), 1)
    )

    def masked(a, row):
        live = place_in_row < frag_s[2, row]
        return jnp.where(live, state[a, pl.ds(row, TILES, stride=ROWS), :], -1.0 if a == 2 else 0.0)

    def fill_x(a):
        def fill(i, carry):
            for k in range(1, 4):
                x_out[a, k - 1, i] = masked(a, rank_s[0, k * WIDE + i])
            return carry

        lax.fori_loop(0, ROOM, fill, 0, unroll=4)

    def x_copy(a, k):
        return pltpu.make_async_remote_copy(
            src_ref=x_out.at[a, k - 1], dst_ref=x_in[a].at[3 - k], send_sem=x_send.at[a, k - 1],
            recv_sem=x_recv.at[a, 3 - k], device_id=x_peer(k), device_id_type=MESH,
        )

    def start_x(a, k):
        for part in range(2):
            rows = pl.ds(part * (ROOM // 2), ROOM // 2)
            pltpu.make_async_remote_copy(
                src_ref=x_out.at[a, k - 1, rows], dst_ref=x_in[a].at[3 - k, rows], send_sem=x_send.at[a, k - 1],
                recv_sem=x_recv.at[a, 3 - k], device_id=x_peer(k), device_id_type=MESH,
            ).start()

    def meta_copy(k):
        return pltpu.make_async_remote_copy(
            src_ref=meta_v, dst_ref=meta_in.at[3 - k], send_sem=meta_send.at[k - 1],
            recv_sem=meta_recv.at[3 - k], device_id=x_peer(k), device_id_type=MESH,
        )

    def column_peer(i):
        return partner(0, i % 4, (i // 4) % 4, i // 16)

    def post_near(dy, dz, dcore):
        target = partner(0, dy, dz, dcore)
        there, i = (target[0] % 2) * N_FSDP + target[1], dy + 4 * dz + 16 * dcore
        for slot in range(CAP):
            row = own_s[0, there * CAP + slot]
            for a in range(3):
                near_out[i, a, slot] = masked(a, row)
        pltpu.make_async_remote_copy(
            src_ref=near_out.at[i, pl.ds(1, 2)], dst_ref=recv.at[:, pl.ds(here * 8, CAP)],
            send_sem=near_send, recv_sem=near_recv, device_id=target, device_id_type=MESH,
        ).start()
        pltpu.make_async_remote_copy(
            src_ref=near_out.at[i, 0], dst_ref=recv_one.at[pl.ds(here * 8, CAP)],
            send_sem=one_send, recv_sem=one_recv, device_id=target, device_id_type=MESH,
        ).start()

    def post_line(i, carry):
        post_near((1 + i // 2) * (i % 2), (1 + i // 2) * ((i + 1) % 2), 0)
        return carry

    def post_plane(i, carry):
        post_near(1 + i % 3, 1 + (i + i // 3) % 3, 0)
        return carry

    def post_core(i, carry):
        post_near(i % 4, (i + i // 4) % 4, 1)
        return carry

    def moved(a, there, origin, slot):
        return x_in[a][origin - 1, meta_s[origin - 1, 1, (4 - origin) * WIDE + there * CAP + slot]]

    def post_far(a):
        def post(i, carry):
            target = column_peer(i)
            there = (target[0] % 2) * N_FSDP + target[1]
            for origin in range(1, 4):
                for slot in range(CAP):
                    far_out[a, i, (origin - 1) * CAP + slot] = moved(a, there, origin, slot)
            pltpu.make_async_remote_copy(
                src_ref=far_out.at[a, i], dst_ref=arrivals(a).at[pl.ds(here * 8 + CAP, 3 * CAP)],
                send_sem=far_send.at[a], recv_sem=far_recv.at[a], device_id=target, device_id_type=MESH,
            ).start()
            return carry

        for k in range(1, 4):
            x_copy(a, k).wait_recv()
        lax.fori_loop(1, COLUMN, post, 0)
        for origin in range(1, 4):
            for slot in range(CAP):
                arrivals(a)[here * 8 + origin * CAP + slot] = moved(a, here, origin, slot)

    def post_flag(i, carry):
        pltpu.make_async_remote_copy(
            src_ref=flag_mine, dst_ref=flag_in.at[here], send_sem=flag_send, recv_sem=flag_recv,
            device_id=column_peer(i), device_id_type=MESH,
        ).start()
        return carry

    for load in state_loads:
        load.wait()
    frag_load_s.wait()
    for copy in table_copies:
        copy.wait()
    fill_x(1)
    pl.semaphore_wait(barrier, 10)
    for k in range(1, 4):
        pl.semaphore_signal(y_sem, inc=1, device_id=y_peer(k), device_id_type=MESH)
    for k in (1, 3, 2):
        start_x(1, k)
    for k in (1, 3, 2):
        meta_copy(k).start()
    fill_x(2)
    for k in (1, 3, 2):
        start_x(2, k)
    pl.semaphore_wait(y_sem, 3)
    for k in range(1, 4):
        pl.semaphore_signal(z_sem, inc=1, device_id=z_peer(k), device_id_type=MESH)
    lax.fori_loop(0, 6, post_line, 0)
    fill_x(0)
    for k in (1, 3, 2):
        start_x(0, k)
    pl.semaphore_wait(z_sem, 3)
    lax.fori_loop(0, 9, post_plane, 0)
    lax.fori_loop(0, 16, post_core, 0)
    for step in range(4):
        term_load(1, step).wait()

        def widen(i, carry, step=step):
            rows = pl.ds(pl.multiple_of(i * 16, 16), 16)
            for j in range(TILES):
                pair_out[step, j, rows, :] = terms[1, step, rows, pl.ds(j * LANES, LANES)].astype(jnp.float32)
            return carry

        lax.fori_loop(0, ROWS // 16, widen, 0)
        pair_copy(step).start()
    for slot in range(CAP):
        row = own_s[0, here * CAP + slot]
        for a in range(3):
            arrivals(a)[here * 8 + slot] = masked(a, row)
    add_pair(0)
    hop_copy(0).start()
    hop_copy(1).start()
    for way in range(2):
        add_pair(1 + way)
        last_copy(way).start()
    add_pair(3)
    for k in range(1, 4):
        meta_copy(k).wait_recv()
    flag = meta_v[pl.ds(2, 1), pl.ds(0, LANES)]
    for origin in range(3):
        flag = jnp.maximum(flag, meta_in[origin, pl.ds(2, 1), pl.ds(0, LANES)])
    flag = jnp.broadcast_to(flag.astype(jnp.float32), (8, LANES))
    flag_mine[...] = flag
    flag_in[here] = flag
    meta_load = pltpu.make_async_copy(meta_in, meta_s, small_sem.at[6])
    meta_load.start()
    lax.fori_loop(1, COLUMN, post_flag, 0)
    meta_load.wait()
    for a in order_of_arrays:
        post_far(a)
    for way in range(2):
        hop_copy(way).wait()

        def add_hop(i, carry, way=way):
            rows = pl.ds(pl.multiple_of(i * 16, 16), 16)
            for j in range(TILES // 2):
                sums[1 + way, way * (TILES // 2) + j, rows, :] += hop_in[way, j, rows, :]
            return carry

        lax.fori_loop(0, ROWS // 16, add_hop, 0)
    for part in range(PARTS):
        for way in range(2):
            acc_copy(way, part).start()
    for way in range(2):
        last_copy(way).wait()

    def add_last(i, carry):
        rows = pl.ds(pl.multiple_of(i * 16, 16), 16)
        for j in range(TILES):
            near = last_in[1, j, rows, :] if j < TILES // 2 else last_in[0, j - TILES // 2, rows, :]
            total[pl.ds(pl.multiple_of(j * ROWS + i * 16, 16), 16), :] = sums[3, j, rows, :] + near
        return carry

    lax.fori_loop(0, ROWS // 16, add_last, 0)

    others = COLUMN - 1
    near_here = recv.at[:, pl.ds(0, others * CAP)]
    pltpu.make_async_copy(near_here, near_here, near_recv).wait()
    for a in (1, 2):
        far_here = recv.at[a - 1, pl.ds(0, others * 3 * CAP)]
        pltpu.make_async_copy(far_here, far_here, far_recv.at[a]).wait()
    def update_moments(row, carry):
        slot = row_s[0, row]
        moment, second = recv[0, slot], recv[1, slot]
        live = second >= 0.0
        second = jnp.where(live, second, 0.0)
        grad = jnp.where(live, total[pl.ds(row, TILES, stride=ROWS), :], 0.0)
        new_moment = beta_one * moment + (1.0 - beta_one) * grad
        new_second = beta_two * second + (1.0 - beta_two) * grad * grad
        moment_hat = new_moment / (1.0 - beta_one**step_count)
        second_hat = new_second / (1.0 - beta_two**step_count)
        step_size[row] = moment_hat / (jnp.sqrt(second_hat) + epsilon)
        out[1, pl.ds(row, TILES, stride=ROWS), :] = new_moment
        out[2, pl.ds(row, TILES, stride=ROWS), :] = new_second
        return carry

    def update_master(row, carry):
        master = recv_one[row_s[0, row]]
        out[0, pl.ds(row, TILES, stride=ROWS), :] = master - learn_rate * (step_size[row] + decay_weight * master)
        return carry

    for part in range(PARTS):
        for way in range(2):
            acc_copy(way, part).wait_recv()
        for j in range(TILES):
            total[pl.ds(j * ROWS + part * CHUNK, CHUNK), :] += acc_in[j, pl.ds(part * CHUNK, CHUNK), :]
        lax.fori_loop(part * CHUNK, (part + 1) * CHUNK, update_moments, 0, unroll=8)
    flags_here = flag_in.at[pl.ds(0, others)]
    pltpu.make_async_copy(flags_here, flags_here, flag_recv).wait()
    flag_out[0] = jnp.max(flag_in[...]).astype(jnp.int32)
    one_here = recv_one.at[pl.ds(0, others * CAP)]
    pltpu.make_async_copy(one_here, one_here, one_recv).wait()
    far_here = recv_one.at[pl.ds(0, others * 3 * CAP)]
    pltpu.make_async_copy(far_here, far_here, far_recv.at[0]).wait()
    lax.fori_loop(0, ROWS, update_master, 0, unroll=8)

    near_sent = near_out.at[pl.ds(1, others), pl.ds(1, 2)]
    pltpu.make_async_copy(near_sent, near_sent, near_send).wait()
    one_sent = near_out.at[pl.ds(1, others), 0]
    pltpu.make_async_copy(one_sent, one_sent, one_send).wait()
    for a in range(3):
        far_sent = far_out.at[a, pl.ds(1, others)]
        pltpu.make_async_copy(far_sent, far_sent, far_send.at[a]).wait()
    flags_sent = flag_in.at[pl.ds(0, others)]
    pltpu.make_async_copy(flags_sent, flags_sent, flag_send).wait()
    for k in range(1, 4):
        meta_copy(k).wait_send()
        for a in range(3):
            x_copy(a, k).wait_send()
    for step in range(4):
        pair_copy(step).wait_send()
    for way in range(2):
        for part in range(PARTS):
            acc_copy(way, part).wait_send()


def write_out(updated, master_hbm, moment_hbm, second_hbm, sem):
    stores = []
    for a, target in enumerate((master_hbm, moment_hbm, second_hbm)):
        for j in range(TILES):
            stores.append(
                pltpu.make_async_copy(
                    updated.at[a, pl.ds(j * ROWS, ROWS)], target.at[:, pl.ds(j * LANES, LANES)], sem.at[a, j]
                )
            )
    for store in stores:
        store.start()
    for store in stores:
        store.wait()


def local(old_master, old_moment, old_second, frag_list, pair_counts, grad_partial):
    anywhere = pl.BlockSpec(memory_space=pl.ANY)
    on_chip = pl.BlockSpec(memory_space=pltpu.VMEM)
    shape = jax.ShapeDtypeStruct((ROWS, FRAG), jnp.float32)
    f32, i32 = jnp.float32, jnp.int32
    dma = pltpu.SemaphoreType.DMA
    arguments = (old_master, old_moment, old_second, frag_list, pair_counts.reshape(1, DEVICES), grad_partial)
    updated, flag = pl.pallas_call(
        kernel_fast,
        out_shape=(pltpu.VMEM((3, TILES * ROWS, LANES), f32), pltpu.SMEM((1,), i32)),
        in_specs=[anywhere] * 6,
        out_specs=(on_chip, pl.BlockSpec(memory_space=pltpu.SMEM)),
        scratch_shapes=[
            pltpu.VMEM((3, TILES * ROWS, LANES), f32),
            pltpu.VMEM((3, ROWS), i32),
            pltpu.VMEM((1, DEVICES), i32),
            pltpu.VMEM((8, DEVICES * CAP), i32),
            pltpu.VMEM((8, DEVICES * CAP), i32),
            pltpu.VMEM((8, ROWS), i32),
            pltpu.SMEM((3, ROWS), i32),
            pltpu.SMEM((8, DEVICES * CAP), i32),
            pltpu.SMEM((8, DEVICES * CAP), i32),
            pltpu.SMEM((3, 8, DEVICES * CAP), i32),
            pltpu.SMEM((8, ROWS), i32),
            pltpu.VMEM((3, 3, ROOM, TILES, LANES), f32),
            pltpu.VMEM((3, ROOM, TILES, LANES), f32),
            pltpu.VMEM((3, ROOM, TILES, LANES), f32),
            pltpu.VMEM((3, ROOM, TILES, LANES), f32),
            pltpu.VMEM((3, 8, DEVICES * CAP), i32),
            pltpu.VMEM((COLUMN, 3, CAP, TILES, LANES), f32),
            pltpu.VMEM((3, COLUMN, 3 * CAP, TILES, LANES), f32),
            pltpu.VMEM((8, LANES), f32),
            pltpu.VMEM((COLUMN, 8, LANES), f32),
            pltpu.VMEM((2, DEVICES * CAP, TILES, LANES), f32),
            pltpu.VMEM((DEVICES * CAP, TILES, LANES), f32),
            pltpu.VMEM((ROWS, TILES, LANES), f32),
            pltpu.VMEM((2, 4, ROWS, FRAG), jnp.bfloat16),
            pltpu.VMEM((4, TILES, ROWS, LANES), f32),
            pltpu.VMEM((4, TILES, ROWS, LANES), f32),
            pltpu.VMEM((4, TILES, ROWS, LANES), f32),
            pltpu.VMEM((2, TILES // 2, ROWS, LANES), f32),
            pltpu.VMEM((2, TILES // 2, ROWS, LANES), f32),
            pltpu.VMEM((TILES, ROWS, LANES), f32),
            pltpu.VMEM((TILES * ROWS, LANES), f32),
            dma((3, TILES)),
            dma((7,)),
            dma((2, 4)),
            dma((3, 3)),
            dma((3, 3)),
            dma((3,)),
            dma((3,)),
            dma,
            dma,
            dma,
            dma,
            dma((3,)),
            dma((3,)),
            dma,
            dma,
            dma((4,)),
            dma((4,)),
            dma((2,)),
            dma((2,)),
            dma((2,)),
            dma((2,)),
            dma((2, PARTS)),
            dma((2, PARTS)),
            pltpu.SemaphoreType.REGULAR,
            pltpu.SemaphoreType.REGULAR,
        ],
        compiler_params=pltpu.CompilerParams(
            collective_id=0, has_side_effects=True, vmem_limit_bytes=48 * 1024 * 1024
        ),
    )(*[pltpu.with_memory_space_constraint(a, pltpu.HBM) for a in arguments])

    def slow():
        return pl.pallas_call(
            kernel,
            out_shape=pltpu.VMEM((3, TILES * ROWS, LANES), f32),
            in_specs=[anywhere] * 6,
            out_specs=on_chip,
            scratch_shapes=[
                pltpu.VMEM((3, TILES * ROWS, LANES), f32),
                pltpu.VMEM((3, ROWS), i32),
                pltpu.VMEM((1, DEVICES), i32),
                pltpu.VMEM((8, DEVICES * CAP), i32),
                pltpu.VMEM((8, ROWS), i32),
                pltpu.SMEM((3, ROWS), i32),
                pltpu.SMEM((8, DEVICES * CAP), i32),
                pltpu.SMEM((8, ROWS), i32),
                pltpu.VMEM((DEVICES, CAP, 3 * TILES, LANES), f32),
                pltpu.VMEM((DEVICES * CAP, 3 * TILES, LANES), f32),
                pltpu.VMEM((2, 4, ROWS, FRAG), jnp.bfloat16),
                pltpu.VMEM((4, TILES, ROWS, LANES), f32),
                pltpu.VMEM((4, TILES, ROWS, LANES), f32),
                pltpu.VMEM((4, TILES, ROWS, LANES), f32),
                pltpu.VMEM((2, TILES // 2, ROWS, LANES), f32),
                pltpu.VMEM((2, TILES // 2, ROWS, LANES), f32),
                pltpu.VMEM((TILES, ROWS, LANES), f32),
                pltpu.VMEM((TILES * ROWS, LANES), f32),
                dma((3, TILES)),
                dma((5,)),
                dma((2, 4)),
                dma,
                dma,
                dma((4,)),
                dma((4,)),
                dma((2,)),
                dma((2,)),
                dma((2,)),
                dma((2,)),
                dma((2,)),
                dma((2,)),
                pltpu.SemaphoreType.REGULAR,
                pltpu.SemaphoreType.REGULAR,
            ],
            compiler_params=pltpu.CompilerParams(
                collective_id=1, has_side_effects=True, vmem_limit_bytes=48 * 1024 * 1024
            ),
        )(*[pltpu.with_memory_space_constraint(a, pltpu.HBM) for a in arguments])

    def write(updated):
        return pl.pallas_call(
            write_out,
            out_shape=(shape, shape, shape),
            in_specs=[anywhere],
            out_specs=(anywhere, anywhere, anywhere),
            scratch_shapes=[dma((3, TILES))],
            compiler_params=pltpu.CompilerParams(vmem_limit_bytes=1024 * 1024),
        )(pltpu.with_memory_space_constraint(updated, pltpu.VMEM))

    return lax.cond(flag[0] > 0, lambda: write(slow()), lambda: write(updated))


def solution(mesh):
    return jax.shard_map(
        local,
        mesh=mesh,
        in_specs=(
            P(("ctx", "fsdp"), None),
            P(("ctx", "fsdp"), None),
            P(("ctx", "fsdp"), None),
            P(None, ("ctx", "fsdp")),
            P(None, ("ctx", "fsdp")),
            P("ctx", None, "fsdp", None, None),
        ),
        out_specs=(P(("ctx", "fsdp"), None), P(("ctx", "fsdp"), None), P(("ctx", "fsdp"), None)),
        check_vma=False,
    )
```
